128 devices in a mesh: seq: 16 (over x, z), fsdp: 8 (over y, core).
Axes of the slice: x: 4, y: 4, z: 4, core: 2. Of those that a mesh axis runs over, the one named last changes fastest.
Arguments:
- tokens: bfloat16 [16384, 1024], P(('seq', 'fsdp')), may hold values from -6 to 6
- cotangent: bfloat16 [16384, 1024], P(('seq', 'fsdp')), may hold values from -6 to 6
- norm_gain: bfloat16 [1024], replicated, may hold values from 0.5 to 1.5
- q_weight: bfloat16 [1024, 1024], P('seq', 'fsdp'), may hold values from -0.1875 to 0.1875
- q_bias: bfloat16 [1024], P('fsdp'), may hold values from -1.75 to 1.75
- key_matrix: bfloat16 [1024, 512], P('seq', 'fsdp'), may hold values from -0.1875 to 0.1875
- key_bias: bfloat16 [512], P('fsdp'), may hold values from -1.75 to 1.75
- value_matrix: bfloat16 [1024, 512], P('seq', 'fsdp'), may hold values from -0.1875 to 0.1875
- value_bias: bfloat16 [512], P('fsdp'), may hold values from -1.75 to 1.75
- o_weight: bfloat16 [1024, 1024], P('fsdp', 'seq'), may hold values from -1 to 1
- o_bias: bfloat16 [1024], replicated, may hold values from -1.75 to 1.75
- sinks: bfloat16 [16], P('fsdp'), may hold values from -4 to 4
- moe_gain: bfloat16 [1024], replicated, may hold values from 0.5 to 1.5
- router_weight: bfloat16 [1024, 32], replicated, may hold values from -0.09375 to 0.09375
- router_bias: bfloat16 [32], replicated, may hold values from -1.25 to 1.25
- gate_up_weight: bfloat16 [32, 1024, 2, 512], P('seq', None, None, 'fsdp'), may hold values from -0.1875 to 0.1875
- gate_up_bias: bfloat16 [32, 2, 512], P('seq', None, 'fsdp'), may hold values from -0.625 to 0.625
- down_weight: bfloat16 [32, 512, 1024], P('seq', 'fsdp'), may hold values from -0.75 to 0.75
- down_bias: bfloat16 [32, 1024], P('seq'), may hold values from -0.625 to 0.625
- routes: int32 [16384, 8], P(('seq', 'fsdp')), may hold values from 0 to 31, all different within a row; in each aligned block of 128 rows (0 to 127, 128 to 255, ...) at most 48 rows name the same one
Outputs:
- mixed: bfloat16 [16384, 1024], P(('seq', 'fsdp'))
- tokens_grad: bfloat16 [16384, 1024], P(('seq', 'fsdp'))
- norm_gain_grad: float32 [1024], replicated
- q_weight_grad: float32 [1024, 1024], P('seq', 'fsdp')
- q_bias_grad: float32 [1024], P('fsdp')
- k_weight_grad: float32 [1024, 512], P('seq', 'fsdp')
- k_bias_grad: float32 [512], P('fsdp')
- v_weight_grad: float32 [1024, 512], P('seq', 'fsdp')
- v_bias_grad: float32 [512], P('fsdp')
- o_weight_grad: float32 [1024, 1024], P('fsdp', 'seq')
- o_bias_grad: float32 [1024], replicated
- sinks_grad: float32 [16], P('fsdp')
- moe_gain_grad: float32 [1024], replicated
- router_weight_grad: float32 [1024, 32], replicated
- router_bias_grad: float32 [32], replicated
- gate_up_weight_grad: float32 [32, 1024, 2, 512], P('seq', None, None, 'fsdp')
- gate_up_bias_grad: float32 [32, 2, 512], P('seq', None, 'fsdp')
- down_weight_grad: float32 [32, 512, 1024], P('seq', 'fsdp')
- down_bias_grad: float32 [32, 1024], P('seq')
The draws below stay inside these ranges and needn't reach their ends.
Inputs may be any that keep to these rules, and one draw needn't show every extreme that they name: `routes`: each row names 8 different experts and every expert is named somewhere. Among the 128 rows of one device no expert is named more than 48 times; in every draw some device names some expert exactly 48 times.
All inputs are finite; a program needn't handle non-finite values.
Results may differ from the reference program's by a relative error of at most 0.028.
Values may be sent and summed in bfloat16 or wider, within the bound.
No kernel may reach another device: no remote copies, remote signals or barrier semaphores. Data moves between devices by JAX's collectives and lax.ppermute only.
A program may use at most 192 MiB of HBM per device.

```python
import math
import jax
import jax.numpy as jnp
import numpy as np
from jax import lax

MODEL_WIDTH = 1024
QUERY_HEADS = 16
KEY_VALUE_HEADS = 8
HEAD_WIDTH = 64
FF = 512
TOPK = 8
WINDOW = 128
E = 32
SEQUENCE_ROWS = 1024
TOK_DEV = 128
TOKEN_COUNT = 16384
CAP = 48


def shard_levels(key, dims, split, least, high):
    def one(dim, shards_of):
        steps = jax.random.uniform(jax.random.fold_in(jax.random.fold_in(key, 6), dim), (shards_of,), jnp.float32, least / len(split), high / len(split))
        return jnp.repeat(jnp.exp(steps), dims[dim] // shards_of).reshape((-1,) + (1,) * (len(dims) - dim - 1))

    loudness = one(*split[0])
    for cut in split[1:]:
        loudness = loudness * one(*cut)
    return loudness


def routed_block(rng, own, number, rows, count, top, reach, skew):
    ranking = jax.random.permutation(rng, count)
    crowded, usual = shares(count, rows * top, reach, skew, True), shares(count, rows * top, reach, skew, False)
    places = jnp.arange(count)

    def named(tallies, rotation):
        used = int((tallies > 0).sum())
        fixed = max(1, used // 4)
        moved = fixed + (places - fixed + rotation * (used - fixed)) % max(1, count - fixed)
        return jnp.zeros((count,), jnp.int32).at[ranking[jnp.where(places < fixed, places, moved)]].set(jnp.asarray(tallies, jnp.int32))

    tallies = jnp.where(number % 4 == 0, named(crowded, number // 4), named(usual, number - number // 4 - 1))
    mixed = jax.random.permutation(jax.random.fold_in(own, 3), count)
    giver, taker = mixed[0:count // 2 * 2:2], mixed[1:count // 2 * 2:2]
    slack = jnp.minimum(tallies[giver] - 1, reach - tallies[taker]) // 2
    slack = jnp.where((giver == ranking[0]) | (taker == ranking[0]) | (tallies[taker] == 0), 0, jnp.maximum(slack, 0))
    moved = jax.random.randint(jax.random.fold_in(own, 4), (count // 2,), 0, 1 << 20) % (slack + 1)
    tallies = tallies.at[giver].add(-moved).at[taker].add(moved)
    labels = jnp.searchsorted(jnp.cumsum(tallies), jnp.arange(rows * top), side="right").astype(jnp.int32)
    table = labels.reshape(top, rows).T
    table = table[jax.random.permutation(jax.random.fold_in(own, 1), rows)]
    rotation = jax.random.randint(jax.random.fold_in(own, 2), (rows, 1), 0, top)
    return jnp.take_along_axis(table, (jnp.arange(top)[None, :] + rotation) % top, axis=1)


def shares(number_of, total, reach, skew, full):
    portions = [(1 << 20) // math.isqrt(standing ** skew) + 1 for standing in range(1, number_of + 1)]
    largest = reach if full else min(reach, max(-(-total // number_of), total * portions[0] // sum(portions)))
    least = 1 if total - largest >= number_of - 1 else 0
    given, surplus = [largest] + [least] * (number_of - 1), total - largest - least * (number_of - 1)
    while surplus > 0:
        movable = [i for i in range(1, number_of) if given[i] < largest] or [i for i in range(1, number_of) if given[i] < reach]
        pool, left = sum([portions[i] for i in movable]), surplus
        for i in movable:
            extra = min(reach - given[i], max(1, left * portions[i] // pool), surplus)
            given[i] = given[i] + extra
            surplus = surplus - extra
    return np.array(given)


def noise(own_key, extent, scale, reach, cuts=(), kind=jnp.bfloat16):
    gain = shard_levels(own_key, extent, cuts, -0.22, 0.18) if cuts else 1.0
    entries = jax.random.normal(own_key, extent, jnp.float32) * scale * gain
    return jnp.minimum(jnp.maximum(entries, -reach), reach).astype(kind)


def setup_inputs(seed: int = 0) -> dict:
    key_of = jax.random.split(jax.random.key(seed), 21)
    tokens = noise(key_of[0], (TOKEN_COUNT, MODEL_WIDTH), 1.0, 6.0, ((0, 128),))
    cotangent = noise(key_of[1], (TOKEN_COUNT, MODEL_WIDTH), 1.0, 6.0, ((0, 128),))
    norm_gain = jnp.clip(1.0 + 0.1 * jax.random.normal(key_of[2], (MODEL_WIDTH,), jnp.float32), 0.5, 1.5).astype(jnp.bfloat16)
    q_weight = noise(key_of[3], (MODEL_WIDTH, QUERY_HEADS * HEAD_WIDTH), MODEL_WIDTH ** -0.5, 0.1875, ((0, 16), (1, 8)))
    q_bias = noise(key_of[4], (QUERY_HEADS * HEAD_WIDTH,), 0.3, 1.75, ((0, 8),))
    key_matrix = noise(key_of[5], (MODEL_WIDTH, KEY_VALUE_HEADS * HEAD_WIDTH), MODEL_WIDTH ** -0.5, 0.1875, ((0, 16), (1, 8)))
    key_bias = noise(key_of[6], (KEY_VALUE_HEADS * HEAD_WIDTH,), 0.3, 1.75, ((0, 8),))
    value_matrix = noise(key_of[7], (MODEL_WIDTH, KEY_VALUE_HEADS * HEAD_WIDTH), MODEL_WIDTH ** -0.5, 0.1875, ((0, 16), (1, 8)))
    value_bias = noise(key_of[8], (KEY_VALUE_HEADS * HEAD_WIDTH,), 0.3, 1.75, ((0, 8),))
    o_weight = noise(key_of[9], (QUERY_HEADS * HEAD_WIDTH, MODEL_WIDTH), (QUERY_HEADS * HEAD_WIDTH // 32) ** -0.5, 1.0, ((0, 8), (1, 16)))
    o_bias = noise(key_of[10], (MODEL_WIDTH,), 0.3, 1.75)
    sinks = noise(key_of[11], (QUERY_HEADS,), 1.0, 4.0, ((0, 8),))
    moe_gain = jnp.clip(1.0 + 0.1 * jax.random.normal(key_of[12], (MODEL_WIDTH,), jnp.float32), 0.5, 1.5).astype(jnp.bfloat16)
    router_weight = noise(key_of[13], (MODEL_WIDTH, E), (4 * MODEL_WIDTH) ** -0.5, 0.09375)
    router_bias = noise(key_of[14], (E,), 0.2, 1.25)
    gate_up_weight = noise(key_of[15], (E, MODEL_WIDTH, 2, FF), MODEL_WIDTH ** -0.5, 0.1875, ((0, 16), (3, 8)))
    gate_up_bias = noise(key_of[16], (E, 2, FF), 0.1, 0.625, ((0, 16), (2, 8)))
    down_weight = noise(key_of[17], (E, FF, MODEL_WIDTH), (FF // 8) ** -0.5, 0.75, ((0, 16), (1, 8)))
    down_bias = noise(key_of[18], (E, MODEL_WIDTH), 0.1, 0.625, ((0, 16),))
    routes_keys = jax.random.split(jax.random.fold_in(key_of[19], 1), TOKEN_COUNT // TOK_DEV)
    routes_turns = jax.random.permutation(jax.random.fold_in(key_of[19], 3), TOKEN_COUNT // TOK_DEV)
    routes = jax.vmap(lambda own, number: routed_block(jax.random.fold_in(key_of[19], 2), own, number, TOK_DEV, E, TOPK, CAP, 2))(routes_keys, routes_turns).reshape((TOKEN_COUNT, TOPK))
    return {"tokens": tokens, "cotangent": cotangent, "norm_gain": norm_gain, "q_weight": q_weight, "q_bias": q_bias, "key_matrix": key_matrix, "key_bias": key_bias, "value_matrix": value_matrix, "value_bias": value_bias, "o_weight": o_weight, "o_bias": o_bias, "sinks": sinks, "moe_gain": moe_gain, "router_weight": router_weight, "router_bias": router_bias, "gate_up_weight": gate_up_weight, "gate_up_bias": gate_up_bias, "down_weight": down_weight, "down_bias": down_bias, "routes": routes}


norm_eps = 1e-05
rope_base = 150000.0
swiglu_limit = 7.0
glu_alpha = 1.702
masked_score = -1000000000.0
highest = lax.Precision.HIGHEST

@jax.custom_vjp
def lower_precision(v):
    return lax.optimization_barrier(v.astype(jnp.bfloat16)).astype(jnp.float32)

@jax.custom_vjp
def low_back(v):
    return v

def low_keep(v):
    return (lower_precision(v), None)

def low_pass(kept, grad):
    return (grad,)

def back_keep(v):
    return (v, None)

def back_low(kept, grad):
    return (lower_precision(grad),)
lower_precision.defvjp(low_keep, low_pass)
low_back.defvjp(back_keep, back_low)

def rms_scale(values, gain_vec):
    return values * lax.rsqrt(lax.optimization_barrier(jnp.mean(values * values, axis=-1, keepdims=True)) + norm_eps) * gain_vec

def rotary_tables(positions, head_size):
    half_size = head_size // 2
    inverse = rope_base ** (-(jnp.arange(half_size, dtype=jnp.float32) * 2.0 / head_size))
    angles = positions.astype(jnp.float32)[:, None] * inverse[None, :]
    return (jnp.cos(angles), jnp.sin(angles))

def rotary_embedding(values, cosine_table, sine_rows_table):
    half_size = values.shape[-1] // 2
    leading = values[..., :half_size]
    trailing = values[..., half_size:]
    cos_rows = cosine_table[:, None, :]
    sin_rows = sine_rows_table[:, None, :]
    return jnp.concatenate([leading * cos_rows - trailing * sin_rows, trailing * cos_rows + leading * sin_rows], axis=-1)

def soft_clamp(values):
    return swiglu_limit * jnp.tanh(values / swiglu_limit)

def expert_act(pre_act):
    gate_part = soft_clamp(pre_act[..., 0, :])
    up_part = soft_clamp(pre_act[..., 1, :])
    return (up_part + 1.0) * gate_part * jax.nn.sigmoid(glu_alpha * gate_part)

def attend_window(query_rotated, key_rotated, value_everything, sink_logit_table):
    count_of_blocks = TOKEN_COUNT // SEQUENCE_ROWS
    query_group_width = QUERY_HEADS // KEY_VALUE_HEADS
    pad_rows = ((WINDOW, 0), (0, 0), (0, 0))
    key_pad = jnp.pad(key_rotated, pad_rows)
    value_pad = jnp.pad(value_everything, pad_rows)
    query_blocks = query_rotated.reshape(count_of_blocks, SEQUENCE_ROWS, KEY_VALUE_HEADS, query_group_width, HEAD_WIDTH)
    starts = jnp.arange(count_of_blocks, dtype=jnp.int32) * SEQUENCE_ROWS
    sink_logit_values = sink_logit_table.reshape(KEY_VALUE_HEADS, query_group_width)[:, :, None]

    def one_block(pieces):
        q_block, start_row = pieces
        key_block = lax.dynamic_slice_in_dim(key_pad, start_row, WINDOW + SEQUENCE_ROWS, 0)
        value_block = lax.dynamic_slice_in_dim(value_pad, start_row, WINDOW + SEQUENCE_ROWS, 0)
        raw_scores = jnp.einsum('rkgd,skd->kgrs', q_block, key_block, precision=highest) * HEAD_WIDTH ** (-0.5)
        raw_scores = low_back(raw_scores)
        query_pos = start_row + jnp.arange(SEQUENCE_ROWS, dtype=jnp.int32)
        key_pos = start_row - WINDOW + jnp.arange(WINDOW + SEQUENCE_ROWS, dtype=jnp.int32)
        offset = query_pos[:, None] - key_pos[None, :]
        allowed = (offset >= 0) & (offset < WINDOW) & (key_pos[None, :] >= 0)
        scores = jnp.where(allowed[None, None], raw_scores, masked_score)
        row_top = jnp.maximum(lax.optimization_barrier(jnp.max(scores, axis=-1)), sink_logit_values)
        weights = jnp.exp(scores - row_top[..., None])
        denominator = lax.optimization_barrier(jnp.sum(weights, axis=-1)) + jnp.exp(sink_logit_values - row_top)
        soft_probs = lower_precision(weights / denominator[..., None])
        return jnp.einsum('kgrs,skd->rkgd', soft_probs, value_block, precision=highest)
    outputs = lax.map(jax.checkpoint(one_block), (query_blocks, starts))
    return outputs.reshape(TOKEN_COUNT, QUERY_HEADS * HEAD_WIDTH)

def forward(tokens, norm_gain, q_weight, q_bias, key_matrix, key_bias, value_matrix, value_bias, o_weight, o_bias, sinks, moe_gain, router_weight, router_bias, gate_up_weight, gate_up_bias, down_weight, down_bias, routes):
    h_one = lower_precision(rms_scale(tokens, norm_gain))
    positions = jnp.arange(TOKEN_COUNT, dtype=jnp.int32)
    cosine_table, sine_rows_table = rotary_tables(positions, HEAD_WIDTH)
    q_pre = low_back(jnp.dot(h_one, q_weight, precision=highest) + q_bias)
    key_projected = low_back(jnp.dot(h_one, key_matrix, precision=highest) + key_bias)
    value_everything = low_back(lower_precision(jnp.dot(h_one, value_matrix, precision=highest) + value_bias))
    query_rotated = lower_precision(rotary_embedding(q_pre.reshape(TOKEN_COUNT, QUERY_HEADS, HEAD_WIDTH), cosine_table, sine_rows_table))
    key_rotated = lower_precision(rotary_embedding(key_projected.reshape(TOKEN_COUNT, KEY_VALUE_HEADS, HEAD_WIDTH), cosine_table, sine_rows_table))
    attended_rows = attend_window(query_rotated.reshape(TOKEN_COUNT, KEY_VALUE_HEADS, QUERY_HEADS // KEY_VALUE_HEADS, HEAD_WIDTH), key_rotated, value_everything.reshape(TOKEN_COUNT, KEY_VALUE_HEADS, HEAD_WIDTH), sinks)
    attended_rows = low_back(lower_precision(attended_rows))
    residual = tokens + low_back(jnp.dot(attended_rows, o_weight, precision=highest)) + o_bias
    h_two = lower_precision(rms_scale(residual, moe_gain))
    logits = jnp.dot(h_two, router_weight, precision=highest) + router_bias
    gate_probs = jax.nn.softmax(jnp.take_along_axis(logits, routes, axis=1), axis=-1)
    buffer_rows = TOKEN_COUNT // TOK_DEV * CAP
    flat_ids = routes.reshape(TOKEN_COUNT * TOPK).astype(jnp.int32)
    expert_ids = jnp.arange(E, dtype=jnp.int32)
    flat_hot = (flat_ids[:, None] == expert_ids[None, :]).astype(jnp.int32)
    slot_rank = lax.optimization_barrier(jnp.sum((jnp.cumsum(flat_hot, axis=0) - flat_hot) * flat_hot, axis=1)).astype(jnp.int32)
    slot_id = (flat_ids * buffer_rows + slot_rank).astype(jnp.int32)
    token_of = (jnp.arange(TOKEN_COUNT * TOPK, dtype=jnp.int32) // TOPK).astype(jnp.int32)
    owners = jnp.zeros((E * buffer_rows,), jnp.int32).at[slot_id].set(token_of)
    owners = owners.reshape(E, buffer_rows)
    counts = lax.optimization_barrier(jnp.sum(flat_hot, axis=0)).astype(jnp.int32)
    live_slots = jnp.arange(buffer_rows, dtype=jnp.int32)[None, :] < counts[:, None]

    def one_expert(pieces):
        w_gu, b_gu, w_down, b_down, owner_rows, live_rows = pieces
        row_data = jnp.where(live_rows[:, None], h_two[owner_rows], 0.0)
        pre_act = low_back(jnp.einsum('rd,dgh->rgh', row_data, w_gu, precision=highest) + b_gu)
        hidden = lower_precision(expert_act(pre_act))
        return low_back(jnp.dot(hidden, w_down, precision=highest) + b_down)
    slot_out = lax.map(jax.checkpoint(one_expert), (gate_up_weight, gate_up_bias, down_weight, down_bias, owners, live_slots))
    per_slot = slot_out.reshape(E * buffer_rows, MODEL_WIDTH)[slot_id].reshape(TOKEN_COUNT, TOPK, MODEL_WIDTH)
    return residual + lax.optimization_barrier(jnp.sum(gate_probs[:, :, None] * per_slot, axis=1))

def reference(tokens, cotangent, norm_gain, q_weight, q_bias, key_matrix, key_bias, value_matrix, value_bias, o_weight, o_bias, sinks, moe_gain, router_weight, router_bias, gate_up_weight, gate_up_bias, down_weight, down_bias, routes):
    floats = tuple((source.astype(jnp.float32) for source in (tokens, norm_gain, q_weight, q_bias, key_matrix, key_bias, value_matrix, value_bias, o_weight, o_bias, sinks, moe_gain, router_weight, router_bias, gate_up_weight, gate_up_bias, down_weight, down_bias)))

    def wrapped(*params):
        return forward(*params, routes)
    block_out, pullback = jax.vjp(wrapped, *floats)
    gradients = pullback(cotangent.astype(jnp.float32))
    return (block_out.astype(jnp.bfloat16), gradients[0].astype(jnp.bfloat16), gradients[1], gradients[2], gradients[3], gradients[4], gradients[5], gradients[6], gradients[7], gradients[8], gradients[9], gradients[10], gradients[11], gradients[12], gradients[13], gradients[14], gradients[15], gradients[16], gradients[17])
```

```python
import jax
import jax.numpy as jnp
import numpy as np
from jax import lax
from jax.sharding import Mesh, PartitionSpec as P

HEAD_WIDTH = 64
WINDOW = 128
norm_eps = 1e-05
rope_base = 150000.0
swiglu_limit = 7.0
glu_alpha = 1.702
masked_score = -1000000000.0
highest = lax.Precision.HIGHEST

SEQ = ("x", "z")
FSDP = ("y", "c")
COLUMN = ("x", "z", "c")
ALL = ("x", "z", "y", "c")
f32 = jnp.float32
bf16 = jnp.bfloat16


def dot(a, b, dims=((1,), (0,))):
    return lax.dot_general(a, b, (dims, ((), ())), preferred_element_type=f32)


def inv_rms(values):
    return lax.rsqrt(jnp.mean(values * values, axis=-1, keepdims=True) + norm_eps)


def rotary_tables(positions):
    half_size = HEAD_WIDTH // 2
    inverse = rope_base ** (-(jnp.arange(half_size, dtype=f32) * 2.0 / HEAD_WIDTH))
    angles = positions.astype(f32)[:, None] * inverse[None, :]
    return jnp.cos(angles), jnp.sin(angles)


def rotate(values, cosine, sine):
    half = HEAD_WIDTH // 2
    lead, trail = values[..., :half], values[..., half:]
    cos, sin = cosine[:, None, :], sine[:, None, :]
    return jnp.concatenate([lead * cos - trail * sin, trail * cos + lead * sin], axis=-1)


def exchange(value, axes):
    return lax.all_to_all(value, axes, split_axis=0, concat_axis=0, tiled=True)


def broadcast_exchange(value, axes, count):
    return exchange(jnp.broadcast_to(value[None], (count,) + value.shape), axes)


def after(value, *earlier):
    return lax.optimization_barrier((value,) + earlier)[0]


def soft_clamp(values):
    return swiglu_limit * jnp.tanh(values / swiglu_limit)


def expert_act(gate, up):
    gate_part = soft_clamp(gate)
    return (soft_clamp(up) + 1.0) * gate_part * jax.nn.sigmoid(glu_alpha * gate_part)


def sum_block(partial, ys, tok):
    model = partial.shape[-1]
    parts = partial.astype(bf16).reshape(ys, 2, tok, model).transpose(1, 0, 2, 3)
    pair = exchange(parts, "c").astype(f32)
    own = (pair[0] + pair[1]).astype(bf16)
    return jnp.sum(exchange(own, "y").astype(f32), axis=0)


def gather_block(rows):
    return lax.all_gather(rows, FSDP, axis=0, tiled=True)


def shards(
    tokens, cotangent, norm_gain, q_weight, q_bias, key_matrix, key_bias, value_matrix, value_bias,
    o_weight, o_bias, sinks, moe_gain, router_weight, router_bias, gate_up_weight, gate_up_bias,
    down_weight, down_bias, routes,
):
    zs, ys = lax.axis_size("z"), lax.axis_size("y")
    seqs = lax.axis_size("x") * zs
    seq_index = lax.axis_index("x") * zs + lax.axis_index("z")
    core = lax.axis_index("c")
    tok, model = tokens.shape
    rows = tok * ys * 2
    experts = 2 * seqs
    top = routes.shape[1]
    cap = 3 * tok * top // (2 * experts)
    slots = experts * cap
    ff_own = gate_up_weight.shape[-1]
    window = WINDOW
    scale = HEAD_WIDTH ** (-0.5)

    x_float = tokens.astype(f32)
    gain_one = norm_gain.astype(f32)
    x_root = inv_rms(x_float)
    h_low = (x_float * x_root * gain_one).astype(bf16)
    block_h = gather_block(h_low)

    packed = jnp.concatenate([q_weight, key_matrix, value_matrix, o_weight.T], axis=1)
    packed = broadcast_exchange(packed, SEQ, seqs).reshape(model, packed.shape[1])
    w_qkv, w_o = packed[:, :256], packed[:, 256:]

    ids = jnp.arange(experts, dtype=jnp.int32)
    hot = jnp.sum((routes[:, :, None] == ids[None, None, :]).astype(f32), axis=1)
    hot_low = hot.astype(bf16)
    before = jnp.asarray(np.tril(np.ones((tok, tok)), -1), bf16)
    rank = dot(before, hot_low)
    spread_np = np.repeat(np.eye(experts), cap, axis=1)
    spread = jnp.asarray(spread_np, bf16)
    wide = dot(jnp.where(hot > 0, rank, -1.0).astype(bf16), spread)
    place = (wide == jnp.asarray(np.arange(slots) % cap, f32)[None, :]).astype(bf16)

    pad = jnp.zeros((tok, 128 - experts), bf16)
    g_send = dot(place, jnp.concatenate([cotangent, hot_low, pad], axis=1), ((0,), (0,))).astype(bf16)
    g_send = after(g_send.reshape(experts, cap, model + 128), packed)
    g_all = exchange(g_send, COLUMN).reshape(slots, model + 128)
    g_rows, hot_rows = g_all[:, :model], g_all[:, model : model + experts].astype(f32)

    gu_shard = gate_up_weight.reshape(2, model, 2 * ff_own)
    gu_bias_row = gate_up_bias.reshape(2, 1, 2 * ff_own)
    gu_shard = jnp.concatenate(
        [gu_shard, gu_bias_row, jnp.zeros((2, 15, 2 * ff_own), bf16)], axis=1
    )
    gu_pair = exchange(gu_shard, "c")
    gu_pair = gu_pair.reshape(2, model + 16, 2, ff_own).transpose(1, 2, 0, 3).reshape(model + 16, 4 * ff_own)
    gu_full = lax.all_gather(gu_pair, "y", axis=0)
    w_gate_up = gu_full[:, :model]
    b_gate_up = gu_full[:, model].astype(f32)
    down_pair = exchange(down_weight, "c").reshape(2 * ff_own, model)
    w_down = lax.all_gather(down_pair, "y", axis=0, tiled=True)
    b_down = lax.dynamic_index_in_dim(down_bias, core, 0, keepdims=True).astype(f32)

    bias_qkv = jnp.concatenate([q_bias, key_bias, value_bias]).astype(f32)
    qkv = dot(block_h, w_qkv) + bias_qkv[None]
    positions = seq_index * rows + jnp.arange(rows, dtype=jnp.int32)
    cosine, sine = rotary_tables(positions)
    q_low = rotate(qkv[:, :128].reshape(rows, 2, 64), cosine, sine).astype(bf16)
    k_low = rotate(qkv[:, 128:192].reshape(rows, 1, 64), cosine, sine).astype(bf16)[:, 0]
    v_low = qkv[:, 192:].astype(bf16)
    kv = jnp.concatenate([k_low, v_low], axis=1)
    steps = [(s, s + 1) for s in range(seqs - 1)]
    halo = lax.ppermute(kv[rows - window :], SEQ, steps)
    blocks = rows // window
    kv_all = jnp.concatenate([halo, kv], axis=0).reshape(blocks + 1, window, 128)
    kv_win = jnp.concatenate([kv_all[:-1], kv_all[1:]], axis=1)
    k_win, v_win = kv_win[..., :64], kv_win[..., 64:]
    q_blk = q_low.reshape(blocks, window, 2, 64)
    qi = np.arange(window)[:, None]
    ki = np.arange(2 * window)[None, :]
    off = qi + window - ki
    band = jnp.asarray((off >= 0) & (off < window))[None]
    first = (jnp.arange(blocks) + seq_index * blocks) == 0
    allowed = band & ~(first[:, None, None] & jnp.asarray(ki < window)[None])
    sink_logits = sinks.astype(f32)[None, :, None]

    def score_table():
        raw = jnp.einsum("brgd,bsd->bgrs", q_blk, k_win, preferred_element_type=f32) * scale
        return jnp.where(allowed[:, None], raw, masked_score)

    scores = score_table()
    row_top = jnp.maximum(jnp.max(scores, axis=-1), sink_logits)
    weights = jnp.exp(scores - row_top[..., None])
    denominator = jnp.sum(weights, axis=-1) + jnp.exp(sink_logits - row_top)
    log_denom = row_top + jnp.log(denominator)
    probs_low = (weights / denominator[..., None]).astype(bf16)
    attended = jnp.einsum("bgrs,bsd->brgd", probs_low, v_win, preferred_element_type=f32)
    attn_low = attended.reshape(rows, 128).astype(bf16)
    partial_out = dot(attn_low, w_o, ((1,), (1,)))

    residual = x_float + sum_block(partial_out, ys, tok) + o_bias.astype(f32)
    gain_two = moe_gain.astype(f32)
    r_root = inv_rms(residual)
    normed = residual * r_root
    h2_low = (normed * gain_two).astype(bf16)
    logits = dot(h2_low, router_weight) + router_bias.astype(f32)

    def gates(values, mask):
        masked = jnp.where(mask > 0, values, masked_score)
        top_value = jnp.max(masked, axis=-1, keepdims=True)
        ex = jnp.where(mask > 0, jnp.exp(masked - top_value), 0.0)
        total = jnp.sum(ex, axis=-1, keepdims=True)
        return ex / jnp.where(total > 0, total, 1.0)

    gate_probs = gates(logits, hot)

    h2_send = dot(place, h2_low, ((0,), (0,))).astype(bf16).reshape(experts, cap, model)
    rows_in = exchange(h2_send, COLUMN).reshape(slots, model)

    u = dot(g_rows, w_down, ((1,), (1,)))
    row_logits = dot(rows_in, router_weight) + router_bias.astype(f32)
    mine = (ids == 2 * seq_index + core).astype(f32)
    p_rows = jnp.sum(gates(row_logits, hot_rows) * mine, axis=-1, keepdims=True)
    pre = jnp.einsum("rd,ydn->yrn", rows_in, w_gate_up, preferred_element_type=f32) + b_gate_up[:, None]
    half = 2 * ff_own
    hidden, act_back = jax.vjp(expert_act, pre[..., :half], pre[..., half:])
    hidden_low = hidden.astype(bf16)
    u_blk = u.reshape(slots, ys, half).transpose(1, 0, 2)
    grad_gate_row = jnp.sum(hidden_low.astype(f32) * u_blk, axis=(0, 2)) + jnp.sum(
        g_rows.astype(f32) * b_down, axis=-1
    )
    dgate_back = exchange(grad_gate_row.reshape(experts, cap), COLUMN).reshape(slots)
    d_gate, d_up = act_back(p_rows[None] * u_blk)
    grad_pre = jnp.concatenate([d_gate, d_up], axis=-1).astype(bf16)
    grad_in = jnp.einsum("yrn,ydn->rd", grad_pre, w_gate_up, preferred_element_type=f32).astype(bf16)
    grad_back = exchange(grad_in.reshape(experts, cap, model), COLUMN).reshape(slots, model)

    y_rows = p_rows * (jnp.einsum("yrh,yhd->rd", hidden_low, w_down.reshape(ys, half, model), preferred_element_type=f32) + b_down)
    y_send = after(y_rows.astype(bf16).reshape(experts, cap, model), grad_back)
    y_back = exchange(y_send, COLUMN).reshape(slots, model)
    block_out = (residual + dot(place, y_back)).astype(bf16)

    dy = (p_rows * g_rows.astype(f32)).astype(bf16)
    grad_down_bias = jnp.sum(dy, axis=0, dtype=f32)
    grad_down = jnp.einsum("yrh,rd->yhd", hidden_low, dy, preferred_element_type=f32)
    grad_gu = jnp.einsum("rd,yrn->ydn", rows_in, grad_pre, preferred_element_type=f32)
    grad_gu_bias = jnp.sum(grad_pre, axis=1, dtype=f32)

    mix = cotangent.astype(f32)
    grad_gate = dot_f32(place.astype(f32) * dgate_back[None, :], jnp.asarray(spread_np.T, f32))
    grad_logits = gate_probs * (grad_gate - jnp.sum(gate_probs * grad_gate, axis=-1, keepdims=True))
    router_float = router_weight.astype(f32)
    grad_h2 = dot(place, grad_back) + jnp.einsum("te,de->td", grad_logits, router_float, precision=highest)
    grad_router_w = jnp.einsum("td,te->de", h2_low.astype(f32), grad_logits, precision=highest)
    grad_router_b = jnp.sum(grad_logits, axis=0)

    def norm_back(grad, value_normed, root, gain):
        scaled = grad * gain
        inner = jnp.mean(scaled * value_normed, axis=-1, keepdims=True)
        return root * (scaled - value_normed * inner)

    grad_gain_two = jnp.sum(grad_h2 * normed, axis=0)
    grad_res = mix + norm_back(grad_h2, normed, r_root, gain_two)
    grad_o_bias = jnp.sum(grad_res, axis=0)
    block_grad = gather_block(grad_res.astype(bf16))

    grad_att = dot(block_grad, w_o).astype(bf16).reshape(blocks, window, 2, 64)
    grad_wo = dot(block_grad, attn_low, ((0,), (0,)))
    soft = jnp.exp(score_table() - log_denom[..., None])
    grad_probs = jnp.einsum("brgd,bsd->bgrs", grad_att, v_win, preferred_element_type=f32)
    row_delta = jnp.sum(soft * grad_probs, axis=-1)
    grad_scores = (soft * (grad_probs - row_delta[..., None])).astype(bf16)
    grad_sinks = -jnp.sum(jnp.exp(sink_logits - log_denom) * row_delta, axis=(0, 2))
    grad_q = jnp.einsum("bgrs,bsd->brgd", grad_scores, k_win, preferred_element_type=f32) * scale
    grad_k = jnp.einsum("bgrs,brgd->bsd", grad_scores, q_blk, preferred_element_type=f32) * scale
    grad_v = jnp.einsum("bgrs,brgd->bsd", soft.astype(bf16), grad_att, preferred_element_type=f32)
    grad_kv = jnp.concatenate([grad_k, grad_v], axis=-1)
    back = [(s + 1, s) for s in range(seqs - 1)]
    returned = lax.ppermute(grad_kv[0, :window].astype(bf16), SEQ, back).astype(f32)
    prior = jnp.concatenate([grad_kv[1:, :window], returned[None]], axis=0)
    grad_kv = (grad_kv[:, window:] + prior).reshape(rows, 128)
    dq_pre = rotate(grad_q.reshape(rows, 2, 64), cosine, -sine).reshape(rows, 128).astype(bf16)
    dk_pre = rotate(grad_kv[:, None, :64], cosine, -sine).reshape(rows, 64).astype(bf16)
    dqkv = jnp.concatenate([dq_pre, dk_pre, grad_kv[:, 64:].astype(bf16)], axis=1)
    grad_wqkv = dot(block_h, dqkv, ((0,), (0,)))
    grad_bqkv = jnp.sum(dqkv, axis=0, dtype=f32)
    gain_part = jnp.sum(w_qkv.astype(f32) * grad_wqkv, axis=1) / gain_one
    grad_h = sum_block(dot(dqkv, w_qkv, ((1,), (1,))), ys, tok)
    x_normed = x_float * x_root
    tokens_grad = (grad_res + norm_back(grad_h, x_normed, x_root, gain_one)).astype(bf16)

    grad_w = jnp.concatenate([grad_wqkv, grad_wo], axis=1).astype(bf16).reshape(seqs, model // seqs, 384)
    grad_w = jnp.sum(exchange(grad_w, SEQ).astype(f32), axis=0)
    small = jnp.concatenate([grad_bqkv, grad_sinks, jnp.zeros((126,), f32), gain_part])
    small = jnp.sum(broadcast_exchange(small.reshape(-1, 128), SEQ, seqs).reshape(seqs, -1), axis=0)
    gain_sum = jnp.sum(broadcast_exchange(small[384:].reshape(-1, 128), FSDP, ys * 2).reshape(ys * 2, -1), axis=0)

    whole = jnp.concatenate(
        [grad_router_w.reshape(-1), grad_router_b, grad_o_bias, grad_gain_two, jnp.zeros((2016,), f32)]
    ).reshape(-1, 288)
    whole = jnp.sum(exchange(whole, ALL), axis=0)
    whole = broadcast_exchange(whole, ALL, seqs * ys * 2).reshape(-1)
    router_w_grad = whole[: model * experts].reshape(model, experts)
    rest = whole[model * experts :]

    gu_out = jnp.concatenate(
        [grad_gu, grad_gu_bias[:, None], jnp.zeros((ys, 15, 2 * half), f32)], axis=1
    ).astype(bf16)
    gu_out = jnp.sum(exchange(gu_out, "y").astype(f32), axis=0).astype(bf16)
    gu_out = gu_out.reshape(model + 16, 2, 2, ff_own).transpose(2, 0, 1, 3).reshape(2, model + 16, 2 * ff_own)
    gu_out = exchange(gu_out, "c").astype(f32)
    grad_gu_own = gu_out[:, :model].reshape(2, model, 2, ff_own)
    grad_gub_own = gu_out[:, model].reshape(2, 2, ff_own)
    down_out = jnp.sum(exchange(grad_down.astype(bf16), "y").astype(f32), axis=0).astype(bf16)
    down_out = exchange(down_out.reshape(2, ff_own, model), "c").astype(f32)
    db = jnp.sum(broadcast_exchange(grad_down_bias[None], "y", ys), axis=0)
    db = broadcast_exchange(db, "c", 2).reshape(2, model)

    return (
        block_out, tokens_grad, gain_sum,
        grad_w[:, :128], small[:128], grad_w[:, 128:192], small[128:192], grad_w[:, 192:256], small[192:256],
        grad_w[:, 256:].T, rest[32 : 32 + model], small[256:258], rest[32 + model : 32 + 2 * model],
        router_w_grad, rest[:32],
        grad_gu_own, grad_gub_own, down_out, db,
    )


def dot_f32(a, b):
    return jnp.dot(a, b, precision=highest)


def solution(mesh):
    sizes = dict(mesh.shape)
    side = int(round(sizes["seq"] ** 0.5))
    wide = Mesh(
        mesh.devices.reshape(side, sizes["seq"] // side, sizes["fsdp"] // 2, 2), ("x", "z", "y", "c")
    )
    in_specs = (
        P(ALL, None), P(ALL, None), P(), P(SEQ, FSDP), P(FSDP), P(SEQ, FSDP), P(FSDP), P(SEQ, FSDP), P(FSDP),
        P(FSDP, SEQ), P(), P(FSDP), P(), P(), P(), P(SEQ, None, None, FSDP), P(SEQ, None, FSDP),
        P(SEQ, FSDP, None), P(SEQ, None), P(ALL, None),
    )
    out_specs = (
        P(ALL, None), P(ALL, None), P(), P(SEQ, FSDP), P(FSDP), P(SEQ, FSDP), P(FSDP), P(SEQ, FSDP), P(FSDP),
        P(FSDP, SEQ), P(), P(FSDP), P(), P(), P(), P(SEQ, None, None, FSDP), P(SEQ, None, FSDP),
        P(SEQ, FSDP, None), P(SEQ, None),
    )
    return jax.shard_map(shards, mesh=wide, in_specs=in_specs, out_specs=out_specs, check_vma=False)
```

```python
import jax
import jax.numpy as jnp
import numpy as np
from jax import lax
from jax.experimental import pallas as pl
from jax.experimental.pallas import tpu as pltpu
from jax.sharding import Mesh, PartitionSpec as P

HEAD_WIDTH = 64
WINDOW = 128
norm_eps = 1e-05
rope_base = 150000.0
swiglu_limit = 7.0
glu_alpha = 1.702
masked_score = -1000000000.0

SEQ = ("x", "z")
FSDP = ("y", "c")
COLUMN = ("x", "z", "c")
ALL = ("x", "z", "y", "c")
f32 = jnp.float32
bf16 = jnp.bfloat16
SCALE = HEAD_WIDTH ** (-0.5)
SHIFTS = (0, 1, -1, 2)


def dot(a, b, dims=((1,), (0,))):
    return lax.dot_general(a, b, (dims, ((), ())), preferred_element_type=f32)


ROWS_BY = ((0,), (0,))
BY_ROWS = ((1,), (1,))


def inv_rms(values):
    return lax.rsqrt(jnp.mean(values * values, axis=-1, keepdims=True) + norm_eps)


def norm_back(grad, normed, root, gain):
    scaled = grad * gain
    return root * (scaled - normed * jnp.mean(scaled * normed, axis=-1, keepdims=True))


def halves(value):
    high = value.astype(bf16)
    return high, (value - high.astype(f32)).astype(bf16)


def lanes(shape):
    return lax.broadcasted_iota(jnp.int32, shape, len(shape) - 1)


def sublanes(shape):
    return lax.broadcasted_iota(jnp.int32, shape, len(shape) - 2)


def swap_halves(values):
    lane = lanes(values.shape) % HEAD_WIDTH
    return jnp.where(lane < 32, pltpu.roll(values, 96, 1), pltpu.roll(values, 32, 1))


def turn(values, cos, sin):
    return values * cos + swap_halves(values) * sin


def exchange(value, axes):
    return lax.all_to_all(value, axes, split_axis=0, concat_axis=0, tiled=True)


def broadcast_exchange(value, axes, count):
    return exchange(jnp.broadcast_to(value[None], (count,) + value.shape), axes)


def after(value, *earlier):
    return lax.optimization_barrier((value,) + earlier)[0]


def along_y(value, steps):
    count = lax.axis_size("y")
    return lax.ppermute(value, "y", [(k, (k + steps) % count) for k in range(count)])


def other_core(value):
    return lax.ppermute(value, "c", [(0, 1), (1, 0)])


def kernel_call(body, outs, ins, flops=0, scalars=1, scratch=(), vmem=40):
    specs = [pl.BlockSpec(memory_space=pltpu.SMEM)] * scalars
    specs += [pl.BlockSpec(memory_space=pltpu.VMEM)] * (len(ins) - scalars)
    out_shape = [jax.ShapeDtypeStruct(shape, kind) for shape, kind in outs]
    moved = sum(a.size * a.dtype.itemsize for a in ins)
    moved += sum(s.size * jnp.dtype(s.dtype).itemsize for s in out_shape)
    return pl.pallas_call(
        body,
        out_shape=out_shape,
        in_specs=specs,
        out_specs=[pl.BlockSpec(memory_space=pltpu.VMEM)] * len(outs),
        scratch_shapes=scratch,
        compiler_params=pltpu.CompilerParams(vmem_limit_bytes=vmem << 20),
        cost_estimate=pl.CostEstimate(flops=flops, bytes_accessed=moved, transcendentals=0),
    )(*ins)


def norm_body(x_ref, gain_ref, q_ref, k_ref, v_ref, o_ref, h_ref, packed_ref):
    x = x_ref[...].astype(f32)
    h_ref[...] = (x * inv_rms(x) * gain_ref[...].astype(f32)).astype(bf16)
    packed = jnp.concatenate([q_ref[...], k_ref[...], v_ref[...], o_ref[...]], axis=1)
    for n in range(packed_ref.shape[0]):
        packed_ref[n] = packed


def waves(within_ref, base_ref, b):
    cos_in, sin_in = within_ref[:WINDOW, :], within_ref[WINDOW:, :]
    cos_at, sin_at = base_ref[b : b + 1, :], base_ref[16 + b : 17 + b, :]
    sine = sin_at * cos_in + cos_at * sin_in
    first = lanes(sine.shape) % HEAD_WIDTH < HEAD_WIDTH // 2
    return cos_at * cos_in - sin_at * sin_in, jnp.where(first, -sine, sine)


def plan_body(cap, experts, routes_ref, g_ref, place_ref, send_ref):
    tok, top = routes_ref.shape
    model = g_ref.shape[1]
    slots = place_ref.shape[1]
    routes = routes_ref[...]
    ids = lanes((tok, 128))
    hot = jnp.zeros((tok, 128), f32)
    for k in range(top):
        hot += (routes[:, k : k + 1] == ids).astype(f32)
    hot_low = hot.astype(bf16)
    before = (lanes((tok, tok)) < sublanes((tok, tok))).astype(f32).astype(bf16)
    rank = dot(before, hot_low)
    marked = jnp.where(hot > 0, rank, -1.0).astype(bf16)
    slot = lanes((128, slots))
    start = sublanes((128, slots)) * cap
    spread = ((slot >= start) & (slot < start + cap)).astype(f32).astype(bf16)
    wide = dot(marked, spread)
    lane = lanes((tok, slots)).astype(f32)
    within = lane - cap * jnp.floor((lane + 0.5) * (1.0 / cap))
    place = (wide == within).astype(f32).astype(bf16)
    place_ref[...] = place
    send_ref[:, :model] = dot(place, g_ref[...], ROWS_BY).astype(bf16)
    send_ref[:, model:] = dot(place, hot_low, ROWS_BY).astype(bf16)


def assemble(at_ref, pieces, block_ref, tok, ys):
    y, core = at_ref[0], at_ref[1]
    for n, piece in enumerate(pieces):
        from_y = lax.rem(y - SHIFTS[n % 4] + ys, ys)
        from_core = core if n < 4 else 1 - core
        start = pl.multiple_of((from_y * 2 + from_core) * tok, tok)
        block_ref[pl.ds(start, tok), :] = piece[...]


def project_body(ys, at_ref, sink_ref, *refs):
    block_ref, halos, refs = refs[0], refs[1:5], refs[5:]
    w_ref, bias_ref, within_ref, base_ref = refs[:4]
    q_ref, k_ref, v_ref, att_ref, out_ref, halo_ref = refs[4:]
    rows = block_ref.shape[0]
    tok = rows // (2 * ys)
    halo_ref[...] = halos[0][...] + halos[1][...] + halos[2][...] + halos[3][...]
    weights = w_ref[:, :256]
    low = lanes((WINDOW, 128)) < 64

    def keys_values(kv, b, wave):
        at = slice(b * WINDOW, (b + 1) * WINDOW)
        turned = pltpu.roll(kv, 64, 1)
        k_ref[at, :] = turn(jnp.where(low, kv, turned), *wave).astype(bf16)
        v_ref[at, :] = jnp.where(low, turned, kv).astype(bf16)

    keys_values(dot(halo_ref[...], weights[:, 128:]) + bias_ref[:, 128:], 0, waves(within_ref, base_ref, 0))
    for r in range(0, rows, 2 * WINDOW):
        both = dot(block_ref[r : r + 2 * WINDOW, :], weights) + bias_ref[...]
        for k in range(2):
            qkv = both[k * WINDOW : (k + 1) * WINDOW]
            b = r // WINDOW + k
            wave = waves(within_ref, base_ref, b + 1)
            q_ref[b * WINDOW : (b + 1) * WINDOW, :] = turn(qkv[:, :128], *wave).astype(bf16)
            keys_values(qkv[:, 128:], b + 1, wave)
    sink = sink_column(sink_ref)
    for b in range(rows // WINDOW):
        part = slice(b * WINDOW, (b + 1) * WINDOW)
        near = slice(b * WINDOW, (b + 2) * WINDOW)
        q2 = stack_heads(q_ref[part, :])
        probs, _ = soft_rows(q2, k_ref[near, :], band(at_ref, b == 0), sink)
        both = dot(probs.astype(bf16), v_ref[near, :])
        att_ref[part, :] = jnp.where(low, both[:WINDOW], both[WINDOW:]).astype(bf16)
    to_other(at_ref, att_ref, w_ref[:, 256:384], out_ref, tok, ys)


def band(at_ref, first):
    shape = (2 * WINDOW, 2 * WINDOW)
    i, j = sublanes(shape), lanes(shape)
    off = jnp.where(i >= WINDOW, i - WINDOW, i) + WINDOW - j
    allowed = (off >= 0) & (off < WINDOW)
    if first:
        allowed = allowed & ((j >= WINDOW) | (at_ref[2] > 0))
    return allowed


def stack_heads(pair):
    low = lanes(pair.shape) < 64
    zero = jnp.zeros_like(pair)
    return jnp.concatenate([jnp.where(low, pair, zero), jnp.where(low, zero, pair)], axis=0)


def soft_rows(q2, keys, allowed, sink):
    scores = jnp.where(allowed, dot(q2, keys, BY_ROWS) * SCALE, masked_score)
    top = jnp.maximum(jnp.max(scores, axis=-1, keepdims=True), sink)
    weights = jnp.exp(scores - top)
    sunk = jnp.exp(sink - top)
    inverse = 1.0 / (jnp.sum(weights, axis=-1, keepdims=True) + sunk)
    return weights * inverse, sunk * inverse


def sink_column(sink_ref):
    row = sublanes((2 * WINDOW, 1))
    return jnp.where(row < WINDOW, sink_ref[0], sink_ref[1])


def to_other(at_ref, rows_ref, weights, out_ref, tok, ys):
    for n, shift in enumerate(SHIFTS):
        to_y = lax.rem(at_ref[0] + shift + ys, ys)
        theirs = pl.multiple_of((to_y * 2 + 1 - at_ref[1]) * tok, tok)
        out_ref[n] = dot(rows_ref[pl.ds(theirs, tok), :], weights, BY_ROWS).astype(bf16)


def pair_body(ys, lo, hi, at_ref, rows_ref, w_ref, other_ref, *outs):
    tok = other_ref.shape[1]
    for n, shift in enumerate(SHIFTS):
        to_y = lax.rem(at_ref[0] + shift + ys, ys)
        mine = pl.multiple_of((to_y * 2 + at_ref[1]) * tok, tok)
        own = dot(rows_ref[pl.ds(mine, tok), :], w_ref[:, lo:hi], BY_ROWS)
        outs[n][...] = (own + other_ref[n].astype(f32)).astype(outs[n].dtype)


def gates(values, mask):
    masked = jnp.where(mask, values, masked_score)
    ex = jnp.where(mask, jnp.exp(masked - jnp.max(masked, axis=-1, keepdims=True)), 0.0)
    total = jnp.sum(ex, axis=-1, keepdims=True)
    return ex / jnp.where(total > 0, total, 1.0)


def route_body(
    cap, first_ref, a_ref, b_ref, c_ref, x_ref, ob_ref, gain_ref, rw_ref, rb_ref, place_ref, routes_ref,
    res_ref, h2_ref, gate_ref, send_ref,
):
    tok, experts = gate_ref.shape
    total = first_ref[...] + a_ref[...].astype(f32) + b_ref[...].astype(f32) + c_ref[...].astype(f32)
    residual = x_ref[...].astype(f32) + total + ob_ref[...].astype(f32)
    res_ref[...] = residual
    h2 = (residual * inv_rms(residual) * gain_ref[...].astype(f32)).astype(bf16)
    h2_ref[...] = h2
    send_ref[...] = dot(place_ref[...], h2, ROWS_BY).astype(bf16)
    logits = dot(h2, rw_ref[...]) + rb_ref[...].astype(f32)
    routes = routes_ref[...]
    ids = lanes((tok, experts))
    hot = jnp.zeros((tok, experts), f32)
    for k in range(routes.shape[1]):
        hot += (routes[:, k : k + 1] == ids).astype(f32)
    gate_ref[...] = gates(logits, hot > 0)


def expert_body(
    ys, at_ref, rows_ref, side_ref, u_ref, w_ref, rw_ref, rb_ref, hidden_ref, dpre_ref, early_ref, back_ref, p_ref
):
    model = rows_ref.shape[1]
    experts = rw_ref.shape[1]
    rows = rows_ref[...]
    count = rows.shape[0]
    logits = dot(rows, rw_ref[...]) + rb_ref[...].astype(f32)
    mask = side_ref[:, :experts] > 0
    mine = lanes((count, experts)) == at_ref[3]
    p = jnp.sum(jnp.where(mine, gates(logits, mask), 0.0), axis=-1, keepdims=True)
    p_ref[...] = jnp.broadcast_to(p, p_ref.shape)
    dgate = side_ref[:, experts : experts + 1]
    grad = jnp.zeros((count, model), f32)
    half = (w_ref.shape[1] - 16) // 3
    own = half // 2
    for n in range(ys):
        weights = w_ref[n, : 2 * half, :]
        first, second = w_ref[n, 3 * half : 3 * half + 1, :half], w_ref[n, 3 * half + 8 : 3 * half + 9, :half]
        bias = jnp.concatenate([first[:, :own], second[:, :own], first[:, own:], second[:, own:]], axis=1)
        pre = dot(rows, weights, BY_ROWS) + bias.astype(f32)
        gt = jnp.tanh(pre[:, :half] * (1.0 / swiglu_limit))
        ut = jnp.tanh(pre[:, half:] * (1.0 / swiglu_limit))
        gate, up = swiglu_limit * gt, swiglu_limit * ut + 1.0
        sig = jax.nn.sigmoid(glu_alpha * gate)
        gs = gate * sig
        hidden = (up * gs).astype(bf16)
        u = u_ref[:, n * half : (n + 1) * half]
        dgate += jnp.sum(hidden.astype(f32) * u, axis=-1, keepdims=True)
        hidden_ref[:, n * half : (n + 1) * half] = hidden
        dh = p * u
        d_gate = dh * up * (sig + glu_alpha * gs * (1.0 - sig)) * (1.0 - gt * gt)
        d_up = dh * gs * (1.0 - ut * ut)
        dpre = jnp.concatenate([d_gate, d_up], axis=1).astype(bf16)
        dpre_ref[:, 2 * n * half : 2 * (n + 1) * half] = dpre
        grad += dot(dpre, weights)
    early_ref[:, 128:] = grad[:, :128].astype(bf16)
    back_ref[...] = grad[:, 128:].astype(bf16)
    high, rest = halves(dgate)
    middle, low = halves(dgate - high.astype(f32))
    lane = lanes((count, 128))
    parts = jnp.where(lane == 0, high.astype(f32), jnp.where(lane == 1, middle.astype(f32), low.astype(f32)))
    early_ref[:, :128] = jnp.where(lane < 3, parts, 0.0).astype(bf16)


def by_chunks(body, step, at, cut_in, whole_in, outs, flops):
    slots = cut_in[0].shape[0]

    def cut(width):
        return pl.BlockSpec((step, width), lambda n: (n, 0))

    def whole(a):
        return pl.BlockSpec(a.shape, lambda n: (0,) * a.ndim)

    return pl.pallas_call(
        body,
        grid=(slots // step,),
        out_shape=[jax.ShapeDtypeStruct((slots, w_), kind) for w_, kind in outs],
        in_specs=[pl.BlockSpec(memory_space=pltpu.SMEM)]
        + [cut(a.shape[1]) for a in cut_in]
        + [whole(a) for a in whole_in],
        out_specs=[cut(w_) for w_, _ in outs],
        compiler_params=pltpu.CompilerParams(vmem_limit_bytes=60 << 20),
        cost_estimate=pl.CostEstimate(flops=flops, bytes_accessed=16 << 20, transcendentals=0),
    )(at, *cut_in, *whole_in)


def split_experts_body(at_ref, gu_ref, down_ref, bias_ref, own_ref, theirs_ref):
    wide, half = gu_ref.shape[1], down_ref.shape[1]
    for ref, expert in ((own_ref, at_ref[1]), (theirs_ref, 1 - at_ref[1])):
        ref[:wide, :] = gu_ref[expert]
        ref[wide : wide + half, :] = down_ref[expert]
        ref[wide + half :, :] = jnp.zeros((16, ref.shape[1]), bf16)
        ref[wide + half : wide + half + 1, :wide] = bias_ref[expert]


def join_experts_body(own_ref, theirs_ref, out_ref):
    half = (own_ref.shape[0] - 16) // 3
    for n in range(3):
        part = slice(n * half, (n + 1) * half)
        out_ref[2 * n * half : (2 * n + 1) * half, :] = own_ref[part, :]
        out_ref[(2 * n + 1) * half : (2 * n + 2) * half, :] = theirs_ref[part, :]
    out_ref[6 * half :, :] = jnp.concatenate(
        [own_ref[3 * half : 3 * half + 8, :], theirs_ref[3 * half : 3 * half + 8, :]], axis=0
    )


def early_body(experts, at_ref, g_ref, w_ref, bd_ref, u_ref, side_ref):
    model = w_ref.shape[2]
    half = (w_ref.shape[1] - 16) // 3
    g = g_ref[:, :model]
    for n in range(w_ref.shape[0]):
        u_ref[:, n * half : (n + 1) * half] = dot(g, w_ref[n, 2 * half : 3 * half, :], BY_ROWS)
    bias = jnp.sum(g.astype(f32) * bd_ref[...], axis=-1, keepdims=True)
    hot = g_ref[:, model:].astype(f32)
    side_ref[...] = jnp.where(lanes(hot.shape) < experts, hot, bias)


def weights_body(ys, at_ref, rows_ref, g_ref, hidden_ref, dpre_ref, p_ref, w_ref, bd_ref, y_ref, sum_ref, gain_ref):
    slots, model = rows_ref.shape
    ff = hidden_ref.shape[1]
    half = ff // ys
    step = 256
    w_down = jnp.concatenate([w_ref[n, 2 * half : 3 * half, :] for n in range(ys)], axis=0)
    dys = []
    bias = jnp.zeros((1, model), f32)
    for r in range(0, slots, step):
        part = slice(r, r + step)
        p = p_ref[part, :1]
        y = dot(hidden_ref[part, :], w_down) + bd_ref[...]
        y_ref[part, :] = (p * y).astype(bf16)
        dy = (p * g_ref[part, :model].astype(f32)).astype(bf16)
        bias += jnp.sum(dy.astype(f32), axis=0, keepdims=True)
        dys.append(dy)
    dy = jnp.concatenate(dys, axis=0)
    high, low = halves(bias)
    row = sublanes((16, model))
    gain = jnp.zeros((1, model), f32)
    for n in range(ys):
        dpre = dpre_ref[:, 2 * n * half : 2 * (n + 1) * half]
        dw = dot(dpre, rows_ref[...], ROWS_BY)
        gain += jnp.sum(dw * w_ref[n, : 2 * half, :].astype(f32), axis=0, keepdims=True)
        sum_ref[n, : 2 * half, :] = dw.astype(bf16)
        hidden = hidden_ref[:, n * half : (n + 1) * half]
        sum_ref[n, 2 * half : 3 * half, :] = dot(hidden, dy, ROWS_BY).astype(bf16)
        b = jnp.sum(dpre.astype(f32), axis=0, keepdims=True)
        b = jnp.concatenate([b, jnp.zeros((1, model - 2 * half), f32)], axis=1)
        tail = jnp.where(row == 1, high.astype(f32), jnp.where(row == 2, low.astype(f32), 0.0))
        sum_ref[n, 3 * half :, :] = jnp.where(row == 0, b, tail).astype(bf16)
    gain_ref[...] = gain


def experts_out_body(at_ref, own_ref, theirs_ref, gu_ref, down_ref, gub_ref, db_ref):
    core = at_ref[1]
    half = down_ref.shape[1]
    gu_ref[core, :half, :] = own_ref[:half, :].astype(f32)
    gu_ref[core, half:, :] = own_ref[2 * half : 3 * half, :].astype(f32)
    gu_ref[1 - core] = theirs_ref[: 2 * half, :].astype(f32)
    down_ref[core] = own_ref[4 * half : 5 * half, :].astype(f32)
    down_ref[1 - core] = theirs_ref[2 * half : 3 * half, :].astype(f32)
    own, theirs = own_ref[6 * half :, :].astype(f32), theirs_ref[3 * half :, :].astype(f32)

    def by_expert(mine, other):
        return jnp.where(sublanes((2, mine.shape[1])) == core, mine, other)

    mine = jnp.concatenate([own[:1, :half], own[:1, 2 * half : 3 * half]], axis=1)
    other = jnp.concatenate([theirs[:1, half : 2 * half], theirs[:1, 3 * half : 4 * half]], axis=1)
    gub_ref[...] = by_expert(mine, other)
    db_ref[...] = by_expert(own[1:2] + own[2:3], theirs[1:2] + theirs[2:3])


def sums_body(in_ref, q_ref, k_ref, v_ref, o_ref, small_ref, last_ref):
    total = in_ref[0].astype(f32)
    for n in range(1, in_ref.shape[0]):
        total += in_ref[n].astype(f32)
    share = q_ref.shape[0]
    q_ref[...] = total[:share, :128]
    k_ref[...] = total[:share, 128:192]
    v_ref[...] = total[:share, 192:256]
    o_ref[...] = total[:share, 256:]
    sums = jnp.concatenate([total[share:, :128], total[share:, 128:256], total[share:, 256:]], axis=0)
    small_ref[...] = sums[32:40]
    for n in range(last_ref.shape[0]):
        last_ref[n] = sums


def last_body(in_ref, router_ref, vectors_ref):
    experts = router_ref.shape[0]
    for n in range(in_ref.shape[0]):
        router_ref[:, n * 128 : (n + 1) * 128] = in_ref[n, :experts, :]
    row = sublanes((8, 128))
    o_bias = gain_two = gain_one = jnp.zeros((8, 128), f32)
    for n in range(in_ref.shape[0]):
        o_bias = jnp.where(row == n, in_ref[n, experts : experts + 1, :], o_bias)
        gain_two = jnp.where(row == n, in_ref[n, experts + 1 : experts + 2, :], gain_two)
        gain_one = gain_one + in_ref[n, experts + 8 :, :]
    vectors_ref[:8, :] = o_bias
    vectors_ref[8:16, :] = gain_two
    vectors_ref[16:24, :] = gain_one
    vectors_ref[24:, :] = in_ref[0, experts : experts + 8, :]


def logits_back_body(cap, early_ref, place_ref, gate_ref, h2_ref, rw_ref, part_ref, gain_ref, grad_ref, sums_ref):
    tok, experts = gate_ref.shape
    slots = place_ref.shape[1]
    place = place_ref[...]
    slot = sublanes((slots, experts))
    start = lanes((slots, experts)) * cap
    own = (slot >= start) & (slot < start + cap)
    dgate = jnp.zeros((tok, experts), f32)
    for k in range(3):
        column = early_ref[:, k : k + 1].astype(f32)
        dgate += dot(place, jnp.where(own, column, 0.0).astype(bf16))
    gate = gate_ref[...]
    dlogits = gate * (dgate - jnp.sum(gate * dgate, axis=-1, keepdims=True))
    high, low = halves(dlogits)
    router = rw_ref[...]
    grad = dot(high, router, BY_ROWS) + dot(low, router, BY_ROWS)
    grad_ref[...] = grad
    h2 = h2_ref[...]
    router_grad = dot(high, h2, ROWS_BY) + dot(low, h2, ROWS_BY)
    gain = part_ref[...] + jnp.sum(grad * h2.astype(f32), axis=0, keepdims=True)
    gain = gain / gain_ref[...].astype(f32)
    router_b = jnp.concatenate(
        [jnp.sum(dlogits, axis=0, keepdims=True), jnp.zeros((1, 128 - experts), f32)], axis=1
    )
    for n in range(sums_ref.shape[0]):
        part = slice(n * 128, (n + 1) * 128)
        sums_ref[n, :experts, :] = router_grad[:, part]
        sums_ref[n, experts:, :] = jnp.concatenate(
            [jnp.zeros((1, 128), f32), gain[:, part], router_b, jnp.zeros((13, 128), f32)], axis=0
        )


def unroute_body(early_ref, back_ref, place_ref, grad_ref, res_ref, g_ref, gain_ref, dres_ref, da_ref):
    place = place_ref[...]
    grad = jnp.concatenate([dot(place, early_ref[:, 128:]), dot(place, back_ref[...])], axis=1) + grad_ref[...]
    residual = res_ref[...]
    root = inv_rms(residual)
    dres = g_ref[...].astype(f32) + norm_back(grad, residual * root, root, gain_ref[...].astype(f32))
    dres_ref[...] = dres
    da_ref[...] = dres.astype(bf16)


def block_back(at_ref, sink, b, q_ref, datt_ref, k_ref, v_ref):
    part = slice(b * WINDOW, (b + 1) * WINDOW)
    near = slice(b * WINDOW, (b + 2) * WINDOW)
    low = lanes((WINDOW, 128)) < 64
    q2 = stack_heads(q_ref[part, :])
    g2 = stack_heads(datt_ref[part, :])
    keys = k_ref[near, :]
    probs, sunk = soft_rows(q2, keys, band(at_ref, b == 0), sink)
    dprobs = dot(g2, v_ref[near, :], BY_ROWS)
    delta = jnp.sum(probs * dprobs, axis=-1, keepdims=True)
    dscores = (probs * (dprobs - delta)).astype(bf16)
    dq2 = dot(dscores, keys)
    dq = jnp.where(low, dq2[:WINDOW], dq2[WINDOW:]) * SCALE
    dk2 = dot(dscores, q2, ROWS_BY) * SCALE
    dv2 = dot(probs.astype(bf16), g2, ROWS_BY)
    wide = lanes(dk2.shape) < 64
    dkv = jnp.where(wide, dk2 + pltpu.roll(dk2, 64, 1), dv2 + pltpu.roll(dv2, 64, 1))
    return dq, dkv, sunk * delta


def turn_back(values, cos, sin):
    return values * cos - swap_halves(values) * sin


def back_first_body(ys, at_ref, sink_ref, *refs):
    pieces, refs = refs[:8], refs[8:]
    w_ref, q_ref, k_ref, v_ref = refs[:4]
    block_ref, datt_ref, head_ref, dq_ref, carry_ref, sink_out_ref = refs[4:]
    tok = pieces[0].shape[0]
    assemble(at_ref, pieces, block_ref, tok, ys)
    weights = w_ref[:, 256:384]
    for r in range(0, block_ref.shape[0], 256):
        datt_ref[r : r + 256, :] = dot(block_ref[r : r + 256, :], weights).astype(bf16)
    dq, dkv, sunk = block_back(at_ref, sink_column(sink_ref), 0, q_ref, datt_ref, k_ref, v_ref)
    head_ref[...] = dkv[:WINDOW].astype(bf16)
    carry_ref[...] = dkv[WINDOW:]
    dq_ref[...] = dq
    sink_out_ref[...] = jnp.broadcast_to(sunk, sink_out_ref.shape)


def back_rest_body(
    at_ref, sink_ref, datt_ref, q_ref, k_ref, v_ref, within_ref, base_ref, dq_ref, carry_ref, sunk_ref,
    dqkv_ref, last_ref, sink_out_ref,
):
    rows = q_ref.shape[0]
    sink = sink_column(sink_ref)
    low = lanes((WINDOW, 128)) < 64
    sink_sum = sunk_ref[:, :1]
    carry = carry_ref[...]
    for b in range(rows // WINDOW):
        part = slice(b * WINDOW, (b + 1) * WINDOW)
        wave = waves(within_ref, base_ref, b + 1)
        if b == 0:
            dq = dq_ref[...]
        else:
            dq, dkv, sunk = block_back(at_ref, sink, b, q_ref, datt_ref, k_ref, v_ref)
            sink_sum += sunk
            done = carry + dkv[:WINDOW]
            carry = dkv[WINDOW:]
            before = slice((b - 1) * WINDOW, b * WINDOW)
            dqkv_ref[before, 128:] = jnp.where(low, turn_back(done, *last_wave), done).astype(bf16)
        dqkv_ref[part, :128] = turn_back(dq, *wave).astype(bf16)
        last_wave = wave
    last_ref[...] = carry
    dqkv_ref[rows - WINDOW :, 128:] = jnp.zeros((WINDOW, 128), bf16)
    total0 = jnp.sum(sink_sum[:WINDOW], axis=0, keepdims=True)
    total1 = jnp.sum(sink_sum[WINDOW:], axis=0, keepdims=True)
    lane = lanes((8, 128))
    sink_out_ref[...] = -jnp.where(lane == 0, total0, jnp.where(lane == 1, total1, 0.0))


def unproject_body(ys, tok, at_ref, part_ref, last_ref, ret_ref, within_ref, base_ref, w_ref, dqkv_ref, out_ref):
    rows = part_ref.shape[0]
    low = lanes((WINDOW, 128)) < 64
    dqkv_ref[...] = part_ref[...]
    dkv = last_ref[...] + ret_ref[...].astype(f32)
    turned = turn_back(dkv, *waves(within_ref, base_ref, rows // WINDOW))
    dqkv_ref[rows - WINDOW :, 128:] = jnp.where(low, turned, dkv).astype(bf16)
    to_other(at_ref, dqkv_ref, w_ref[:, :256], out_ref, tok, ys)


def attention_weights_body(
    at_ref, dqkv_ref, block_ref, grad_ref, att_ref, w_ref, gain_ref, sink_ref, sums_ref, send_ref
):
    model = block_ref.shape[1]
    bias = jnp.sum(dqkv_ref[...].astype(f32), axis=0, keepdims=True)
    bias = jnp.concatenate([bias, sink_ref[:1, :]], axis=1)
    step = 256
    seqs = send_ref.shape[0]
    share = model // seqs
    per = step // share
    ones = jnp.ones((8, 256), bf16)
    gains = []
    for d in range(0, model, step):
        dw = dot(block_ref[:, d : d + step], dqkv_ref[...], ROWS_BY)
        dwo = dot(grad_ref[:, d : d + step], att_ref[...], ROWS_BY)
        for k in range(per):
            part = slice(k * share, (k + 1) * share)
            send_ref[d // share + k, :share, :256] = dw[part].astype(bf16)
            send_ref[d // share + k, :share, 256:] = dwo[part].astype(bf16)
        first, second = halves(dw * w_ref[d : d + step, :256].astype(f32))
        gains.append((dot(ones, first, BY_ROWS) + dot(ones, second, BY_ROWS))[:1])
    gain = jnp.concatenate(gains, axis=1) / gain_ref[...].astype(f32)
    row = sublanes((8, 128))
    own = pl.multiple_of((at_ref[0] * 2 + at_ref[1]) * 128, 128)
    o_bias = jnp.sum(grad_ref[:, pl.ds(own, 128)].astype(f32), axis=0, keepdims=True)
    middle = jnp.where(row == 0, o_bias, sums_ref[32:40, :])
    for n, line in enumerate([bias[:, :128], bias[:, 128:256], bias[:, 256:]]):
        middle = jnp.where(row == n + 4, line, middle)
    gain = jnp.concatenate([gain[:, n * 128 : (n + 1) * 128] for n in range(8)], axis=0)
    third = jnp.concatenate([middle, gain], axis=0)
    tail = jnp.concatenate([sums_ref[:16, :], sums_ref[16:32, :], third], axis=1).astype(bf16)
    for s in range(seqs):
        send_ref[s, share:, :] = tail


def finish_body(first_ref, a_ref, b_ref, c_ref, x_ref, gain_ref, dres_ref, out_ref):
    grad = first_ref[...] + a_ref[...].astype(f32) + b_ref[...].astype(f32) + c_ref[...].astype(f32)
    x = x_ref[...].astype(f32)
    root = inv_rms(x)
    out = dres_ref[...] + norm_back(grad, x * root, root, gain_ref[...].astype(f32))
    out_ref[...] = out.astype(bf16)


def gather_pieces(own):
    mine = [own] + list(lax.optimization_barrier(tuple(along_y(own, s) for s in SHIFTS[1:])))
    return mine + [other_core(piece) for piece in mine]


def sum_pieces(ys, at, rows, weights, lo, hi, out):
    theirs = other_core(out)
    tok, model = out.shape[1:]
    first, *rest = kernel_call(
        lambda *refs: pair_body(ys, lo, hi, *refs),
        [((tok, model), f32)] + [((tok, model), bf16)] * 3,
        [at, rows, weights, theirs],
    )
    return [first] + [along_y(piece, s) for piece, s in zip(rest, SHIFTS[1:])]


def shards(
    tokens, cotangent, norm_gain, q_weight, q_bias, key_matrix, key_bias, value_matrix, value_bias,
    o_weight, o_bias, sinks, moe_gain, router_weight, router_bias, gate_up_weight, gate_up_bias,
    down_weight, down_bias, routes,
):
    zs, ys = lax.axis_size("z"), lax.axis_size("y")
    seqs = lax.axis_size("x") * zs
    seq_index = lax.axis_index("x") * zs + lax.axis_index("z")
    core = lax.axis_index("c")
    tok, model = tokens.shape
    rows = tok * ys * 2
    experts = 2 * seqs
    top = routes.shape[1]
    cap = 3 * tok * top // (2 * experts)
    slots = experts * cap
    ff_own = gate_up_weight.shape[-1]
    ff = 2 * ff_own * ys
    at = jnp.stack([lax.axis_index("y"), core, seq_index, 2 * seq_index + core]).astype(jnp.int32)
    gain_one, gain_two = norm_gain[None], moe_gain[None]

    h_low, packed = kernel_call(
        norm_body,
        [((tok, model), bf16), ((seqs, model // seqs, 384), bf16)],
        [tokens, gain_one, q_weight, key_matrix, value_matrix, o_weight.T],
        scalars=0,
    )
    count = 2 * ys
    last = count - 1
    halo = [lax.ppermute(h_low, ALL, [(s * count + last, (s + 1) * count + last) for s in range(seqs - 1)])]
    block_h = lax.all_gather(h_low, FSDP, axis=0, tiled=True)
    halo.append(lax.ppermute(halo[0], FSDP, [(7, 3)]))
    halo.append(lax.ppermute(halo[0] + halo[1], FSDP, [(7, 1), (3, 5)]))
    halo.append(lax.ppermute(halo[0] + halo[1] + halo[2], FSDP, [(7, 6), (5, 4), (3, 2), (1, 0)]))

    packed = exchange(after(packed, halo[0]), SEQ).reshape(model, 384)

    place, g_send = kernel_call(
        lambda *refs: plan_body(cap, experts, *refs),
        [((tok, slots), bf16), ((slots, model + 128), bf16)],
        [routes, cotangent],
        scalars=0,
        flops=2 * tok * slots * (model + 256),
    )
    g_send = after(g_send, packed, halo[2])
    g_all = exchange(g_send.reshape(experts, cap, model + 128), COLUMN).reshape(slots, model + 128)

    own, theirs = kernel_call(
        split_experts_body,
        [((3 * ff_own + 16, model), bf16)] * 2,
        [at, gate_up_weight.transpose(0, 2, 3, 1).reshape(2, 2 * ff_own, model), down_weight,
         gate_up_bias.reshape(2, 1, 2 * ff_own)],
    )
    (shard,) = kernel_call(
        join_experts_body, [((6 * ff_own + 16, model), bf16)], [own, other_core(theirs)], scalars=0
    )
    w_all = lax.all_gather(shard, "y", axis=0)
    b_down = lax.dynamic_index_in_dim(down_bias, core, 0, keepdims=True).astype(f32)

    wave = np.tile(np.arange(HEAD_WIDTH // 2), 4).astype(np.float32)
    inverse = rope_base ** (-(jnp.asarray(wave) * 2.0 / HEAD_WIDTH))
    inner = jnp.arange(WINDOW, dtype=f32)[:, None] * inverse[None, :]
    starts = seq_index * rows - WINDOW + WINDOW * jnp.arange(16, dtype=jnp.int32)
    outer = starts.astype(f32)[:, None] * inverse[None, :]
    within = jnp.concatenate([jnp.cos(inner), jnp.sin(inner)], axis=0)
    base = jnp.concatenate([jnp.cos(outer), jnp.sin(outer)], axis=0)
    bias_qkv = jnp.concatenate([q_bias, key_bias, value_bias]).astype(f32)[None]
    sink_low = sinks.astype(f32)
    q_low, k_low, v_low, attn_low, out_other = kernel_call(
        lambda *refs: project_body(ys, *refs),
        [((rows, 128), bf16), ((rows + WINDOW, 128), bf16), ((rows + WINDOW, 128), bf16),
         ((rows, 128), bf16), ((4, tok, model), bf16)],
        [after(at, shard, g_send), sink_low, block_h, *halo, packed, bias_qkv, within, base],
        scalars=2,
        scratch=[pltpu.VMEM((WINDOW, model), bf16)],
        flops=2 * rows * model * 384 + 8 * rows * 2 * WINDOW * 128,
    )
    sums = sum_pieces(ys, at, attn_low, packed, 256, 384, out_other)

    residual, h2_low, gate_probs, h2_send = kernel_call(
        lambda *refs: route_body(cap, *refs),
        [((tok, model), f32), ((tok, model), bf16), ((tok, experts), f32), ((slots, model), bf16)],
        [*sums, tokens, o_bias[None], gain_two, router_weight, router_bias[None], place, routes],
        scalars=0,
        flops=2 * tok * slots * model,
    )
    h2_send = after(h2_send, g_all)
    rows_in = exchange(h2_send.reshape(experts, cap, model), COLUMN).reshape(slots, model)

    u, side = by_chunks(
        lambda *refs: early_body(experts, *refs), 512, at, [g_all], [w_all, b_down], [(ff, f32), (128, f32)],
        2 * slots * model * ff,
    )
    hidden, grad_pre, early, back, p_rows = by_chunks(
        lambda *refs: expert_body(ys, *refs), 512, at, [rows_in, side, u],
        [w_all, router_weight, router_bias[None]],
        [(ff, bf16), (2 * ff, bf16), (256, bf16), (model - 128, bf16), (128, f32)], 8 * slots * model * ff,
    )
    early = exchange(early.reshape(experts, cap, 256), COLUMN).reshape(slots, 256)
    back = after(back, early).reshape(experts, cap, model - 128)
    back = exchange(back, COLUMN).reshape(slots, model - 128)
    y_send, expert_sum, gain_part = kernel_call(
        lambda *refs: weights_body(ys, *refs),
        [((slots, model), bf16), ((ys, 6 * ff_own + 16, model), bf16), ((1, model), f32)],
        [at, rows_in, g_all, hidden, grad_pre, p_rows, w_all, b_down],
        flops=8 * slots * model * ff,
        vmem=60,
    )
    expert_sum = lax.psum_scatter(after(expert_sum, early), "y", scatter_dimension=0, tiled=False)

    grad_low, sums_all = kernel_call(
        lambda *refs: logits_back_body(cap, *refs),
        [((tok, model), f32), ((2 * ys, experts + 16, 128), f32)],
        [early, place, gate_probs, h2_low, router_weight, gain_part, gain_two],
        scalars=0,
        flops=2 * tok * slots * experts * 3,
    )
    sums_all = lax.psum_scatter(sums_all, FSDP, scatter_dimension=0, tiled=False)
    dres, da = kernel_call(
        unroute_body,
        [((tok, model), f32), ((tok, model), bf16)],
        [early, back, place, grad_low, residual, cotangent, gain_two],
        scalars=0,
        flops=2 * tok * slots * model,
        vmem=60,
    )
    da_pieces = gather_pieces(da)
    y_back = exchange(y_send.reshape(experts, cap, model), COLUMN).reshape(slots, model)
    block_out = (residual + dot(place, y_back)).astype(bf16)

    block_grad, datt, head, dq_first, carry, sunk = kernel_call(
        lambda *refs: back_first_body(ys, *refs),
        [((rows, model), bf16), ((rows, 128), bf16), ((WINDOW, 128), bf16), ((WINDOW, 128), f32),
         ((WINDOW, 128), f32), ((2 * WINDOW, 128), f32)],
        [at, sink_low, *da_pieces, packed, q_low, k_low, v_low],
        scalars=2,
        flops=2 * rows * model * 128,
    )
    returned = lax.ppermute(head, SEQ, [(s + 1, s) for s in range(seqs - 1)])
    dqkv, tail, grad_sinks = kernel_call(
        back_rest_body,
        [((rows, 256), bf16), ((WINDOW, 128), f32), ((8, 128), f32)],
        [at, sink_low, datt, q_low, k_low, v_low, within, base, dq_first, carry, sunk],
        scalars=2,
        flops=20 * rows * 2 * WINDOW * 128,
    )
    dqkv, dh_other = kernel_call(
        lambda *refs: unproject_body(ys, tok, *refs),
        [((rows, 256), bf16), ((4, tok, model), bf16)],
        [at, dqkv, tail, returned, within, base, packed],
        flops=2 * rows * model * 128,
    )
    (grad_w,) = kernel_call(
        attention_weights_body,
        [((seqs, model // seqs + 16, 384), bf16)],
        [at, dqkv, block_h, block_grad, attn_low, packed, gain_one, grad_sinks, sums_all],
        flops=2 * rows * model * 384,
    )
    dh_sums = sum_pieces(ys, at, dqkv, packed, 0, 256, dh_other)

    share = model // seqs
    grad_w = after(exchange(after(grad_w, y_back), SEQ), dh_sums[1])
    grad_q, grad_k, grad_v, grad_o, small, last = kernel_call(
        sums_body,
        [((share, 128), f32), ((share, 64), f32), ((share, 64), f32), ((share, 128), f32), ((8, 128), f32),
         ((2 * ys, experts + 16, 128), f32)],
        [grad_w],
        scalars=0,
    )
    router_grad, vectors = kernel_call(
        last_body, [((experts, model), f32), ((32, 128), f32)], [exchange(last, FSDP)], scalars=0
    )

    expert_sum = after(expert_sum, dh_sums[0])
    parts = [expert_sum[n * ff_own : (n + 1) * ff_own] for n in (1, 3, 5)] + [expert_sum[6 * ff_own :]]
    grad_gu, grad_down, grad_gub, grad_db = kernel_call(
        experts_out_body,
        [((2, 2 * ff_own, model), f32), ((2, ff_own, model), f32), ((2, 2 * ff_own), f32), ((2, model), f32)],
        [at, expert_sum, other_core(jnp.concatenate(parts, axis=0))],
    )
    grad_gu = grad_gu.reshape(2, 2, ff_own, model).transpose(0, 3, 1, 2)
    grad_gub = grad_gub.reshape(2, 2, ff_own)
    dres = after(dres, block_out, last)
    (tokens_grad,) = kernel_call(
        finish_body, [((tok, model), bf16)], [*dh_sums, tokens, gain_one, dres], scalars=0
    )

    return (
        block_out, tokens_grad, vectors[16:24].reshape(model), grad_q, small[4], grad_k, small[5, :64], grad_v,
        small[5, 64:], grad_o.T, vectors[:8].reshape(model), small[6, :2], vectors[8:16].reshape(model),
        router_grad.T, vectors[26, :experts], grad_gu, grad_gub, grad_down, grad_db,
    )


def solution(mesh):
    sizes = dict(mesh.shape)
    side = int(round(sizes["seq"] ** 0.5))
    wide = Mesh(
        mesh.devices.reshape(side, sizes["seq"] // side, sizes["fsdp"] // 2, 2), ("x", "z", "y", "c")
    )
    in_specs = (
        P(ALL, None), P(ALL, None), P(), P(SEQ, FSDP), P(FSDP), P(SEQ, FSDP), P(FSDP), P(SEQ, FSDP), P(FSDP),
        P(FSDP, SEQ), P(), P(FSDP), P(), P(), P(), P(SEQ, None, None, FSDP), P(SEQ, None, FSDP),
        P(SEQ, FSDP, None), P(SEQ, None), P(ALL, None),
    )
    out_specs = (
        P(ALL, None), P(ALL, None), P(), P(SEQ, FSDP), P(FSDP), P(SEQ, FSDP), P(FSDP), P(SEQ, FSDP), P(FSDP),
        P(FSDP, SEQ), P(), P(FSDP), P(), P(), P(), P(SEQ, None, None, FSDP), P(SEQ, None, FSDP),
        P(SEQ, FSDP, None), P(SEQ, None),
    )
    return jax.shard_map(shards, mesh=wide, in_specs=in_specs, out_specs=out_specs, check_vma=False)
```

```python
import jax
import jax.numpy as jnp
import numpy as np
from jax import lax
from jax.experimental import pallas as pl
from jax.experimental.pallas import tpu as pltpu
from jax.sharding import Mesh, PartitionSpec as P

HEAD_WIDTH = 64
WINDOW = 128
norm_eps = 1e-05
rope_base = 150000.0
swiglu_limit = 7.0
glu_alpha = 1.702
masked_score = -1000000000.0

SEQ = ("x", "z")
FSDP = ("y", "c")
COLUMN = ("x", "z", "c")
ALL = ("x", "z", "y", "c")
f32 = jnp.float32
bf16 = jnp.bfloat16
SCALE = HEAD_WIDTH ** (-0.5)
SHIFTS = (0, 1, -1, 2)


def dot(a, b, dims=((1,), (0,))):
    return lax.dot_general(a, b, (dims, ((), ())), preferred_element_type=f32)


ROWS_BY = ((0,), (0,))
BY_ROWS = ((1,), (1,))


def inv_rms(values):
    return lax.rsqrt(jnp.mean(values * values, axis=-1, keepdims=True) + norm_eps)


def norm_back(grad, normed, root, gain):
    scaled = grad * gain
    return root * (scaled - normed * jnp.mean(scaled * normed, axis=-1, keepdims=True))


def halves(value):
    high = value.astype(bf16)
    return high, (value - high.astype(f32)).astype(bf16)


def lanes(shape):
    return lax.broadcasted_iota(jnp.int32, shape, len(shape) - 1)


def sublanes(shape):
    return lax.broadcasted_iota(jnp.int32, shape, len(shape) - 2)


def swap_halves(values):
    lane = lanes(values.shape) % HEAD_WIDTH
    return jnp.where(lane < 32, pltpu.roll(values, 96, 1), pltpu.roll(values, 32, 1))


def turn(values, cos, sin):
    return values * cos + swap_halves(values) * sin


def exchange(value, axes):
    return lax.all_to_all(value, axes, split_axis=0, concat_axis=0, tiled=True)


def broadcast_exchange(value, axes, count):
    return exchange(jnp.broadcast_to(value[None], (count,) + value.shape), axes)


def after(value, *earlier):
    return lax.optimization_barrier((value,) + earlier)[0]


def along(axis, value, steps):
    count = lax.axis_size(axis)
    return lax.ppermute(value, axis, [(k, (k + steps) % count) for k in range(count)])


def other_core(value):
    return lax.ppermute(value, "c", [(0, 1), (1, 0)])


def kernel_call(body, outs, ins, flops=0, scalars=1, scratch=(), vmem=40):
    specs = [pl.BlockSpec(memory_space=pltpu.SMEM)] * scalars
    specs += [pl.BlockSpec(memory_space=pltpu.VMEM)] * (len(ins) - scalars)
    out_shape = [jax.ShapeDtypeStruct(shape, kind) for shape, kind in outs]
    moved = sum(a.size * a.dtype.itemsize for a in ins)
    moved += sum(s.size * jnp.dtype(s.dtype).itemsize for s in out_shape)
    return pl.pallas_call(
        body,
        out_shape=out_shape,
        in_specs=specs,
        out_specs=[pl.BlockSpec(memory_space=pltpu.VMEM)] * len(outs),
        scratch_shapes=scratch,
        compiler_params=pltpu.CompilerParams(vmem_limit_bytes=vmem << 20),
        cost_estimate=pl.CostEstimate(flops=flops, bytes_accessed=moved, transcendentals=0),
    )(*ins)


def norm_body(x_ref, gain_ref, q_ref, k_ref, v_ref, o_ref, h_ref, packed_ref):
    x = x_ref[...].astype(f32)
    h_ref[...] = (x * inv_rms(x) * gain_ref[...].astype(f32)).astype(bf16)
    packed_ref[...] = jnp.concatenate([q_ref[...], k_ref[...], v_ref[...], o_ref[...]], axis=1)


def stack_body(*refs):
    count = refs[0].shape[0]
    for n, ref in enumerate(refs[:-1]):
        refs[-1][n * count : (n + 1) * count, :] = ref[...]


def waves(within_ref, base_ref, b):
    cos_in, sin_in = within_ref[:WINDOW, :], within_ref[WINDOW:, :]
    cos_at, sin_at = base_ref[b : b + 1, :], base_ref[16 + b : 17 + b, :]
    sine = sin_at * cos_in + cos_at * sin_in
    first = lanes(sine.shape) % HEAD_WIDTH < HEAD_WIDTH // 2
    return cos_at * cos_in - sin_at * sin_in, jnp.where(first, -sine, sine)


def plan_body(cap, experts, routes_ref, g_ref, place_ref, send_ref):
    tok, top = routes_ref.shape
    model = g_ref.shape[1]
    slots = place_ref.shape[1]
    routes = routes_ref[...]
    ids = lanes((tok, 128))
    hot = jnp.zeros((tok, 128), f32)
    for k in range(top):
        hot += (routes[:, k : k + 1] == ids).astype(f32)
    hot_low = hot.astype(bf16)
    before = (lanes((tok, tok)) < sublanes((tok, tok))).astype(f32).astype(bf16)
    rank = dot(before, hot_low)
    marked = jnp.where(hot > 0, rank, -1.0).astype(bf16)
    slot = lanes((128, slots))
    start = sublanes((128, slots)) * cap
    spread = ((slot >= start) & (slot < start + cap)).astype(f32).astype(bf16)
    wide = dot(marked, spread)
    lane = lanes((tok, slots)).astype(f32)
    within = lane - cap * jnp.floor((lane + 0.5) * (1.0 / cap))
    place = (wide == within).astype(f32).astype(bf16)
    place_ref[...] = place
    send_ref[:, :model] = dot(place, g_ref[...], ROWS_BY).astype(bf16)
    send_ref[:, model:] = dot(place, hot_low, ROWS_BY).astype(bf16)


def assemble(at_ref, pieces, block_ref, tok, ys):
    y, core = at_ref[0], at_ref[1]
    for n, piece in enumerate(pieces):
        from_y = lax.rem(y - SHIFTS[n % 4] + ys, ys)
        from_core = core if n < 4 else 1 - core
        start = pl.multiple_of((from_y * 2 + from_core) * tok, tok)
        block_ref[pl.ds(start, tok), :] = piece[...]


def project_body(ys, at_ref, sink_ref, *refs):
    block_ref, halos, w_pieces, refs = refs[0], refs[1 : 1 + 2 * ys], refs[1 + 2 * ys : 5 + 2 * ys], refs[5 + 2 * ys :]
    bias_ref, within_ref, base_ref = refs[:3]
    w_ref, q_ref, k_ref, v_ref, att_ref, out_ref, halo_ref = refs[3:]
    share = w_pieces[0].shape[0] // 4
    for n, piece in enumerate(w_pieces):
        for k in range(4):
            from_z = lax.rem(at_ref[5] - SHIFTS[n] + 4, 4)
            from_x = lax.rem(at_ref[4] - SHIFTS[k] + 4, 4)
            start = pl.multiple_of((from_x * 4 + from_z) * share, share)
            w_ref[pl.ds(start, share), :] = piece[k * share : (k + 1) * share, :]
    rows = block_ref.shape[0]
    tok = rows // (2 * ys)
    halo_ref[...] = sum((ref[...] for ref in halos[1:]), halos[0][...])
    weights = w_ref[:, :256]
    low = lanes((WINDOW, 128)) < 64

    def keys_values(kv, b, wave):
        at = slice(b * WINDOW, (b + 1) * WINDOW)
        turned = pltpu.roll(kv, 64, 1)
        k_ref[at, :] = turn(jnp.where(low, kv, turned), *wave).astype(bf16)
        v_ref[at, :] = jnp.where(low, turned, kv).astype(bf16)

    keys_values(dot(halo_ref[...], weights[:, 128:]) + bias_ref[:, 128:], 0, waves(within_ref, base_ref, 0))
    for r in range(0, rows, 2 * WINDOW):
        both = dot(block_ref[r : r + 2 * WINDOW, :], weights) + bias_ref[...]
        for k in range(2):
            qkv = both[k * WINDOW : (k + 1) * WINDOW]
            b = r // WINDOW + k
            wave = waves(within_ref, base_ref, b + 1)
            q_ref[b * WINDOW : (b + 1) * WINDOW, :] = turn(qkv[:, :128], *wave).astype(bf16)
            keys_values(qkv[:, 128:], b + 1, wave)
    sink = sink_column(sink_ref)
    for b in range(rows // WINDOW):
        part = slice(b * WINDOW, (b + 1) * WINDOW)
        near = slice(b * WINDOW, (b + 2) * WINDOW)
        q2 = stack_heads(q_ref[part, :])
        probs, _ = soft_rows(q2, k_ref[near, :], band(at_ref, b == 0), sink)
        both = dot(probs.astype(bf16), v_ref[near, :])
        att_ref[part, :] = jnp.where(low, both[:WINDOW], both[WINDOW:]).astype(bf16)
    to_other(at_ref, att_ref, w_ref[:, 256:384], out_ref, tok, ys)


def band(at_ref, first):
    shape = (2 * WINDOW, 2 * WINDOW)
    i, j = sublanes(shape), lanes(shape)
    off = jnp.where(i >= WINDOW, i - WINDOW, i) + WINDOW - j
    allowed = (off >= 0) & (off < WINDOW)
    if first:
        allowed = allowed & ((j >= WINDOW) | (at_ref[2] > 0))
    return allowed


def stack_heads(pair):
    low = lanes(pair.shape) < 64
    zero = jnp.zeros_like(pair)
    return jnp.concatenate([jnp.where(low, pair, zero), jnp.where(low, zero, pair)], axis=0)


def soft_rows(q2, keys, allowed, sink):
    scores = jnp.where(allowed, dot(q2, keys, BY_ROWS) * SCALE, masked_score)
    top = jnp.maximum(jnp.max(scores, axis=-1, keepdims=True), sink)
    weights = jnp.exp(scores - top)
    sunk = jnp.exp(sink - top)
    inverse = 1.0 / (jnp.sum(weights, axis=-1, keepdims=True) + sunk)
    return weights * inverse, sunk * inverse


def sink_column(sink_ref):
    row = sublanes((2 * WINDOW, 1))
    return jnp.where(row < WINDOW, sink_ref[0], sink_ref[1])


def to_other(at_ref, rows_ref, weights, out_ref, tok, ys):
    for n, shift in enumerate(SHIFTS):
        to_y = lax.rem(at_ref[0] + shift + ys, ys)
        theirs = pl.multiple_of((to_y * 2 + 1 - at_ref[1]) * tok, tok)
        out_ref[n] = dot(rows_ref[pl.ds(theirs, tok), :], weights, BY_ROWS).astype(bf16)


def pair_body(ys, lo, hi, at_ref, rows_ref, w_ref, other_ref, *outs):
    tok = other_ref.shape[1]
    for n, shift in enumerate(SHIFTS):
        to_y = lax.rem(at_ref[0] + shift + ys, ys)
        mine = pl.multiple_of((to_y * 2 + at_ref[1]) * tok, tok)
        own = dot(rows_ref[pl.ds(mine, tok), :], w_ref[:, lo:hi], BY_ROWS)
        outs[n][...] = (own + other_ref[n].astype(f32)).astype(outs[n].dtype)


def gates(values, mask):
    masked = jnp.where(mask, values, masked_score)
    ex = jnp.where(mask, jnp.exp(masked - jnp.max(masked, axis=-1, keepdims=True)), 0.0)
    total = jnp.sum(ex, axis=-1, keepdims=True)
    return ex / jnp.where(total > 0, total, 1.0)


def route_body(
    cap, first_ref, a_ref, b_ref, c_ref, x_ref, ob_ref, gain_ref, rw_ref, rb_ref, place_ref, routes_ref,
    res_ref, h2_ref, gate_ref, send_ref,
):
    tok, experts = gate_ref.shape
    total = first_ref[...] + a_ref[...].astype(f32) + b_ref[...].astype(f32) + c_ref[...].astype(f32)
    residual = x_ref[...].astype(f32) + total + ob_ref[...].astype(f32)
    res_ref[...] = residual
    h2 = (residual * inv_rms(residual) * gain_ref[...].astype(f32)).astype(bf16)
    h2_ref[...] = h2
    send_ref[...] = dot(place_ref[...], h2, ROWS_BY).astype(bf16)
    logits = dot(h2, rw_ref[...]) + rb_ref[...].astype(f32)
    routes = routes_ref[...]
    ids = lanes((tok, experts))
    hot = jnp.zeros((tok, experts), f32)
    for k in range(routes.shape[1]):
        hot += (routes[:, k : k + 1] == ids).astype(f32)
    gate_ref[...] = gates(logits, hot > 0)


def expert_body(
    ys, at_ref, rows_ref, side_ref, u_ref, w_ref, rw_ref, rb_ref, hidden_ref, dpre_ref, back_ref, p_ref
):
    model = rows_ref.shape[1]
    experts = rw_ref.shape[1]
    rows = rows_ref[...]
    count = rows.shape[0]
    logits = dot(rows, rw_ref[...]) + rb_ref[...].astype(f32)
    mask = side_ref[:, :experts] > 0
    mine = lanes((count, experts)) == at_ref[3]
    p = jnp.sum(jnp.where(mine, gates(logits, mask), 0.0), axis=-1, keepdims=True)
    p_ref[...] = jnp.broadcast_to(p, p_ref.shape)
    dgate = side_ref[:, experts : experts + 1]
    grad = jnp.zeros((count, model), f32)
    half = (w_ref.shape[1] - 16) // 3
    own = half // 2
    for n in range(ys):
        weights = w_ref[n, : 2 * half, :]
        first, second = w_ref[n, 3 * half : 3 * half + 1, :half], w_ref[n, 3 * half + 8 : 3 * half + 9, :half]
        bias = jnp.concatenate([first[:, :own], second[:, :own], first[:, own:], second[:, own:]], axis=1)
        pre = dot(rows, weights, BY_ROWS) + bias.astype(f32)
        gt = jnp.tanh(pre[:, :half] * (1.0 / swiglu_limit))
        ut = jnp.tanh(pre[:, half:] * (1.0 / swiglu_limit))
        gate, up = swiglu_limit * gt, swiglu_limit * ut + 1.0
        sig = jax.nn.sigmoid(glu_alpha * gate)
        gs = gate * sig
        hidden = (up * gs).astype(bf16)
        u = u_ref[:, n * half : (n + 1) * half]
        dgate += jnp.sum(hidden.astype(f32) * u, axis=-1, keepdims=True)
        hidden_ref[:, n * half : (n + 1) * half] = hidden
        dh = p * u
        d_gate = dh * up * (sig + glu_alpha * gs * (1.0 - sig)) * (1.0 - gt * gt)
        d_up = dh * gs * (1.0 - ut * ut)
        dpre = jnp.concatenate([d_gate, d_up], axis=1).astype(bf16)
        dpre_ref[:, 2 * n * half : 2 * (n + 1) * half] = dpre
        grad += dot(dpre, weights)
    back_ref[:, :model] = grad.astype(bf16)
    high, rest = halves(dgate)
    middle, low = halves(dgate - high.astype(f32))
    lane = lanes((count, 128))
    parts = jnp.where(lane == 0, high.astype(f32), jnp.where(lane == 1, middle.astype(f32), low.astype(f32)))
    back_ref[:, model:] = jnp.where(lane < 3, parts, 0.0).astype(bf16)


def by_chunks(body, step, at, cut_in, whole_in, outs, flops):
    slots = cut_in[0].shape[0]

    def cut(width):
        return pl.BlockSpec((step, width), lambda n: (n, 0))

    def whole(a):
        return pl.BlockSpec(a.shape, lambda n: (0,) * a.ndim)

    return pl.pallas_call(
        body,
        grid=(slots // step,),
        out_shape=[jax.ShapeDtypeStruct((slots, w_), kind) for w_, kind in outs],
        in_specs=[pl.BlockSpec(memory_space=pltpu.SMEM)]
        + [cut(a.shape[1]) for a in cut_in]
        + [whole(a) for a in whole_in],
        out_specs=[cut(w_) for w_, _ in outs],
        compiler_params=pltpu.CompilerParams(vmem_limit_bytes=60 << 20),
        cost_estimate=pl.CostEstimate(flops=flops, bytes_accessed=16 << 20, transcendentals=0),
    )(at, *cut_in, *whole_in)


def split_experts_body(at_ref, gu_ref, down_ref, bias_ref, own_ref, theirs_ref):
    wide, half = gu_ref.shape[1], down_ref.shape[1]
    for ref, expert in ((own_ref, at_ref[1]), (theirs_ref, 1 - at_ref[1])):
        ref[:wide, :] = gu_ref[expert]
        ref[wide : wide + half, :] = down_ref[expert]
        ref[wide + half :, :] = jnp.zeros((16, ref.shape[1]), bf16)
        ref[wide + half : wide + half + 1, :wide] = bias_ref[expert]


def join_experts_body(own_ref, theirs_ref, out_ref):
    half = (own_ref.shape[0] - 16) // 3
    for n in range(3):
        part = slice(n * half, (n + 1) * half)
        out_ref[2 * n * half : (2 * n + 1) * half, :] = own_ref[part, :]
        out_ref[(2 * n + 1) * half : (2 * n + 2) * half, :] = theirs_ref[part, :]
    out_ref[6 * half :, :] = jnp.concatenate(
        [own_ref[3 * half : 3 * half + 8, :], theirs_ref[3 * half : 3 * half + 8, :]], axis=0
    )


def early_body(experts, at_ref, g_ref, w_ref, bd_ref, u_ref, side_ref):
    model = w_ref.shape[2]
    half = (w_ref.shape[1] - 16) // 3
    g = g_ref[:, :model]
    for n in range(w_ref.shape[0]):
        u_ref[:, n * half : (n + 1) * half] = dot(g, w_ref[n, 2 * half : 3 * half, :], BY_ROWS)
    bias = jnp.sum(g.astype(f32) * bd_ref[...], axis=-1, keepdims=True)
    hot = g_ref[:, model:].astype(f32)
    side_ref[...] = jnp.where(lanes(hot.shape) < experts, hot, bias)


def weights_body(ys, at_ref, rows_ref, g_ref, hidden_ref, dpre_ref, p_ref, w_ref, bd_ref, y_ref, sum_ref):
    slots, model = rows_ref.shape
    ff = hidden_ref.shape[1]
    half = ff // ys
    step = 256
    w_down = jnp.concatenate([w_ref[n, 2 * half : 3 * half, :] for n in range(ys)], axis=0)
    dys = []
    bias = jnp.zeros((1, model), f32)
    for r in range(0, slots, step):
        part = slice(r, r + step)
        p = p_ref[part, :1]
        y = dot(hidden_ref[part, :], w_down) + bd_ref[...]
        y_ref[part, :] = (p * y).astype(bf16)
        dy = (p * g_ref[part, :model].astype(f32)).astype(bf16)
        bias += jnp.sum(dy.astype(f32), axis=0, keepdims=True)
        dys.append(dy)
    dy = jnp.concatenate(dys, axis=0)
    high, low = halves(bias)
    row = sublanes((16, model))
    for n in range(ys):
        dpre = dpre_ref[:, 2 * n * half : 2 * (n + 1) * half]
        dw = dot(dpre, rows_ref[...], ROWS_BY)
        hidden = hidden_ref[:, n * half : (n + 1) * half]
        ddown = dot(hidden, dy, ROWS_BY)
        own = half // 2
        parts = [dw[:own], dw[half : half + own], ddown[:own], dw[own:half], dw[half + own :], ddown[own:]]
        for k, part in enumerate(parts):
            sum_ref[n, k * own : (k + 1) * own, :] = part.astype(bf16)
        b = jnp.sum(dpre.astype(f32), axis=0, keepdims=True)
        b = jnp.concatenate([b, jnp.zeros((1, model - 2 * half), f32)], axis=1)
        tail = jnp.where(row == 1, high.astype(f32), jnp.where(row == 2, low.astype(f32), 0.0))
        sum_ref[n, 3 * half :, :] = jnp.where(row == 0, b, tail).astype(bf16)


def experts_out_body(at_ref, own_ref, theirs_ref, gu_ref, down_ref, gub_ref, db_ref):
    core = at_ref[1]
    half = down_ref.shape[1]
    gu_ref[core] = own_ref[: 2 * half, :].astype(f32)
    gu_ref[1 - core] = theirs_ref[3 * half : 5 * half, :].astype(f32)
    down_ref[core] = own_ref[2 * half : 3 * half, :].astype(f32)
    down_ref[1 - core] = theirs_ref[5 * half : 6 * half, :].astype(f32)
    own, theirs = own_ref[6 * half :, :].astype(f32), theirs_ref[6 * half :, :].astype(f32)

    def by_expert(mine, other):
        return jnp.where(sublanes((2, mine.shape[1])) == core, mine, other)

    mine = jnp.concatenate([own[:1, :half], own[:1, 2 * half : 3 * half]], axis=1)
    other = jnp.concatenate([theirs[:1, half : 2 * half], theirs[:1, 3 * half : 4 * half]], axis=1)
    gub_ref[...] = by_expert(mine, other)
    db_ref[...] = by_expert(own[1:2] + own[2:3], theirs[1:2] + theirs[2:3])


def sums_body(in_ref, q_ref, k_ref, v_ref, o_ref, qb_ref, kb_ref, vb_ref, sink_ref, last_ref):
    total = in_ref[0].astype(f32)
    for n in range(1, in_ref.shape[0]):
        total += in_ref[n].astype(f32)
    share = q_ref.shape[0]
    q_ref[...] = total[:share, :128]
    k_ref[...] = total[:share, 128:192]
    v_ref[...] = total[:share, 192:256]
    o_ref[...] = total[:share, 256:]
    sums = jnp.concatenate([total[share:, :128], total[share:, 128:256], total[share:, 256:]], axis=0)
    qb_ref[...] = sums[36:37]
    kb_ref[...] = sums[37:38, :64]
    vb_ref[...] = sums[37:38, 64:]
    sink_ref[...] = sums[38:39, :2]
    for n in range(last_ref.shape[0]):
        last_ref[n] = sums


def last_body(in_ref, router_ref, router_b_ref, o_bias_ref, gain_two_ref, gain_one_ref):
    experts = router_ref.shape[0]
    for n in range(in_ref.shape[0]):
        router_ref[:, n * 128 : (n + 1) * 128] = in_ref[n, :experts, :]
    row = sublanes((8, 128))
    o_bias = gain_two = gain_one = jnp.zeros((8, 128), f32)
    for n in range(in_ref.shape[0]):
        o_bias = jnp.where(row == n, in_ref[n, experts : experts + 1, :], o_bias)
        gain_two = jnp.where(row == n, in_ref[n, experts + 1 : experts + 2, :], gain_two)
        gain_one = gain_one + in_ref[n, experts + 8 :, :]
    o_bias_ref[...] = o_bias
    gain_two_ref[...] = gain_two
    gain_one_ref[...] = gain_one
    router_b_ref[...] = in_ref[0, experts + 2 : experts + 3, :experts]


def unroute_body(
    cap, back_ref, place_ref, gate_ref, h2_ref, res_ref, g_ref, rw_ref, gain_ref, dres_ref, da_ref
):
    tok, experts = gate_ref.shape
    slots, model = place_ref.shape[1], h2_ref.shape[1]
    place = place_ref[...]
    slot = sublanes((slots, experts))
    start = lanes((slots, experts)) * cap
    own = (slot >= start) & (slot < start + cap)
    dgate = jnp.zeros((tok, experts), f32)
    for k in range(3):
        column = back_ref[:, model + k : model + k + 1].astype(f32)
        dgate += dot(place, jnp.where(own, column, 0.0).astype(bf16))
    gate = gate_ref[...]
    dlogits = gate * (dgate - jnp.sum(gate * dgate, axis=-1, keepdims=True))
    high, low = halves(dlogits)
    router = rw_ref[...]
    grad = dot(place, back_ref[:, :model]) + dot(high, router, BY_ROWS) + dot(low, router, BY_ROWS)
    h2 = h2_ref[...]
    router_grad = dot(high, h2, ROWS_BY) + dot(low, h2, ROWS_BY)
    residual = res_ref[...]
    root = inv_rms(residual)
    normed = residual * root
    dres = g_ref[...].astype(f32) + norm_back(grad, normed, root, gain_ref[...].astype(f32))
    dres_ref[...] = dres
    o_bias = jnp.sum(dres, axis=0, keepdims=True)
    gain_sum = jnp.sum(grad * normed, axis=0, keepdims=True)
    router_b = jnp.sum(dlogits, axis=0, keepdims=True)
    router_b = jnp.concatenate([router_b, jnp.zeros((1, 128 - experts), f32)], axis=1)
    router_b = jnp.concatenate([router_b] * (model // 128), axis=1)
    row = sublanes((16, model))
    rest = jnp.where(row == 0, o_bias, jnp.where(row == 1, gain_sum, jnp.where(row == 2, router_b, 0.0)))
    da_ref[:tok, :] = dres.astype(bf16)
    da_ref[tok : tok + experts, :] = router_grad.astype(bf16)
    da_ref[tok + experts :, :] = rest.astype(bf16)


def block_back(at_ref, sink, b, q_ref, datt_ref, k_ref, v_ref):
    part = slice(b * WINDOW, (b + 1) * WINDOW)
    near = slice(b * WINDOW, (b + 2) * WINDOW)
    low = lanes((WINDOW, 128)) < 64
    q2 = stack_heads(q_ref[part, :])
    g2 = stack_heads(datt_ref[part, :])
    keys = k_ref[near, :]
    probs, sunk = soft_rows(q2, keys, band(at_ref, b == 0), sink)
    dprobs = dot(g2, v_ref[near, :], BY_ROWS)
    delta = jnp.sum(probs * dprobs, axis=-1, keepdims=True)
    dscores = (probs * (dprobs - delta)).astype(bf16)
    dq2 = dot(dscores, keys)
    dq = jnp.where(low, dq2[:WINDOW], dq2[WINDOW:]) * SCALE
    dk2 = dot(dscores, q2, ROWS_BY) * SCALE
    dv2 = dot(probs.astype(bf16), g2, ROWS_BY)
    wide = lanes(dk2.shape) < 64
    dkv = jnp.where(wide, dk2 + pltpu.roll(dk2, 64, 1), dv2 + pltpu.roll(dv2, 64, 1))
    return dq, dkv, sunk * delta


def turn_back(values, cos, sin):
    return values * cos - swap_halves(values) * sin


def back_first_body(ys, at_ref, sink_ref, *refs):
    pieces, refs = refs[:8], refs[8:]
    w_ref, q_ref, k_ref, v_ref = refs[:4]
    block_ref, datt_ref, head_ref, dq_ref, carry_ref, sink_out_ref, sums_ref = refs[4:]
    tok = block_ref.shape[0] // (2 * ys)
    assemble(at_ref, [piece.at[:tok, :] for piece in pieces], block_ref, tok, ys)
    own = pl.ds(pl.multiple_of((at_ref[0] * 2 + at_ref[1]) * 128, 128), 128)
    total = pieces[0][tok:, own].astype(f32)
    for piece in pieces[1:]:
        total += piece[tok:, own].astype(f32)
    sums_ref[...] = total
    weights = w_ref[:, 256:384]
    for r in range(0, block_ref.shape[0], 256):
        datt_ref[r : r + 256, :] = dot(block_ref[r : r + 256, :], weights).astype(bf16)
    dq, dkv, sunk = block_back(at_ref, sink_column(sink_ref), 0, q_ref, datt_ref, k_ref, v_ref)
    head_ref[...] = dkv[:WINDOW].astype(bf16)
    carry_ref[...] = dkv[WINDOW:]
    dq_ref[...] = dq
    sink_out_ref[...] = jnp.broadcast_to(sunk, sink_out_ref.shape)


def back_rest_body(
    at_ref, sink_ref, datt_ref, q_ref, k_ref, v_ref, within_ref, base_ref, dq_ref, carry_ref, sunk_ref,
    block_ref, att_ref, dqkv_ref, last_ref, sink_out_ref, dwo_ref,
):
    rows = q_ref.shape[0]
    sink = sink_column(sink_ref)
    low = lanes((WINDOW, 128)) < 64
    for d in range(0, dwo_ref.shape[0], 256):
        dwo_ref[d : d + 256, :] = dot(block_ref[:, d : d + 256], att_ref[...], ROWS_BY).astype(bf16)
    sink_sum = sunk_ref[:, :1]
    carry = carry_ref[...]
    for b in range(rows // WINDOW):
        part = slice(b * WINDOW, (b + 1) * WINDOW)
        wave = waves(within_ref, base_ref, b + 1)
        if b == 0:
            dq = dq_ref[...]
        else:
            dq, dkv, sunk = block_back(at_ref, sink, b, q_ref, datt_ref, k_ref, v_ref)
            sink_sum += sunk
            done = carry + dkv[:WINDOW]
            carry = dkv[WINDOW:]
            before = slice((b - 1) * WINDOW, b * WINDOW)
            dqkv_ref[before, 128:] = jnp.where(low, turn_back(done, *last_wave), done).astype(bf16)
        dqkv_ref[part, :128] = turn_back(dq, *wave).astype(bf16)
        last_wave = wave
    last_ref[...] = carry
    dqkv_ref[rows - WINDOW :, 128:] = jnp.zeros((WINDOW, 128), bf16)
    total0 = jnp.sum(sink_sum[:WINDOW], axis=0, keepdims=True)
    total1 = jnp.sum(sink_sum[WINDOW:], axis=0, keepdims=True)
    lane = lanes((8, 128))
    sink_out_ref[...] = -jnp.where(lane == 0, total0, jnp.where(lane == 1, total1, 0.0))


def unproject_body(ys, tok, at_ref, part_ref, last_ref, ret_ref, within_ref, base_ref, w_ref, dqkv_ref, out_ref):
    rows = part_ref.shape[0]
    low = lanes((WINDOW, 128)) < 64
    dqkv_ref[...] = part_ref[...]
    dkv = last_ref[...] + ret_ref[...].astype(f32)
    turned = turn_back(dkv, *waves(within_ref, base_ref, rows // WINDOW))
    dqkv_ref[rows - WINDOW :, 128:] = jnp.where(low, turned, dkv).astype(bf16)
    to_other(at_ref, dqkv_ref, w_ref[:, :256], out_ref, tok, ys)


def attention_weights_body(
    dqkv_ref, block_ref, dwo_ref, w_ref, gain_ref, sink_ref, sums_ref, send_ref
):
    model = block_ref.shape[1]
    bias = jnp.sum(dqkv_ref[...].astype(f32), axis=0, keepdims=True)
    bias = jnp.concatenate([bias, sink_ref[:1, :]], axis=1)
    step = 256
    seqs = send_ref.shape[0]
    share = model // seqs
    per = step // share
    ones = jnp.ones((8, 256), bf16)
    gains = []
    for d in range(0, model, step):
        dw = dot(block_ref[:, d : d + step], dqkv_ref[...], ROWS_BY)
        for k in range(per):
            part = slice(k * share, (k + 1) * share)
            send_ref[d // share + k, :share, :256] = dw[part].astype(bf16)
            send_ref[d // share + k, :share, 256:] = dwo_ref[d + k * share : d + (k + 1) * share, :]
        first, second = halves(dw * w_ref[d : d + step, :256].astype(f32))
        gains.append((dot(ones, first, BY_ROWS) + dot(ones, second, BY_ROWS))[:1])
    gain = jnp.concatenate(gains, axis=1) / gain_ref[...].astype(f32)
    row = sublanes((8, 128))
    middle = sums_ref[32:40, :]
    for n, line in enumerate([bias[:, :128], bias[:, 128:256], bias[:, 256:]]):
        middle = jnp.where(row == n + 4, line, middle)
    gain = jnp.concatenate([gain[:, n * 128 : (n + 1) * 128] for n in range(8)], axis=0)
    third = jnp.concatenate([middle, gain], axis=0)
    tail = jnp.concatenate([sums_ref[:16, :], sums_ref[16:32, :], third], axis=1).astype(bf16)
    for s in range(seqs):
        send_ref[s, share:, :] = tail


def finish_body(first_ref, a_ref, b_ref, c_ref, x_ref, gain_ref, dres_ref, out_ref):
    grad = first_ref[...] + a_ref[...].astype(f32) + b_ref[...].astype(f32) + c_ref[...].astype(f32)
    x = x_ref[...].astype(f32)
    root = inv_rms(x)
    out = dres_ref[...] + norm_back(grad, x * root, root, gain_ref[...].astype(f32))
    out_ref[...] = out.astype(bf16)


def gather_pieces(own):
    mine = [own] + list(lax.optimization_barrier(tuple(along("y", own, s) for s in SHIFTS[1:])))
    return mine + [other_core(piece) for piece in mine]


def sum_pieces(ys, at, rows, weights, lo, hi, out):
    theirs = other_core(out)
    tok, model = out.shape[1:]
    first, *rest = kernel_call(
        lambda *refs: pair_body(ys, lo, hi, *refs),
        [((tok, model), f32)] + [((tok, model), bf16)] * 3,
        [at, rows, weights, theirs],
    )
    sent = tuple(along("y", piece, s) for piece, s in zip(rest, SHIFTS[1:]))
    return [first] + list(lax.optimization_barrier(sent))


def shards(
    tokens, cotangent, norm_gain, q_weight, q_bias, key_matrix, key_bias, value_matrix, value_bias,
    o_weight, o_bias, sinks, moe_gain, router_weight, router_bias, gate_up_weight, gate_up_bias,
    down_weight, down_bias, routes,
):
    zs, ys = lax.axis_size("z"), lax.axis_size("y")
    seqs = lax.axis_size("x") * zs
    seq_index = lax.axis_index("x") * zs + lax.axis_index("z")
    core = lax.axis_index("c")
    tok, model = tokens.shape
    rows = tok * ys * 2
    experts = 2 * seqs
    top = routes.shape[1]
    cap = 3 * tok * top // (2 * experts)
    slots = experts * cap
    ff_own = gate_up_weight.shape[-1]
    ff = 2 * ff_own * ys
    at = jnp.stack(
        [lax.axis_index("y"), core, seq_index, 2 * seq_index + core, lax.axis_index("x"), lax.axis_index("z")]
    ).astype(jnp.int32)
    gain_one, gain_two = norm_gain[None], moe_gain[None]

    h_low, packed = kernel_call(
        norm_body,
        [((tok, model), bf16), ((model // seqs, 384), bf16)],
        [tokens, gain_one, q_weight, key_matrix, value_matrix, o_weight.T],
        scalars=0,
        vmem=60,
    )
    count = 2 * ys
    last = count - 1
    halo = [lax.ppermute(h_low, ALL, [(s * count + last, (s + 1) * count + last) for s in range(seqs - 1)])]
    block_h = lax.all_gather(h_low, FSDP, axis=0, tiled=True)
    halo += [lax.ppermute(halo[0], FSDP, [(last, place)]) for place in range(last)]

    packed = [packed] + [along("x", packed, s) for s in SHIFTS[1:]]
    (packed,) = kernel_call(stack_body, [((4 * model // seqs, 384), bf16)], packed, scalars=0)
    w_pieces = [packed] + list(lax.optimization_barrier(tuple(along("z", packed, s) for s in SHIFTS[1:])))

    place, g_send = kernel_call(
        lambda *refs: plan_body(cap, experts, *refs),
        [((tok, slots), bf16), ((slots, model + 128), bf16)],
        [after(routes, packed), cotangent],
        scalars=0,
        flops=2 * tok * slots * (model + 256),
    )
    g_send = after(g_send, *w_pieces, halo[0])
    g_all = exchange(g_send.reshape(experts, cap, model + 128), COLUMN).reshape(slots, model + 128)

    own, theirs = kernel_call(
        split_experts_body,
        [((3 * ff_own + 16, model), bf16)] * 2,
        [at, gate_up_weight.transpose(0, 2, 3, 1).reshape(2, 2 * ff_own, model), down_weight,
         gate_up_bias.reshape(2, 1, 2 * ff_own)],
    )
    (shard,) = kernel_call(
        join_experts_body, [((6 * ff_own + 16, model), bf16)], [own, other_core(theirs)], scalars=0
    )
    b_down = lax.dynamic_index_in_dim(down_bias, core, 0, keepdims=True).astype(f32)

    wave = np.tile(np.arange(HEAD_WIDTH // 2), 4).astype(np.float32)
    inverse = rope_base ** (-(jnp.asarray(wave) * 2.0 / HEAD_WIDTH))
    inner = after(jnp.arange(WINDOW, dtype=f32), w_pieces[0])[:, None] * inverse[None, :]
    starts = after(seq_index, w_pieces[0]) * rows - WINDOW + WINDOW * jnp.arange(16, dtype=jnp.int32)
    outer = starts.astype(f32)[:, None] * inverse[None, :]
    within = jnp.concatenate([jnp.cos(inner), jnp.sin(inner)], axis=0)
    base = jnp.concatenate([jnp.cos(outer), jnp.sin(outer)], axis=0)
    bias_qkv = jnp.concatenate([after(q_bias, w_pieces[0]), key_bias, value_bias]).astype(f32)[None]
    sink_low = sinks.astype(f32)
    packed, q_low, k_low, v_low, attn_low, out_other = kernel_call(
        lambda *refs: project_body(ys, *refs),
        [((model, 384), bf16), ((rows, 128), bf16), ((rows + WINDOW, 128), bf16), ((rows + WINDOW, 128), bf16),
         ((rows, 128), bf16), ((4, tok, model), bf16)],
        [at, sink_low, block_h, *halo, *w_pieces, bias_qkv, within, base],
        vmem=60,
        scalars=2,
        scratch=[pltpu.VMEM((WINDOW, model), bf16)],
        flops=2 * rows * model * 384 + 8 * rows * 2 * WINDOW * 128,
    )
    sums = sum_pieces(ys, at, attn_low, packed, 256, 384, out_other)

    w_all = lax.all_gather(after(shard, *sums[1:]), "y", axis=0)

    residual, h2_low, gate_probs, h2_send = kernel_call(
        lambda *refs: route_body(cap, *refs),
        [((tok, model), f32), ((tok, model), bf16), ((tok, experts), f32), ((slots, model), bf16)],
        [*sums, tokens, o_bias[None], gain_two, router_weight, router_bias[None], place, routes],
        vmem=60,
        scalars=0,
        flops=2 * tok * slots * model,
    )
    h2_send = after(h2_send, g_all)
    rows_in = exchange(h2_send.reshape(experts, cap, model), COLUMN).reshape(slots, model)

    u, side = by_chunks(
        lambda *refs: early_body(experts, *refs), 512, at, [g_all], [w_all, b_down], [(ff, f32), (128, f32)],
        2 * slots * model * ff,
    )
    hidden, grad_pre, back, p_rows = by_chunks(
        lambda *refs: expert_body(ys, *refs), 512, at, [rows_in, side, u],
        [w_all, router_weight, router_bias[None]],
        [(ff, bf16), (2 * ff, bf16), (model + 128, bf16), (128, f32)], 8 * slots * model * ff,
    )
    back = exchange(back.reshape(experts, cap, model + 128), COLUMN).reshape(slots, model + 128)
    y_send, expert_sum = kernel_call(
        lambda *refs: weights_body(ys, *refs),
        [((slots, model), bf16), ((ys, 6 * ff_own + 16, model), bf16)],
        [at, rows_in, g_all, hidden, grad_pre, p_rows, w_all, b_down],
        flops=8 * slots * model * ff,
        vmem=60,
    )

    dres, da = kernel_call(
        lambda *refs: unroute_body(cap, *refs),
        [((tok, model), f32), ((tok + experts + 16, model), bf16)],
        [back, after(place, expert_sum), gate_probs, h2_low, residual, cotangent, router_weight, gain_two],
        vmem=60,
        scalars=0,
        flops=2 * tok * slots * model,
    )
    da_pieces = gather_pieces(da)
    y_back = exchange(y_send.reshape(experts, cap, model), COLUMN).reshape(slots, model)
    block_out = (residual + dot(place, y_back)).astype(bf16)

    expert_sum = lax.psum_scatter(expert_sum, "y", scatter_dimension=0, tiled=False)

    block_grad, datt, head, dq_first, carry, sunk, sums_all = kernel_call(
        lambda *refs: back_first_body(ys, *refs),
        [((rows, model), bf16), ((rows, 128), bf16), ((WINDOW, 128), bf16), ((WINDOW, 128), f32),
         ((WINDOW, 128), f32), ((2 * WINDOW, 128), f32), ((experts + 16, 128), f32)],
        [at, sink_low, *da_pieces, packed, q_low, k_low, v_low],
        scalars=2,
        flops=2 * rows * model * 128,
    )
    returned = lax.ppermute(head, SEQ, [(s + 1, s) for s in range(seqs - 1)])
    dqkv, tail, grad_sinks, grad_wo = kernel_call(
        back_rest_body,
        [((rows, 256), bf16), ((WINDOW, 128), f32), ((8, 128), f32), ((model, 128), bf16)],
        [at, sink_low, datt, q_low, k_low, v_low, within, base, dq_first, carry, sunk, block_grad, attn_low],
        scalars=2,
        flops=20 * rows * 2 * WINDOW * 128,
    )
    dqkv, dh_other = kernel_call(
        lambda *refs: unproject_body(ys, tok, *refs),
        [((rows, 256), bf16), ((4, tok, model), bf16)],
        [at, dqkv, tail, returned, within, base, packed],
        flops=2 * rows * model * 128,
    )
    (grad_w,) = kernel_call(
        attention_weights_body,
        [((seqs, model // seqs + 16, 384), bf16)],
        [dqkv, block_h, grad_wo, packed, gain_one, grad_sinks, sums_all],
        scalars=0,
        flops=2 * rows * model * 384,
    )
    dh_sums = sum_pieces(ys, at, dqkv, packed, 0, 256, dh_other)

    share = model // seqs
    grad_w = after(exchange(after(grad_w, y_back), SEQ), dh_sums[1])
    grad_q, grad_k, grad_v, grad_o, grad_qb, grad_kb, grad_vb, grad_sinks, last = kernel_call(
        sums_body,
        [((share, 128), f32), ((share, 64), f32), ((share, 64), f32), ((share, 128), f32), ((1, 128), f32),
         ((1, 64), f32), ((1, 64), f32), ((1, 2), f32), ((2 * ys, experts + 16, 128), f32)],
        [grad_w],
        scalars=0,
    )
    router_grad, router_b_grad, o_bias_grad, gain_two_grad, gain_one_grad = kernel_call(
        last_body, [((experts, model), f32), ((1, experts), f32)] + [((8, 128), f32)] * 3, [exchange(last, FSDP)], scalars=0
    )

    expert_sum = after(expert_sum, dh_sums[0])
    grad_gu, grad_down, grad_gub, grad_db = kernel_call(
        experts_out_body,
        [((2, 2 * ff_own, model), f32), ((2, ff_own, model), f32), ((2, 2 * ff_own), f32), ((2, model), f32)],
        [at, expert_sum, other_core(expert_sum)],
        vmem=60,
    )
    grad_gu = grad_gu.reshape(2, 2, ff_own, model).transpose(0, 3, 1, 2)
    grad_gub = grad_gub.reshape(2, 2, ff_own)
    dres = after(dres, block_out, last)
    (tokens_grad,) = kernel_call(
        finish_body, [((tok, model), bf16)], [*dh_sums, tokens, gain_one, dres], scalars=0, vmem=60
    )

    return (
        block_out, tokens_grad, gain_one_grad.reshape(model), grad_q, grad_qb.reshape(-1), grad_k,
        grad_kb.reshape(-1), grad_v, grad_vb.reshape(-1), grad_o.T, o_bias_grad.reshape(model),
        grad_sinks.reshape(-1), gain_two_grad.reshape(model), router_grad.T, router_b_grad.reshape(-1),
        grad_gu, grad_gub, grad_down, grad_db,
    )


def solution(mesh):
    sizes = dict(mesh.shape)
    side = int(round(sizes["seq"] ** 0.5))
    wide = Mesh(
        mesh.devices.reshape(side, sizes["seq"] // side, sizes["fsdp"] // 2, 2), ("x", "z", "y", "c")
    )
    in_specs = (
        P(ALL, None), P(ALL, None), P(), P(SEQ, FSDP), P(FSDP), P(SEQ, FSDP), P(FSDP), P(SEQ, FSDP), P(FSDP),
        P(FSDP, SEQ), P(), P(FSDP), P(), P(), P(), P(SEQ, None, None, FSDP), P(SEQ, None, FSDP),
        P(SEQ, FSDP, None), P(SEQ, None), P(ALL, None),
    )
    out_specs = (
        P(ALL, None), P(ALL, None), P(), P(SEQ, FSDP), P(FSDP), P(SEQ, FSDP), P(FSDP), P(SEQ, FSDP), P(FSDP),
        P(FSDP, SEQ), P(), P(FSDP), P(), P(), P(), P(SEQ, None, None, FSDP), P(SEQ, None, FSDP),
        P(SEQ, FSDP, None), P(SEQ, None),
    )
    return jax.shard_map(shards, mesh=wide, in_specs=in_specs, out_specs=out_specs, check_vma=False)
```

```python
import jax
import jax.numpy as jnp
import numpy as np
from jax import lax
from jax.experimental import pallas as pl
from jax.experimental.pallas import tpu as pltpu
from jax.sharding import Mesh, PartitionSpec as P

HEAD_WIDTH = 64
WINDOW = 128
norm_eps = 1e-05
rope_base = 150000.0
swiglu_limit = 7.0
glu_alpha = 1.702
masked_score = -1000000000.0

SEQ = ("x", "z")
FSDP = ("y", "c")
COLUMN = ("x", "z", "c")
ALL = ("x", "z", "y", "c")
f32 = jnp.float32
bf16 = jnp.bfloat16
SCALE = HEAD_WIDTH ** (-0.5)
SHIFTS = (0, 1, -1, 2)


def dot(a, b, dims=((1,), (0,))):
    return lax.dot_general(a, b, (dims, ((), ())), preferred_element_type=f32)


ROWS_BY = ((0,), (0,))
BY_ROWS = ((1,), (1,))


def inv_rms(values):
    return lax.rsqrt(jnp.mean(values * values, axis=-1, keepdims=True) + norm_eps)


def norm_back(grad, normed, root, gain):
    scaled = grad * gain
    return root * (scaled - normed * jnp.mean(scaled * normed, axis=-1, keepdims=True))


def halves(value):
    high = value.astype(bf16)
    return high, (value - high.astype(f32)).astype(bf16)


def lanes(shape):
    return lax.broadcasted_iota(jnp.int32, shape, len(shape) - 1)


def sublanes(shape):
    return lax.broadcasted_iota(jnp.int32, shape, len(shape) - 2)


def swap_halves(values):
    lane = lanes(values.shape) % HEAD_WIDTH
    return jnp.where(lane < 32, pltpu.roll(values, 96, 1), pltpu.roll(values, 32, 1))


def turn(values, cos, sin):
    return values * cos + swap_halves(values) * sin


def exchange(value, axes):
    return lax.all_to_all(value, axes, split_axis=0, concat_axis=0, tiled=True)


def broadcast_exchange(value, axes, count):
    return exchange(jnp.broadcast_to(value[None], (count,) + value.shape), axes)


def after(value, *earlier):
    return lax.optimization_barrier((value,) + earlier)[0]


def along(axis, value, steps):
    count = lax.axis_size(axis)
    return lax.ppermute(value, axis, [(k, (k + steps) % count) for k in range(count)])


def other_core(value):
    return lax.ppermute(value, "c", [(0, 1), (1, 0)])


def kernel_call(body, outs, ins, flops=0, scalars=1, scratch=(), vmem=32, to_hbm=(), from_hbm=()):
    specs = [pl.BlockSpec(memory_space=pltpu.SMEM)] * scalars
    specs += [pl.BlockSpec(memory_space=pltpu.VMEM)] * (len(ins) - scalars)
    ins = [pltpu.with_memory_space_constraint(a, pltpu.HBM) if n in from_hbm else a for n, a in enumerate(ins)]
    out_shape = [jax.ShapeDtypeStruct(shape, kind) for shape, kind in outs]
    moved = sum(a.size * a.dtype.itemsize for a in ins)
    moved += sum(s.size * jnp.dtype(s.dtype).itemsize for s in out_shape)
    return pl.pallas_call(
        body,
        out_shape=[pltpu.HBM(s.shape, s.dtype) if n in to_hbm else s for n, s in enumerate(out_shape)],
        in_specs=specs,
        out_specs=[pl.BlockSpec(memory_space=pltpu.VMEM)] * len(outs),
        scratch_shapes=scratch,
        compiler_params=pltpu.CompilerParams(vmem_limit_bytes=vmem << 20),
        cost_estimate=pl.CostEstimate(flops=flops, bytes_accessed=moved, transcendentals=0),
    )(*ins)


def norm_body(x_ref, gain_ref, q_ref, k_ref, v_ref, o_ref, h_ref, packed_ref):
    x = x_ref[...].astype(f32)
    h_ref[...] = (x * inv_rms(x) * gain_ref[...].astype(f32)).astype(bf16)
    packed_ref[...] = jnp.concatenate([q_ref[...], k_ref[...], v_ref[...], o_ref[...]], axis=1)


def stack_body(*refs):
    count = refs[0].shape[0]
    for n, ref in enumerate(refs[:-1]):
        refs[-1][n * count : (n + 1) * count, :] = ref[...]


def waves(within_ref, base_ref, b):
    cos_in, sin_in = within_ref[:WINDOW, :], within_ref[WINDOW:, :]
    cos_at, sin_at = base_ref[b : b + 1, :], base_ref[16 + b : 17 + b, :]
    sine = sin_at * cos_in + cos_at * sin_in
    first = lanes(sine.shape) % HEAD_WIDTH < HEAD_WIDTH // 2
    return cos_at * cos_in - sin_at * sin_in, jnp.where(first, -sine, sine)


def plan_body(cap, experts, routes_ref, g_ref, place_ref, send_ref, hot_ref):
    tok, top = routes_ref.shape
    model = g_ref.shape[1]
    slots = place_ref.shape[1]
    routes = routes_ref[...]
    ids = lanes((tok, 128))
    hot = jnp.zeros((tok, 128), f32)
    for k in range(top):
        hot += (routes[:, k : k + 1] == ids).astype(f32)
    hot_low = hot.astype(bf16)
    before = (lanes((tok, tok)) < sublanes((tok, tok))).astype(f32).astype(bf16)
    rank = dot(before, hot_low)
    marked = jnp.where(hot > 0, rank, -1.0).astype(bf16)
    slot = lanes((128, slots))
    start = sublanes((128, slots)) * cap
    spread = ((slot >= start) & (slot < start + cap)).astype(f32).astype(bf16)
    wide = dot(marked, spread)
    lane = lanes((tok, slots)).astype(f32)
    within = lane - cap * jnp.floor((lane + 0.5) * (1.0 / cap))
    place = (wide == within).astype(f32).astype(bf16)
    place_ref[...] = place
    hot_ref[...] = hot[:, :experts]
    send_ref[:, :model] = dot(place, g_ref[...], ROWS_BY).astype(bf16)
    send_ref[:, model:] = dot(place, hot_low, ROWS_BY).astype(bf16)


def assemble(at_ref, pieces, block_ref, tok, ys):
    y, core = at_ref[0], at_ref[1]
    for n, piece in enumerate(pieces):
        from_y = lax.rem(y - SHIFTS[n % 4] + ys, ys)
        from_core = core if n < 4 else 1 - core
        start = pl.multiple_of((from_y * 2 + from_core) * tok, tok)
        block_ref[pl.ds(start, tok), :] = piece[...]


def project_body(ys, at_ref, sink_ref, *refs):
    block_ref, halos, w_pieces, refs = refs[0], refs[1 : 1 + ys], refs[1 + ys : 5 + ys], refs[5 + ys :]
    bias_ref, within_ref, base_ref = refs[:3]
    w_ref, q_ref, k_ref, v_ref, att_ref, out_ref, halo_ref = refs[3:]
    share = w_pieces[0].shape[0] // 4
    for n, piece in enumerate(w_pieces):
        for k in range(4):
            from_z = lax.rem(at_ref[5] - SHIFTS[n] + 4, 4)
            from_x = lax.rem(at_ref[4] - SHIFTS[k] + 4, 4)
            start = pl.multiple_of((from_x * 4 + from_z) * share, share)
            w_ref[pl.ds(start, share), :] = piece[k * share : (k + 1) * share, :]
    rows = block_ref.shape[0]
    tok = rows // (2 * ys)
    halo_ref[...] = sum((ref[...] for ref in halos[1:]), halos[0][...])
    weights = w_ref[:, :256]
    low = lanes((WINDOW, 128)) < 64

    def keys_values(kv, b, wave):
        at = slice(b * WINDOW, (b + 1) * WINDOW)
        turned = pltpu.roll(kv, 64, 1)
        k_ref[at, :] = turn(jnp.where(low, kv, turned), *wave).astype(bf16)
        v_ref[at, :] = jnp.where(low, turned, kv).astype(bf16)

    keys_values(dot(halo_ref[...], weights[:, 128:]) + bias_ref[:, 128:], 0, waves(within_ref, base_ref, 0))
    for r in range(0, rows, 2 * WINDOW):
        both = dot(block_ref[r : r + 2 * WINDOW, :], weights) + bias_ref[...]
        for k in range(2):
            qkv = both[k * WINDOW : (k + 1) * WINDOW]
            b = r // WINDOW + k
            wave = waves(within_ref, base_ref, b + 1)
            q_ref[b * WINDOW : (b + 1) * WINDOW, :] = turn(qkv[:, :128], *wave).astype(bf16)
            keys_values(qkv[:, 128:], b + 1, wave)
    sink = sink_column(sink_ref)
    for b in range(rows // WINDOW):
        part = slice(b * WINDOW, (b + 1) * WINDOW)
        near = slice(b * WINDOW, (b + 2) * WINDOW)
        q2 = stack_heads(q_ref[part, :])
        probs, _ = soft_rows(q2, k_ref[near, :], band(at_ref, b == 0), sink)
        both = dot(probs.astype(bf16), v_ref[near, :])
        att_ref[part, :] = jnp.where(low, both[:WINDOW], both[WINDOW:]).astype(bf16)
    to_other(at_ref, att_ref, w_ref[:, 256:384], out_ref, tok, ys)


def band(at_ref, first):
    shape = (2 * WINDOW, 2 * WINDOW)
    i, j = sublanes(shape), lanes(shape)
    off = jnp.where(i >= WINDOW, i - WINDOW, i) + WINDOW - j
    allowed = (off >= 0) & (off < WINDOW)
    if first:
        allowed = allowed & ((j >= WINDOW) | (at_ref[2] > 0))
    return allowed


def stack_heads(pair):
    low = lanes(pair.shape) < 64
    zero = jnp.zeros_like(pair)
    return jnp.concatenate([jnp.where(low, pair, zero), jnp.where(low, zero, pair)], axis=0)


def soft_rows(q2, keys, allowed, sink):
    scores = jnp.where(allowed, dot(q2, keys, BY_ROWS) * SCALE, masked_score)
    top = jnp.maximum(jnp.max(scores, axis=-1, keepdims=True), sink)
    weights = jnp.exp(scores - top)
    sunk = jnp.exp(sink - top)
    inverse = 1.0 / (jnp.sum(weights, axis=-1, keepdims=True) + sunk)
    return weights * inverse, sunk * inverse


def sink_column(sink_ref):
    row = sublanes((2 * WINDOW, 1))
    return jnp.where(row < WINDOW, sink_ref[0], sink_ref[1])


def to_other(at_ref, rows_ref, weights, out_ref, tok, ys):
    for n, shift in enumerate(SHIFTS):
        to_y = lax.rem(at_ref[0] + shift + ys, ys)
        theirs = pl.multiple_of((to_y * 2 + 1 - at_ref[1]) * tok, tok)
        out_ref[n] = dot(rows_ref[pl.ds(theirs, tok), :], weights, BY_ROWS).astype(bf16)


def pair_body(ys, lo, hi, at_ref, rows_ref, w_ref, other_ref, *outs):
    tok = other_ref.shape[1]
    for n, shift in enumerate(SHIFTS):
        to_y = lax.rem(at_ref[0] + shift + ys, ys)
        mine = pl.multiple_of((to_y * 2 + at_ref[1]) * tok, tok)
        own = dot(rows_ref[pl.ds(mine, tok), :], w_ref[:, lo:hi], BY_ROWS)
        outs[n][...] = (own + other_ref[n].astype(f32)).astype(outs[n].dtype)


def gates(values, mask):
    masked = jnp.where(mask, values, masked_score)
    ex = jnp.where(mask, jnp.exp(masked - jnp.max(masked, axis=-1, keepdims=True)), 0.0)
    total = jnp.sum(ex, axis=-1, keepdims=True)
    return ex / jnp.where(total > 0, total, 1.0)


def route_body(
    first_ref, a_ref, b_ref, c_ref, x_ref, rows_ref, rw_ref, rb_ref, place_ref, hot_ref,
    res_ref, h2_ref, gate_ref, send_ref,
):
    tok, experts = gate_ref.shape
    total = first_ref[...] + a_ref[...].astype(f32) + b_ref[...].astype(f32) + c_ref[...].astype(f32)
    residual = x_ref[...].astype(f32) + total + rows_ref[1:2, :].astype(f32)
    res_ref[...] = residual
    h2 = (residual * inv_rms(residual) * rows_ref[:1, :].astype(f32)).astype(bf16)
    h2_ref[...] = h2
    send_ref[...] = dot(place_ref[...], h2, ROWS_BY).astype(bf16)
    logits = dot(h2, rw_ref[...], BY_ROWS) + rb_ref[...].astype(f32)
    gate_ref[...] = gates(logits, hot_ref[...] > 0)


def expert_body(
    ys, at_ref, rows_ref, side_ref, u_ref, wide_ref, bias_ref, rw_ref, rb_ref, hidden_ref, dpre_ref, back_ref, p_ref
):
    model = rows_ref.shape[1]
    experts = rw_ref.shape[0]
    half = wide_ref.shape[0] // (2 * ys)
    step = 256
    for r in range(0, rows_ref.shape[0], step):
        at = slice(r, r + step)
        rows = rows_ref[at, :]
        logits = dot(rows, rw_ref[...], BY_ROWS) + rb_ref[...].astype(f32)
        mask = side_ref[at, :experts] > 0
        mine = lanes((step, experts)) == at_ref[3]
        p = jnp.sum(jnp.where(mine, gates(logits, mask), 0.0), axis=-1, keepdims=True)
        p_ref[at, :] = jnp.broadcast_to(p, (step, 128))
        pre = dot(rows, wide_ref[...], BY_ROWS) + bias_ref[:1, :]
        dgate = jnp.zeros((step, half), f32)
        for n in range(ys):
            low = 2 * n * half
            gt = jnp.tanh(pre[:, low : low + half] * (1.0 / swiglu_limit))
            ut = jnp.tanh(pre[:, low + half : low + 2 * half] * (1.0 / swiglu_limit))
            gate, up = swiglu_limit * gt, swiglu_limit * ut + 1.0
            sig = 0.5 * jnp.tanh((0.5 * glu_alpha) * gate) + 0.5
            gs = gate * sig
            hidden = (up * gs).astype(bf16)
            u = u_ref[at, n * half : (n + 1) * half]
            dgate += hidden.astype(f32) * u
            hidden_ref[at, n * half : (n + 1) * half] = hidden
            dh = p * u
            d_gate = dh * up * (sig + glu_alpha * gs * (1.0 - sig)) * (1.0 - gt * gt)
            d_up = dh * gs * (1.0 - ut * ut)
            dpre_ref[at, low : low + half] = d_gate.astype(bf16)
            dpre_ref[at, low + half : low + 2 * half] = d_up.astype(bf16)
        back_ref[at, :model] = dot(dpre_ref[at, :], wide_ref[...]).astype(bf16)
        dgate = jnp.sum(dgate, axis=-1, keepdims=True) + side_ref[at, experts : experts + 1]
        high, rest = halves(dgate)
        middle, low = halves(dgate - high.astype(f32))
        lane = lanes((step, 128))
        parts = jnp.where(lane == 0, high.astype(f32), jnp.where(lane == 1, middle.astype(f32), low.astype(f32)))
        back_ref[at, model:] = jnp.where(lane < 3, parts, 0.0).astype(bf16)


def by_chunks(body, step, at, cut_in, whole_in, outs, flops, whole_out=(), vmem=60):
    slots = cut_in[0].shape[0]

    def cut(width):
        return pl.BlockSpec((step, width), lambda n: (n, 0))

    def whole(a):
        return pl.BlockSpec(a.shape, lambda n: (0,) * a.ndim)

    return pl.pallas_call(
        body,
        grid=(slots // step,),
        out_shape=[jax.ShapeDtypeStruct((slots, w_), kind) for w_, kind in outs] + list(whole_out),
        in_specs=[pl.BlockSpec(memory_space=pltpu.SMEM)]
        + [cut(a.shape[1]) for a in cut_in]
        + [whole(a) for a in whole_in],
        out_specs=[cut(w_) for w_, _ in outs] + [whole(a) for a in whole_out],
        compiler_params=pltpu.CompilerParams(vmem_limit_bytes=vmem << 20),
        cost_estimate=pl.CostEstimate(flops=flops, bytes_accessed=16 << 20, transcendentals=0),
    )(at, *cut_in, *whole_in)


def split_experts_body(at_ref, gu_ref, down_ref, bias_ref, own_ref, theirs_ref):
    wide, half = gu_ref.shape[1], down_ref.shape[1]
    for ref, expert in ((own_ref, at_ref[1]), (theirs_ref, 1 - at_ref[1])):
        ref[:wide, :] = gu_ref[expert]
        ref[wide : wide + half, :] = down_ref[expert]
        ref[wide + half :, :] = jnp.zeros((16, ref.shape[1]), bf16)
        ref[wide + half : wide + half + 1, :wide] = bias_ref[expert]


def join_experts_body(own_ref, theirs_ref, out_ref):
    half = (own_ref.shape[0] - 16) // 3
    for n in range(3):
        part = slice(n * half, (n + 1) * half)
        out_ref[2 * n * half : (2 * n + 1) * half, :] = own_ref[part, :]
        out_ref[(2 * n + 1) * half : (2 * n + 2) * half, :] = theirs_ref[part, :]
    out_ref[6 * half :, :] = jnp.concatenate(
        [own_ref[3 * half : 3 * half + 8, :], theirs_ref[3 * half : 3 * half + 8, :]], axis=0
    )


def early_body(experts, at_ref, g_ref, w_ref, bd_ref, u_ref, side_ref, wide_ref, bias_ref):
    model = w_ref.shape[2]
    half = (w_ref.shape[1] - 16) // 3
    own = half // 2

    @pl.when(pl.program_id(0) == 0)
    def _():
        for n in range(w_ref.shape[0]):
            part = slice(2 * n * half, 2 * (n + 1) * half)
            wide_ref[part, :] = w_ref[n, : 2 * half, :]
            first, second = w_ref[n, 3 * half : 3 * half + 1, :half], w_ref[n, 3 * half + 8 : 3 * half + 9, :half]
            bias = jnp.concatenate([first[:, :own], second[:, :own], first[:, own:], second[:, own:]], axis=1)
            bias_ref[:, part] = jnp.broadcast_to(bias.astype(f32), (8, 2 * half))

    g = g_ref[:, :model]
    for n in range(w_ref.shape[0]):
        u_ref[:, n * half : (n + 1) * half] = dot(g, w_ref[n, 2 * half : 3 * half, :], BY_ROWS)
    bias = jnp.sum(g.astype(f32) * bd_ref[...], axis=-1, keepdims=True)
    hot = g_ref[:, model:].astype(f32)
    side_ref[...] = jnp.where(lanes(hot.shape) < experts, hot, bias)


def weights_body(ys, rows_ref, g_ref, hidden_ref, dpre_ref, p_ref, sum_ref):
    slots, model = rows_ref.shape
    ff = hidden_ref.shape[1]
    half = ff // ys
    own = half // 2
    step = 256
    dys = []
    bias = jnp.zeros((1, model), f32)
    for r in range(0, slots, step):
        part = slice(r, r + step)
        dy = (p_ref[part, :1] * g_ref[part, :model].astype(f32)).astype(bf16)
        bias += jnp.sum(dy.astype(f32), axis=0, keepdims=True)
        dys.append(dy)
    dy = jnp.concatenate(dys, axis=0)
    high, low = halves(bias)
    row = sublanes((16, model))
    for n in range(ys):
        dpre = dpre_ref[:, 2 * n * half : 2 * (n + 1) * half]
        dw = dot(dpre, rows_ref[...], ROWS_BY)
        ddown = dot(hidden_ref[:, n * half : (n + 1) * half], dy, ROWS_BY)
        parts = [dw[:own], dw[half : half + own], ddown[:own], dw[own:half], dw[half + own :], ddown[own:]]
        for k, part in enumerate(parts):
            sum_ref[n, k * own : (k + 1) * own, :] = part.astype(bf16)
        b = jnp.sum(dpre.astype(f32), axis=0, keepdims=True)
        b = jnp.concatenate([b, jnp.zeros((1, model - 2 * half), f32)], axis=1)
        tail = jnp.where(row == 1, high.astype(f32), jnp.where(row == 2, low.astype(f32), 0.0))
        sum_ref[n, 3 * half :, :] = jnp.where(row == 0, b, tail).astype(bf16)


def forward_body(ys, at_ref, hidden_ref, p_ref, w_ref, bd_ref, y_ref):
    half = hidden_ref.shape[1] // ys
    w_down = jnp.concatenate([w_ref[n, 2 * half : 3 * half, :] for n in range(ys)], axis=0)
    y_ref[...] = (p_ref[:, :1] * (dot(hidden_ref[...], w_down) + bd_ref[...])).astype(bf16)


def experts_out_body(at_ref, own_ref, theirs_ref, gu_ref, down_ref, gub_ref, db_ref):
    core = at_ref[1]
    half = down_ref.shape[1]
    gu_ref[core] = own_ref[: 2 * half, :].astype(f32)
    gu_ref[1 - core] = theirs_ref[3 * half : 5 * half, :].astype(f32)
    down_ref[core] = own_ref[2 * half : 3 * half, :].astype(f32)
    down_ref[1 - core] = theirs_ref[5 * half : 6 * half, :].astype(f32)
    own, theirs = own_ref[6 * half :, :].astype(f32), theirs_ref[6 * half :, :].astype(f32)

    def by_expert(mine, other):
        return jnp.where(sublanes((2, mine.shape[1])) == core, mine, other)

    mine = jnp.concatenate([own[:1, :half], own[:1, 2 * half : 3 * half]], axis=1)
    other = jnp.concatenate([theirs[:1, half : 2 * half], theirs[:1, 3 * half : 4 * half]], axis=1)
    gub_ref[...] = by_expert(mine, other)
    db_ref[...] = by_expert(own[1:2] + own[2:3], theirs[1:2] + theirs[2:3])


def sums_body(in_ref, q_ref, k_ref, v_ref, o_ref, qb_ref, kb_ref, vb_ref, sink_ref, last_ref):
    total = in_ref[0].astype(f32)
    for n in range(1, in_ref.shape[0]):
        total += in_ref[n].astype(f32)
    share = q_ref.shape[0]
    q_ref[...] = total[:share, :128]
    k_ref[...] = total[:share, 128:192]
    v_ref[...] = total[:share, 192:256]
    o_ref[...] = total[:share, 256:]
    sums = jnp.concatenate([total[share:, :128], total[share:, 128:256], total[share:, 256:]], axis=0)
    qb_ref[...] = sums[36:37]
    kb_ref[...] = sums[37:38, :64]
    vb_ref[...] = sums[37:38, 64:]
    sink_ref[...] = sums[38:39, :2]
    for n in range(last_ref.shape[0]):
        last_ref[n] = sums


def last_body(in_ref, router_ref, router_b_ref, o_bias_ref, gain_two_ref, gain_one_ref):
    experts = router_ref.shape[0]
    for n in range(in_ref.shape[0]):
        router_ref[:, n * 128 : (n + 1) * 128] = in_ref[n, :experts, :]
    row = sublanes((8, 128))
    o_bias = gain_two = gain_one = jnp.zeros((8, 128), f32)
    for n in range(in_ref.shape[0]):
        o_bias = jnp.where(row == n, in_ref[n, experts : experts + 1, :], o_bias)
        gain_two = jnp.where(row == n, in_ref[n, experts + 1 : experts + 2, :], gain_two)
        gain_one = gain_one + in_ref[n, experts + 8 :, :]
    o_bias_ref[...] = o_bias
    gain_two_ref[...] = gain_two
    gain_one_ref[...] = gain_one
    router_b_ref[...] = in_ref[0, experts + 2 : experts + 3, :experts]


def unroute_body(
    cap, back_ref, place_ref, gate_ref, h2_ref, res_ref, g_ref, rw_ref, gain_ref, dres_ref, da_ref
):
    tok, experts = gate_ref.shape
    slots, model = place_ref.shape[1], h2_ref.shape[1]
    place = place_ref[...]
    slot = sublanes((slots, experts))
    start = lanes((slots, experts)) * cap
    own = (slot >= start) & (slot < start + cap)
    dgate = jnp.zeros((tok, experts), f32)
    for k in range(3):
        column = back_ref[:, model + k : model + k + 1].astype(f32)
        dgate += dot(place, jnp.where(own, column, 0.0).astype(bf16))
    gate = gate_ref[...]
    dlogits = gate * (dgate - jnp.sum(gate * dgate, axis=-1, keepdims=True))
    high, low = halves(dlogits)
    router = rw_ref[...]
    grad = dot(place, back_ref[:, :model]) + dot(high, router) + dot(low, router)
    h2 = h2_ref[...]
    router_grad = dot(high, h2, ROWS_BY) + dot(low, h2, ROWS_BY)
    residual = res_ref[...]
    root = inv_rms(residual)
    normed = residual * root
    dres = g_ref[...].astype(f32) + norm_back(grad, normed, root, gain_ref[...].astype(f32))
    dres_ref[...] = dres
    o_bias = jnp.sum(dres, axis=0, keepdims=True)
    gain_sum = jnp.sum(grad * normed, axis=0, keepdims=True)
    router_b = jnp.sum(dlogits, axis=0, keepdims=True)
    router_b = jnp.concatenate([router_b, jnp.zeros((1, 128 - experts), f32)], axis=1)
    router_b = jnp.concatenate([router_b] * (model // 128), axis=1)
    row = sublanes((16, model))
    rest = jnp.where(row == 0, o_bias, jnp.where(row == 1, gain_sum, jnp.where(row == 2, router_b, 0.0)))
    da_ref[:tok, :] = dres.astype(bf16)
    da_ref[tok : tok + experts, :] = router_grad.astype(bf16)
    da_ref[tok + experts :, :] = rest.astype(bf16)


def block_back(at_ref, sink, b, q_ref, datt_ref, k_ref, v_ref):
    part = slice(b * WINDOW, (b + 1) * WINDOW)
    near = slice(b * WINDOW, (b + 2) * WINDOW)
    low = lanes((WINDOW, 128)) < 64
    q2 = stack_heads(q_ref[part, :])
    g2 = stack_heads(datt_ref[part, :])
    keys = k_ref[near, :]
    probs, sunk = soft_rows(q2, keys, band(at_ref, b == 0), sink)
    dprobs = dot(g2, v_ref[near, :], BY_ROWS)
    delta = jnp.sum(probs * dprobs, axis=-1, keepdims=True)
    dscores = (probs * (dprobs - delta)).astype(bf16)
    dq2 = dot(dscores, keys)
    dq = jnp.where(low, dq2[:WINDOW], dq2[WINDOW:]) * SCALE
    dk2 = dot(dscores, q2, ROWS_BY) * SCALE
    dv2 = dot(probs.astype(bf16), g2, ROWS_BY)
    wide = lanes(dk2.shape) < 64
    dkv = jnp.where(wide, dk2 + pltpu.roll(dk2, 64, 1), dv2 + pltpu.roll(dv2, 64, 1))
    return dq, dkv, sunk * delta


def turn_back(values, cos, sin):
    return values * cos - swap_halves(values) * sin


def back_first_body(ys, at_ref, sink_ref, *refs):
    pieces, refs = refs[:8], refs[8:]
    w_ref, q_ref, k_ref, v_ref = refs[:4]
    block_ref, datt_ref, head_ref, dq_ref, carry_ref, sink_out_ref, sums_ref = refs[4:]
    tok = block_ref.shape[0] // (2 * ys)
    assemble(at_ref, [piece.at[:tok, :] for piece in pieces], block_ref, tok, ys)
    own = pl.ds(pl.multiple_of((at_ref[0] * 2 + at_ref[1]) * 128, 128), 128)
    total = pieces[0][tok:, own].astype(f32)
    for piece in pieces[1:]:
        total += piece[tok:, own].astype(f32)
    sums_ref[...] = total
    weights = w_ref[:, 256:384]
    for r in range(0, block_ref.shape[0], 256):
        datt_ref[r : r + 256, :] = dot(block_ref[r : r + 256, :], weights).astype(bf16)
    dq, dkv, sunk = block_back(at_ref, sink_column(sink_ref), 0, q_ref, datt_ref, k_ref, v_ref)
    head_ref[...] = dkv[:WINDOW].astype(bf16)
    carry_ref[...] = dkv[WINDOW:]
    dq_ref[...] = dq
    sink_out_ref[...] = jnp.broadcast_to(sunk, sink_out_ref.shape)


def back_rest_body(
    at_ref, sink_ref, datt_ref, q_ref, k_ref, v_ref, within_ref, base_ref, dq_ref, carry_ref, sunk_ref,
    block_ref, att_ref, dqkv_ref, last_ref, sink_out_ref, dwo_ref,
):
    rows = q_ref.shape[0]
    sink = sink_column(sink_ref)
    low = lanes((WINDOW, 128)) < 64
    for d in range(0, dwo_ref.shape[0], 256):
        dwo_ref[d : d + 256, :] = dot(block_ref[:, d : d + 256], att_ref[...], ROWS_BY).astype(bf16)
    sink_sum = sunk_ref[:, :1]
    carry = carry_ref[...]
    for b in range(rows // WINDOW):
        part = slice(b * WINDOW, (b + 1) * WINDOW)
        wave = waves(within_ref, base_ref, b + 1)
        if b == 0:
            dq = dq_ref[...]
        else:
            dq, dkv, sunk = block_back(at_ref, sink, b, q_ref, datt_ref, k_ref, v_ref)
            sink_sum += sunk
            done = carry + dkv[:WINDOW]
            carry = dkv[WINDOW:]
            before = slice((b - 1) * WINDOW, b * WINDOW)
            dqkv_ref[before, 128:] = jnp.where(low, turn_back(done, *last_wave), done).astype(bf16)
        dqkv_ref[part, :128] = turn_back(dq, *wave).astype(bf16)
        last_wave = wave
    last_ref[...] = carry
    dqkv_ref[rows - WINDOW :, 128:] = jnp.zeros((WINDOW, 128), bf16)
    total0 = jnp.sum(sink_sum[:WINDOW], axis=0, keepdims=True)
    total1 = jnp.sum(sink_sum[WINDOW:], axis=0, keepdims=True)
    lane = lanes((8, 128))
    sink_out_ref[...] = -jnp.where(lane == 0, total0, jnp.where(lane == 1, total1, 0.0))


def unproject_body(ys, tok, at_ref, part_ref, last_ref, ret_ref, within_ref, base_ref, w_ref, dqkv_ref, out_ref):
    rows = part_ref.shape[0]
    low = lanes((WINDOW, 128)) < 64
    dqkv_ref[...] = part_ref[...]
    dkv = last_ref[...] + ret_ref[...].astype(f32)
    turned = turn_back(dkv, *waves(within_ref, base_ref, rows // WINDOW))
    dqkv_ref[rows - WINDOW :, 128:] = jnp.where(low, turned, dkv).astype(bf16)
    to_other(at_ref, dqkv_ref, w_ref[:, :256], out_ref, tok, ys)


def attention_weights_body(
    dqkv_ref, block_ref, dwo_ref, w_ref, gain_ref, sink_ref, sums_ref, send_ref
):
    model = block_ref.shape[1]
    bias = jnp.sum(dqkv_ref[...].astype(f32), axis=0, keepdims=True)
    bias = jnp.concatenate([bias, sink_ref[:1, :]], axis=1)
    step = 256
    seqs = send_ref.shape[0]
    share = model // seqs
    per = step // share
    ones = jnp.ones((8, 256), bf16)
    gains = []
    for d in range(0, model, step):
        dw = dot(block_ref[:, d : d + step], dqkv_ref[...], ROWS_BY)
        for k in range(per):
            part = slice(k * share, (k + 1) * share)
            send_ref[d // share + k, :share, :256] = dw[part].astype(bf16)
            send_ref[d // share + k, :share, 256:] = dwo_ref[d + k * share : d + (k + 1) * share, :]
        first, second = halves(dw * w_ref[d : d + step, :256].astype(f32))
        gains.append((dot(ones, first, BY_ROWS) + dot(ones, second, BY_ROWS))[:1])
    gain = jnp.concatenate(gains, axis=1) / gain_ref[...].astype(f32)
    row = sublanes((8, 128))
    middle = sums_ref[32:40, :]
    for n, line in enumerate([bias[:, :128], bias[:, 128:256], bias[:, 256:]]):
        middle = jnp.where(row == n + 4, line, middle)
    gain = jnp.concatenate([gain[:, n * 128 : (n + 1) * 128] for n in range(8)], axis=0)
    third = jnp.concatenate([middle, gain], axis=0)
    tail = jnp.concatenate([sums_ref[:16, :], sums_ref[16:32, :], third], axis=1).astype(bf16)
    for s in range(seqs):
        send_ref[s, share:, :] = tail


def finish_body(first_ref, a_ref, b_ref, c_ref, x_ref, gain_ref, dres_ref, out_ref):
    grad = first_ref[...] + a_ref[...].astype(f32) + b_ref[...].astype(f32) + c_ref[...].astype(f32)
    x = x_ref[...].astype(f32)
    root = inv_rms(x)
    out = dres_ref[...] + norm_back(grad, x * root, root, gain_ref[...].astype(f32))
    out_ref[...] = out.astype(bf16)


def gather_pieces(own):
    mine = [own] + list(lax.optimization_barrier(tuple(along("y", own, s) for s in SHIFTS[1:])))
    return mine + [other_core(piece) for piece in mine]


def sum_pieces(ys, at, rows, weights, lo, hi, out, **where):
    theirs = other_core(out)
    tok, model = out.shape[1:]
    first, *rest = kernel_call(
        lambda *refs: pair_body(ys, lo, hi, *refs),
        [((tok, model), f32)] + [((tok, model), bf16)] * 3,
        [at, rows, weights, theirs],
        **where,
    )
    sent = tuple(along("y", piece, s) for piece, s in zip(rest, SHIFTS[1:]))
    return [first] + list(lax.optimization_barrier(sent))


def shards(
    tokens, cotangent, norm_gain, q_weight, q_bias, key_matrix, key_bias, value_matrix, value_bias,
    o_weight, o_bias, sinks, moe_gain, router_weight, router_bias, gate_up_weight, gate_up_bias,
    down_weight, down_bias, routes,
):
    zs, ys = lax.axis_size("z"), lax.axis_size("y")
    seqs = lax.axis_size("x") * zs
    seq_index = lax.axis_index("x") * zs + lax.axis_index("z")
    core = lax.axis_index("c")
    tok, model = tokens.shape
    rows = tok * ys * 2
    experts = 2 * seqs
    top = routes.shape[1]
    cap = 3 * tok * top // (2 * experts)
    slots = experts * cap
    ff_own = gate_up_weight.shape[-1]
    ff = 2 * ff_own * ys
    at = jnp.stack(
        [lax.axis_index("y"), core, seq_index, 2 * seq_index + core, lax.axis_index("x"), lax.axis_index("z")]
    ).astype(jnp.int32)
    gain_one, router_rows = norm_gain[None], router_weight.T

    h_low, packed = kernel_call(
        norm_body,
        [((tok, model), bf16), ((model // seqs, 384), bf16)],
        [tokens, gain_one, q_weight, key_matrix, value_matrix, o_weight.T],
        scalars=0,
        vmem=60,
    )
    count = 2 * ys
    last = count - 1
    halo = [
        lax.ppermute(h_low, ALL, [(s * count + last, (s + 1) * count + place) for s in range(seqs - 1)])
        for place in (last, last - 1)
    ]
    block_h = lax.all_gather(h_low, FSDP, axis=0, tiled=True)

    packed = [packed] + [along("x", packed, s) for s in SHIFTS[1:]]
    (packed,) = kernel_call(stack_body, [((4 * model // seqs, 384), bf16)], packed, scalars=0)
    w_pieces = [packed] + list(lax.optimization_barrier(tuple(along("z", packed, s) for s in SHIFTS[1:])))

    place, g_send, hot = kernel_call(
        lambda *refs: plan_body(cap, experts, *refs),
        [((tok, slots), bf16), ((slots, model + 128), bf16), ((tok, experts), f32)],
        [after(routes, packed), cotangent],
        to_hbm=(1,),
        scalars=0,
        flops=2 * tok * slots * (model + 256),
    )
    halo_both = after(halo[0] + halo[1], g_send, *w_pieces)
    halo = [halo_both] + [
        lax.ppermute(halo_both, FSDP, [(last, place), (last - 1, place - 1)]) for place in range(1, last, 2)
    ]
    g_send = after(g_send, *w_pieces, halo_both)
    g_all = exchange(g_send.reshape(experts, cap, model + 128), COLUMN).reshape(slots, model + 128)

    own, theirs = kernel_call(
        split_experts_body,
        [((3 * ff_own + 16, model), bf16)] * 2,
        [at, gate_up_weight.transpose(0, 2, 3, 1).reshape(2, 2 * ff_own, model), down_weight,
         gate_up_bias.reshape(2, 1, 2 * ff_own)],
        from_hbm=(1, 2),
    )
    (shard,) = kernel_call(
        join_experts_body, [((6 * ff_own + 16, model), bf16)], [own, other_core(theirs)], scalars=0
    )
    b_down = lax.dynamic_index_in_dim(down_bias, core, 0, keepdims=True).astype(f32)

    wave = np.tile(np.arange(HEAD_WIDTH // 2), 4).astype(np.float32)
    inverse = rope_base ** (-(jnp.asarray(wave) * 2.0 / HEAD_WIDTH))
    inner = after(jnp.arange(WINDOW, dtype=f32), w_pieces[0])[:, None] * inverse[None, :]
    starts = after(seq_index, w_pieces[0]) * rows - WINDOW + WINDOW * jnp.arange(16, dtype=jnp.int32)
    outer = starts.astype(f32)[:, None] * inverse[None, :]
    within = jnp.concatenate([jnp.cos(inner), jnp.sin(inner)], axis=0)
    base = jnp.concatenate([jnp.cos(outer), jnp.sin(outer)], axis=0)
    gain_rows = after(jnp.stack([moe_gain, o_bias]), w_pieces[0])
    gain_two = gain_rows[:1]
    bias_qkv = jnp.concatenate([after(q_bias, w_pieces[0]), key_bias, value_bias]).astype(f32)[None]
    sink_low = sinks.astype(f32)
    packed, q_low, k_low, v_low, attn_low, out_other = kernel_call(
        lambda *refs: project_body(ys, *refs),
        [((model, 384), bf16), ((rows, 128), bf16), ((rows + WINDOW, 128), bf16), ((rows + WINDOW, 128), bf16),
         ((rows, 128), bf16), ((4, tok, model), bf16)],
        [after(at, gain_rows), sink_low, block_h, *halo, *w_pieces, bias_qkv, within, base],
        to_hbm=(1, 2, 3, 4),
        from_hbm=(2,),
        scalars=2,
        scratch=[pltpu.VMEM((WINDOW, model), bf16)],
        flops=2 * rows * model * 384 + 8 * rows * 2 * WINDOW * 128,
    )
    sums = sum_pieces(ys, at, attn_low, packed, 256, 384, out_other, to_hbm=(0, 1, 2, 3), from_hbm=(1,))

    w_all = lax.all_gather(after(shard, *sums[1:]), "y", axis=0)

    residual, h2_low, gate_probs, h2_send = kernel_call(
        route_body,
        [((tok, model), f32), ((tok, model), bf16), ((tok, experts), f32), ((slots, model), bf16)],
        [*sums, tokens, gain_rows, router_rows, router_bias[None], place, hot],
        to_hbm=(0, 1, 2, 3),
        from_hbm=(0, 4, 6),

        scalars=0,
        flops=2 * tok * slots * model,
    )
    h2_send = after(h2_send, g_all)
    rows_in = exchange(h2_send.reshape(experts, cap, model), COLUMN).reshape(slots, model)

    u, side, wide, wide_bias = by_chunks(
        lambda *refs: early_body(experts, *refs), 512, at, [g_all], [w_all, b_down], [(ff, f32), (128, f32)],
        2 * slots * model * ff,
        [jax.ShapeDtypeStruct((2 * ff, model), bf16), jax.ShapeDtypeStruct((8, 2 * ff), f32)],
    )
    hidden, grad_pre, back, p_rows = by_chunks(
        lambda *refs: expert_body(ys, *refs), 512, at, [rows_in, side, u],
        [wide, wide_bias, router_rows, router_bias[None]],
        [(ff, bf16), (2 * ff, bf16), (model + 128, bf16), (128, f32)], 8 * slots * model * ff,
        vmem=62,
    )
    back = exchange(back.reshape(experts, cap, model + 128), COLUMN).reshape(slots, model + 128)
    (expert_sum,) = kernel_call(
        lambda *refs: weights_body(ys, *refs),
        [((ys, 6 * ff_own + 16, model), bf16)],
        [rows_in, g_all, hidden, grad_pre, p_rows],
        scalars=0,
        flops=6 * slots * model * ff,
        vmem=60,
    )
    (y_send,) = by_chunks(
        lambda *refs: forward_body(ys, *refs), 512, at, [hidden, p_rows], [w_all, b_down], [(model, bf16)],
        2 * slots * model * ff,
    )

    dres, da = kernel_call(
        lambda *refs: unroute_body(cap, *refs),
        [((tok, model), f32), ((tok + experts + 16, model), bf16)],
        [back, after(place, expert_sum, y_send), gate_probs, h2_low, residual, cotangent, router_rows, gain_two],
        to_hbm=(0,),
        from_hbm=(2, 3, 4, 5, 6),
        scalars=0,
        flops=2 * tok * slots * model,
    )
    da_pieces = gather_pieces(da)
    y_back = exchange(y_send.reshape(experts, cap, model), COLUMN).reshape(slots, model)
    block_out = (residual + dot(place, y_back)).astype(bf16)

    expert_sum = lax.psum_scatter(expert_sum, "y", scatter_dimension=0, tiled=False)

    block_grad, datt, head, dq_first, carry, sunk, sums_all = kernel_call(
        lambda *refs: back_first_body(ys, *refs),
        [((rows, model), bf16), ((rows, 128), bf16), ((WINDOW, 128), bf16), ((WINDOW, 128), f32),
         ((WINDOW, 128), f32), ((2 * WINDOW, 128), f32), ((experts + 16, 128), f32)],
        [at, sink_low, *da_pieces, packed, q_low, k_low, v_low],
        scalars=2,
        flops=2 * rows * model * 128,
    )
    returned = lax.ppermute(head, SEQ, [(s + 1, s) for s in range(seqs - 1)])
    dqkv, tail, grad_sinks, grad_wo = kernel_call(
        back_rest_body,
        [((rows, 256), bf16), ((WINDOW, 128), f32), ((8, 128), f32), ((model, 128), bf16)],
        [at, sink_low, datt, q_low, k_low, v_low, within, base, dq_first, carry, sunk, block_grad, attn_low],
        scalars=2,
        flops=20 * rows * 2 * WINDOW * 128,
    )
    dqkv, dh_other = kernel_call(
        lambda *refs: unproject_body(ys, tok, *refs),
        [((rows, 256), bf16), ((4, tok, model), bf16)],
        [at, dqkv, tail, returned, within, base, packed],
        flops=2 * rows * model * 128,
    )
    (grad_w,) = kernel_call(
        attention_weights_body,
        [((seqs, model // seqs + 16, 384), bf16)],
        [dqkv, block_h, grad_wo, packed, gain_one, grad_sinks, sums_all],
        scalars=0,
        flops=2 * rows * model * 384,
    )
    dh_sums = sum_pieces(ys, at, dqkv, packed, 0, 256, dh_other)

    expert_sum = after(expert_sum, dh_sums[0])
    grad_gu, grad_down, grad_gub, grad_db = kernel_call(
        experts_out_body,
        [((2, 2 * ff_own, model), f32), ((2, ff_own, model), f32), ((2, 2 * ff_own), f32), ((2, model), f32)],
        [at, expert_sum, other_core(expert_sum)],
        vmem=60,
    )
    grad_gu = grad_gu.reshape(2, 2, ff_own, model).transpose(0, 3, 1, 2)
    grad_gub = grad_gub.reshape(2, 2, ff_own)
    experts_done = (grad_gu, grad_down, grad_gub, grad_db)

    share = model // seqs
    grad_w = after(exchange(after(grad_w, y_back), SEQ), dh_sums[0], block_out, *experts_done)
    grad_q, grad_k, grad_v, grad_o, grad_qb, grad_kb, grad_vb, grad_sinks, last = kernel_call(
        sums_body,
        [((share, 128), f32), ((share, 64), f32), ((share, 64), f32), ((share, 128), f32), ((1, 128), f32),
         ((1, 64), f32), ((1, 64), f32), ((1, 2), f32), ((2 * ys, experts + 16, 128), f32)],
        [grad_w],
        scalars=0,
    )
    router_grad, router_b_grad, o_bias_grad, gain_two_grad, gain_one_grad = kernel_call(
        last_body, [((experts, model), f32), ((1, experts), f32)] + [((8, 128), f32)] * 3, [exchange(last, FSDP)], scalars=0
    )

    (tokens_grad,) = kernel_call(
        finish_body, [((tok, model), bf16)], [*dh_sums, tokens, gain_one, dres], scalars=0, from_hbm=(6,)
    )

    return (
        block_out, tokens_grad, gain_one_grad.reshape(model), grad_q, grad_qb.reshape(-1), grad_k,
        grad_kb.reshape(-1), grad_v, grad_vb.reshape(-1), grad_o.T, o_bias_grad.reshape(model),
        grad_sinks.reshape(-1), gain_two_grad.reshape(model), router_grad.T, router_b_grad.reshape(-1),
        grad_gu, grad_gub, grad_down, grad_db,
    )


def solution(mesh):
    sizes = dict(mesh.shape)
    side = int(round(sizes["seq"] ** 0.5))
    wide = Mesh(
        mesh.devices.reshape(side, sizes["seq"] // side, sizes["fsdp"] // 2, 2), ("x", "z", "y", "c")
    )
    in_specs = (
        P(ALL, None), P(ALL, None), P(), P(SEQ, FSDP), P(FSDP), P(SEQ, FSDP), P(FSDP), P(SEQ, FSDP), P(FSDP),
        P(FSDP, SEQ), P(), P(FSDP), P(), P(), P(), P(SEQ, None, None, FSDP), P(SEQ, None, FSDP),
        P(SEQ, FSDP, None), P(SEQ, None), P(ALL, None),
    )
    out_specs = (
        P(ALL, None), P(ALL, None), P(), P(SEQ, FSDP), P(FSDP), P(SEQ, FSDP), P(FSDP), P(SEQ, FSDP), P(FSDP),
        P(FSDP, SEQ), P(), P(FSDP), P(), P(), P(), P(SEQ, None, None, FSDP), P(SEQ, None, FSDP),
        P(SEQ, FSDP, None), P(SEQ, None),
    )
    return jax.shard_map(shards, mesh=wide, in_specs=in_specs, out_specs=out_specs, check_vma=False)
```

```python
import jax
import jax.numpy as jnp
import numpy as np
from jax import lax
from jax.experimental import pallas as pl
from jax.experimental.pallas import tpu as pltpu
from jax.sharding import Mesh, PartitionSpec as P

HEAD_WIDTH = 64
WINDOW = 128
norm_eps = 1e-05
rope_base = 150000.0
swiglu_limit = 7.0
glu_alpha = 1.702
masked_score = -1000000000.0

SEQ = ("x", "z")
FSDP = ("y", "c")
COLUMN = ("x", "z", "c")
ALL = ("x", "z", "y", "c")
f32 = jnp.float32
bf16 = jnp.bfloat16
SCALE = HEAD_WIDTH ** (-0.5)
SHIFTS = (0, 1, -1, 2)


def dot(a, b, dims=((1,), (0,))):
    return lax.dot_general(a, b, (dims, ((), ())), preferred_element_type=f32)


ROWS_BY = ((0,), (0,))
BY_ROWS = ((1,), (1,))


def inv_rms(values):
    return lax.rsqrt(jnp.mean(values * values, axis=-1, keepdims=True) + norm_eps)


def norm_back(grad, normed, root, gain):
    scaled = grad * gain
    return root * (scaled - normed * jnp.mean(scaled * normed, axis=-1, keepdims=True))


def halves(value):
    high = value.astype(bf16)
    return high, (value - high.astype(f32)).astype(bf16)


def lanes(shape):
    return lax.broadcasted_iota(jnp.int32, shape, len(shape) - 1)


def sublanes(shape):
    return lax.broadcasted_iota(jnp.int32, shape, len(shape) - 2)


def swap_halves(values):
    lane = lanes(values.shape) % HEAD_WIDTH
    return jnp.where(lane < 32, pltpu.roll(values, 96, 1), pltpu.roll(values, 32, 1))


def turn(values, cos, sin):
    return values * cos + swap_halves(values) * sin


def exchange(value, axes):
    return lax.all_to_all(value, axes, split_axis=0, concat_axis=0, tiled=True)


def broadcast_exchange(value, axes, count):
    return exchange(jnp.broadcast_to(value[None], (count,) + value.shape), axes)


def after(value, *earlier):
    return lax.optimization_barrier((value,) + earlier)[0]


def along(axis, value, steps):
    count = lax.axis_size(axis)
    return lax.ppermute(value, axis, [(k, (k + steps) % count) for k in range(count)])


def other_core(value):
    return lax.ppermute(value, "c", [(0, 1), (1, 0)])


def kernel_call(body, outs, ins, flops=0, scalars=1, scratch=(), vmem=32, to_hbm=(), from_hbm=()):
    specs = [pl.BlockSpec(memory_space=pltpu.SMEM)] * scalars
    specs += [pl.BlockSpec(memory_space=pltpu.VMEM)] * (len(ins) - scalars)
    ins = [pltpu.with_memory_space_constraint(a, pltpu.HBM) if n in from_hbm else a for n, a in enumerate(ins)]
    out_shape = [jax.ShapeDtypeStruct(shape, kind) for shape, kind in outs]
    moved = sum(a.size * a.dtype.itemsize for a in ins)
    moved += sum(s.size * jnp.dtype(s.dtype).itemsize for s in out_shape)
    return pl.pallas_call(
        body,
        out_shape=[pltpu.HBM(s.shape, s.dtype) if n in to_hbm else s for n, s in enumerate(out_shape)],
        in_specs=specs,
        out_specs=[pl.BlockSpec(memory_space=pltpu.VMEM)] * len(outs),
        scratch_shapes=scratch,
        compiler_params=pltpu.CompilerParams(vmem_limit_bytes=vmem << 20),
        cost_estimate=pl.CostEstimate(flops=flops, bytes_accessed=moved, transcendentals=0),
    )(*ins)


def norm_body(x_ref, gain_ref, q_ref, k_ref, v_ref, o_ref, h_ref, packed_ref):
    x = x_ref[...].astype(f32)
    gain = jnp.concatenate([gain_ref[n : n + 1, :].astype(f32) for n in range(gain_ref.shape[0])], axis=1)
    h_ref[...] = (x * inv_rms(x) * gain).astype(bf16)
    packed_ref[...] = jnp.concatenate([q_ref[...], k_ref[...], v_ref[...], o_ref[...]], axis=1)


def stack_body(*refs):
    count = refs[0].shape[0]
    for n, ref in enumerate(refs[:-1]):
        refs[-1][n * count : (n + 1) * count, :] = ref[...]


def waves(within_ref, base_ref, b):
    cos_in, sin_in = within_ref[:WINDOW, :], within_ref[WINDOW:, :]
    cos_at, sin_at = base_ref[b : b + 1, :], base_ref[16 + b : 17 + b, :]
    sine = sin_at * cos_in + cos_at * sin_in
    first = lanes(sine.shape) % HEAD_WIDTH < HEAD_WIDTH // 2
    return cos_at * cos_in - sin_at * sin_in, jnp.where(first, -sine, sine)


def plan_body(cap, experts, routes_ref, g_ref, place_ref, send_ref, hot_ref):
    tok, top = routes_ref.shape
    model = g_ref.shape[1]
    slots = place_ref.shape[1]
    routes = routes_ref[...]
    ids = lanes((tok, 128))
    hot = jnp.zeros((tok, 128), f32)
    for k in range(top):
        hot += (routes[:, k : k + 1] == ids).astype(f32)
    hot_low = hot.astype(bf16)
    before = (lanes((tok, tok)) < sublanes((tok, tok))).astype(f32).astype(bf16)
    rank = dot(before, hot_low)
    marked = jnp.where(hot > 0, rank, -1.0).astype(bf16)
    slot = lanes((128, slots))
    start = sublanes((128, slots)) * cap
    spread = ((slot >= start) & (slot < start + cap)).astype(f32).astype(bf16)
    wide = dot(marked, spread)
    lane = lanes((tok, slots)).astype(f32)
    within = lane - cap * jnp.floor((lane + 0.5) * (1.0 / cap))
    place = (wide == within).astype(f32).astype(bf16)
    place_ref[...] = place
    hot_ref[...] = hot[:, :experts]
    send_ref[:, :model] = dot(place, g_ref[...], ROWS_BY).astype(bf16)
    send_ref[:, model:] = dot(place, hot_low, ROWS_BY).astype(bf16)


def assemble(at_ref, pieces, block_ref, tok, ys):
    y, core = at_ref[0], at_ref[1]
    for n, piece in enumerate(pieces):
        from_y = lax.rem(y - SHIFTS[n % 4] + ys, ys)
        from_core = core if n < 4 else 1 - core
        start = pl.multiple_of((from_y * 2 + from_core) * tok, tok)
        block_ref[pl.ds(start, tok), :] = piece[...]


def project_body(ys, at_ref, sink_ref, *refs):
    block_ref, halos, w_pieces, refs = refs[0], refs[1 : 1 + ys], refs[1 + ys : 5 + ys], refs[5 + ys :]
    bias_ref, within_ref, base_ref = refs[:3]
    w_ref, q_ref, k_ref, v_ref, att_ref, out_ref, halo_ref = refs[3:]
    share = w_pieces[0].shape[0] // 4
    for n, piece in enumerate(w_pieces):
        for k in range(4):
            from_z = lax.rem(at_ref[5] - SHIFTS[n] + 4, 4)
            from_x = lax.rem(at_ref[4] - SHIFTS[k] + 4, 4)
            start = pl.multiple_of((from_x * 4 + from_z) * share, share)
            w_ref[pl.ds(start, share), :] = piece[k * share : (k + 1) * share, :]
    rows = block_ref.shape[0]
    tok = rows // (2 * ys)
    halo_ref[...] = sum((ref[...] for ref in halos[1:]), halos[0][...])
    weights = w_ref[:, :256]
    low = lanes((WINDOW, 128)) < 64

    def keys_values(kv, b, wave):
        at = slice(b * WINDOW, (b + 1) * WINDOW)
        turned = pltpu.roll(kv, 64, 1)
        k_ref[at, :] = turn(jnp.where(low, kv, turned), *wave).astype(bf16)
        v_ref[at, :] = jnp.where(low, turned, kv).astype(bf16)

    keys_values(dot(halo_ref[...], weights[:, 128:]) + bias_ref[:, 128:], 0, waves(within_ref, base_ref, 0))
    for r in range(0, rows, 2 * WINDOW):
        both = dot(block_ref[r : r + 2 * WINDOW, :], weights) + bias_ref[...]
        for k in range(2):
            qkv = both[k * WINDOW : (k + 1) * WINDOW]
            b = r // WINDOW + k
            wave = waves(within_ref, base_ref, b + 1)
            q_ref[b * WINDOW : (b + 1) * WINDOW, :] = turn(qkv[:, :128], *wave).astype(bf16)
            keys_values(qkv[:, 128:], b + 1, wave)
    sink = sink_column(sink_ref)
    for b in range(rows // WINDOW):
        part = slice(b * WINDOW, (b + 1) * WINDOW)
        near = slice(b * WINDOW, (b + 2) * WINDOW)
        q2 = stack_heads(q_ref[part, :])
        probs, _ = soft_rows(q2, k_ref[near, :], band(at_ref, b == 0), sink)
        both = dot(probs.astype(bf16), v_ref[near, :])
        att_ref[part, :] = jnp.where(low, both[:WINDOW], both[WINDOW:]).astype(bf16)
    to_other(at_ref, att_ref, w_ref[:, 256:384], out_ref, tok, ys)


def band(at_ref, first):
    shape = (2 * WINDOW, 2 * WINDOW)
    i, j = sublanes(shape), lanes(shape)
    off = jnp.where(i >= WINDOW, i - WINDOW, i) + WINDOW - j
    allowed = (off >= 0) & (off < WINDOW)
    if first:
        allowed = allowed & ((j >= WINDOW) | (at_ref[2] > 0))
    return allowed


def stack_heads(pair):
    low = lanes(pair.shape) < 64
    zero = jnp.zeros_like(pair)
    return jnp.concatenate([jnp.where(low, pair, zero), jnp.where(low, zero, pair)], axis=0)


def soft_rows(q2, keys, allowed, sink):
    scores = jnp.where(allowed, dot(q2, keys, BY_ROWS) * SCALE, masked_score)
    top = jnp.maximum(jnp.max(scores, axis=-1, keepdims=True), sink)
    weights = jnp.exp(scores - top)
    sunk = jnp.exp(sink - top)
    inverse = 1.0 / (jnp.sum(weights, axis=-1, keepdims=True) + sunk)
    return weights * inverse, sunk * inverse


def sink_column(sink_ref):
    row = sublanes((2 * WINDOW, 1))
    return jnp.where(row < WINDOW, sink_ref[0], sink_ref[1])


def to_other(at_ref, rows_ref, weights, out_ref, tok, ys):
    for n, shift in enumerate(SHIFTS):
        to_y = lax.rem(at_ref[0] + shift + ys, ys)
        theirs = pl.multiple_of((to_y * 2 + 1 - at_ref[1]) * tok, tok)
        out_ref[n] = dot(rows_ref[pl.ds(theirs, tok), :], weights, BY_ROWS).astype(bf16)


def pair_body(ys, lo, hi, at_ref, rows_ref, w_ref, other_ref, *outs):
    tok = other_ref.shape[1]
    for n, shift in enumerate(SHIFTS):
        to_y = lax.rem(at_ref[0] + shift + ys, ys)
        mine = pl.multiple_of((to_y * 2 + at_ref[1]) * tok, tok)
        own = dot(rows_ref[pl.ds(mine, tok), :], w_ref[:, lo:hi], BY_ROWS)
        outs[n][...] = (own + other_ref[n].astype(f32)).astype(outs[n].dtype)


def gates(values, mask):
    masked = jnp.where(mask, values, masked_score)
    ex = jnp.where(mask, jnp.exp(masked - jnp.max(masked, axis=-1, keepdims=True)), 0.0)
    total = jnp.sum(ex, axis=-1, keepdims=True)
    return ex / jnp.where(total > 0, total, 1.0)


def route_body(
    first_ref, a_ref, b_ref, c_ref, x_ref, rows_ref, rw_ref, rb_ref, place_ref, hot_ref,
    res_ref, h2_ref, gate_ref, send_ref,
):
    tok, experts = gate_ref.shape
    total = first_ref[...] + a_ref[...].astype(f32) + b_ref[...].astype(f32) + c_ref[...].astype(f32)
    residual = x_ref[...].astype(f32) + total + rows_ref[1:2, :].astype(f32)
    res_ref[...] = residual
    h2 = (residual * inv_rms(residual) * rows_ref[:1, :].astype(f32)).astype(bf16)
    h2_ref[...] = h2
    send_ref[...] = dot(place_ref[...], h2, ROWS_BY).astype(bf16)
    logits = dot(h2, rw_ref[...], BY_ROWS) + rb_ref[...].astype(f32)
    gate_ref[...] = gates(logits, hot_ref[...] > 0)


def expert_body(
    ys, at_ref, rows_ref, side_ref, u_ref, wide_ref, bias_ref, rw_ref, rb_ref, hidden_ref, dpre_ref, back_ref, p_ref
):
    model = rows_ref.shape[1]
    experts = rw_ref.shape[0]
    half = wide_ref.shape[0] // (2 * ys)
    step = 256
    for r in range(0, rows_ref.shape[0], step):
        at = slice(r, r + step)
        rows = rows_ref[at, :]
        logits = dot(rows, rw_ref[...], BY_ROWS) + rb_ref[...].astype(f32)
        mask = side_ref[at, :experts] > 0
        mine = lanes((step, experts)) == at_ref[3]
        p = jnp.sum(jnp.where(mine, gates(logits, mask), 0.0), axis=-1, keepdims=True)
        p_ref[at, :] = jnp.broadcast_to(p, (step, 128))
        pre = dot(rows, wide_ref[...], BY_ROWS) + bias_ref[:1, :]
        dgate = jnp.zeros((step, half), f32)
        for n in range(ys):
            low = 2 * n * half
            gt = jnp.tanh(pre[:, low : low + half] * (1.0 / swiglu_limit))
            ut = jnp.tanh(pre[:, low + half : low + 2 * half] * (1.0 / swiglu_limit))
            gate, up = swiglu_limit * gt, swiglu_limit * ut + 1.0
            sig = 0.5 * jnp.tanh((0.5 * glu_alpha) * gate) + 0.5
            gs = gate * sig
            hidden = (up * gs).astype(bf16)
            u = u_ref[at, n * half : (n + 1) * half]
            dgate += hidden.astype(f32) * u
            hidden_ref[at, n * half : (n + 1) * half] = hidden
            dh = p * u
            d_gate = dh * up * (sig + glu_alpha * gs * (1.0 - sig)) * (1.0 - gt * gt)
            d_up = dh * gs * (1.0 - ut * ut)
            dpre_ref[at, low : low + half] = d_gate.astype(bf16)
            dpre_ref[at, low + half : low + 2 * half] = d_up.astype(bf16)
        back_ref[at, :model] = dot(dpre_ref[at, :], wide_ref[...]).astype(bf16)
        dgate = jnp.sum(dgate, axis=-1, keepdims=True) + side_ref[at, experts : experts + 1]
        high, rest = halves(dgate)
        middle, low = halves(dgate - high.astype(f32))
        lane = lanes((step, 128))
        parts = jnp.where(lane == 0, high.astype(f32), jnp.where(lane == 1, middle.astype(f32), low.astype(f32)))
        back_ref[at, model:] = jnp.where(lane < 3, parts, 0.0).astype(bf16)


def by_chunks(body, step, at, cut_in, whole_in, outs, flops, whole_out=(), vmem=60):
    slots = cut_in[0].shape[0]

    def cut(width):
        return pl.BlockSpec((step, width), lambda n: (n, 0))

    def whole(a):
        return pl.BlockSpec(a.shape, lambda n: (0,) * a.ndim)

    return pl.pallas_call(
        body,
        grid=(slots // step,),
        out_shape=[jax.ShapeDtypeStruct((slots, w_), kind) for w_, kind in outs] + list(whole_out),
        in_specs=[pl.BlockSpec(memory_space=pltpu.SMEM)]
        + [cut(a.shape[1]) for a in cut_in]
        + [whole(a) for a in whole_in],
        out_specs=[cut(w_) for w_, _ in outs] + [whole(a) for a in whole_out],
        compiler_params=pltpu.CompilerParams(vmem_limit_bytes=vmem << 20),
        cost_estimate=pl.CostEstimate(flops=flops, bytes_accessed=16 << 20, transcendentals=0),
    )(at, *cut_in, *whole_in)


def split_experts_body(at_ref, gu_ref, down_ref, bias_ref, own_ref, theirs_ref):
    wide, half = gu_ref.shape[1], down_ref.shape[1]
    for ref, expert in ((own_ref, at_ref[1]), (theirs_ref, 1 - at_ref[1])):
        ref[:wide, :] = gu_ref[expert]
        ref[wide : wide + half, :] = down_ref[expert]
        ref[wide + half :, :] = jnp.zeros((16, ref.shape[1]), bf16)
        ref[wide + half : wide + half + 1, :wide] = bias_ref[expert]


def join_experts_body(own_ref, theirs_ref, out_ref):
    half = (own_ref.shape[0] - 16) // 3
    for n in range(3):
        part = slice(n * half, (n + 1) * half)
        out_ref[2 * n * half : (2 * n + 1) * half, :] = own_ref[part, :]
        out_ref[(2 * n + 1) * half : (2 * n + 2) * half, :] = theirs_ref[part, :]
    out_ref[6 * half :, :] = jnp.concatenate(
        [own_ref[3 * half : 3 * half + 8, :], theirs_ref[3 * half : 3 * half + 8, :]], axis=0
    )


def early_body(experts, at_ref, g_ref, w_ref, bd_ref, u_ref, side_ref, wide_ref, bias_ref):
    model = w_ref.shape[2]
    half = (w_ref.shape[1] - 16) // 3
    own = half // 2

    @pl.when(pl.program_id(0) == 0)
    def _():
        for n in range(w_ref.shape[0]):
            part = slice(2 * n * half, 2 * (n + 1) * half)
            wide_ref[part, :] = w_ref[n, : 2 * half, :]
            first, second = w_ref[n, 3 * half : 3 * half + 1, :half], w_ref[n, 3 * half + 8 : 3 * half + 9, :half]
            bias = jnp.concatenate([first[:, :own], second[:, :own], first[:, own:], second[:, own:]], axis=1)
            bias_ref[:, part] = jnp.broadcast_to(bias.astype(f32), (8, 2 * half))

    g = g_ref[:, :model]
    for n in range(w_ref.shape[0]):
        u_ref[:, n * half : (n + 1) * half] = dot(g, w_ref[n, 2 * half : 3 * half, :], BY_ROWS)
    bias = jnp.sum(g.astype(f32) * bd_ref[...], axis=-1, keepdims=True)
    hot = g_ref[:, model:].astype(f32)
    side_ref[...] = jnp.where(lanes(hot.shape) < experts, hot, bias)


def weights_body(ys, rows_ref, g_ref, hidden_ref, dpre_ref, p_ref, sum_ref):
    slots, model = rows_ref.shape
    ff = hidden_ref.shape[1]
    half = ff // ys
    own = half // 2
    step = 256
    dys = []
    bias = jnp.zeros((1, model), f32)
    for r in range(0, slots, step):
        part = slice(r, r + step)
        dy = (p_ref[part, :1] * g_ref[part, :model].astype(f32)).astype(bf16)
        bias += jnp.sum(dy.astype(f32), axis=0, keepdims=True)
        dys.append(dy)
    dy = jnp.concatenate(dys, axis=0)
    high, low = halves(bias)
    row = sublanes((16, model))
    for n in range(ys):
        dpre = dpre_ref[:, 2 * n * half : 2 * (n + 1) * half]
        dw = dot(dpre, rows_ref[...], ROWS_BY)
        ddown = dot(hidden_ref[:, n * half : (n + 1) * half], dy, ROWS_BY)
        parts = [dw[:own], dw[half : half + own], ddown[:own], dw[own:half], dw[half + own :], ddown[own:]]
        for k, part in enumerate(parts):
            sum_ref[n, k * own : (k + 1) * own, :] = part.astype(bf16)
        b = jnp.sum(dpre.astype(f32), axis=0, keepdims=True)
        b = jnp.concatenate([b, jnp.zeros((1, model - 2 * half), f32)], axis=1)
        tail = jnp.where(row == 1, high.astype(f32), jnp.where(row == 2, low.astype(f32), 0.0))
        sum_ref[n, 3 * half :, :] = jnp.where(row == 0, b, tail).astype(bf16)


def forward_body(ys, at_ref, hidden_ref, p_ref, w_ref, bd_ref, y_ref):
    half = hidden_ref.shape[1] // ys
    w_down = jnp.concatenate([w_ref[n, 2 * half : 3 * half, :] for n in range(ys)], axis=0)
    y_ref[...] = (p_ref[:, :1] * (dot(hidden_ref[...], w_down) + bd_ref[...])).astype(bf16)


def experts_out_body(at_ref, own_ref, theirs_ref, gu_ref, down_ref, gub_ref, db_ref):
    core = at_ref[1]
    half = down_ref.shape[1]
    gu_ref[core] = own_ref[: 2 * half, :].astype(f32)
    gu_ref[1 - core] = theirs_ref[3 * half : 5 * half, :].astype(f32)
    down_ref[core] = own_ref[2 * half : 3 * half, :].astype(f32)
    down_ref[1 - core] = theirs_ref[5 * half : 6 * half, :].astype(f32)
    own, theirs = own_ref[6 * half :, :].astype(f32), theirs_ref[6 * half :, :].astype(f32)

    def by_expert(mine, other):
        return jnp.where(sublanes((2, mine.shape[1])) == core, mine, other)

    mine = jnp.concatenate([own[:1, :half], own[:1, 2 * half : 3 * half]], axis=1)
    other = jnp.concatenate([theirs[:1, half : 2 * half], theirs[:1, 3 * half : 4 * half]], axis=1)
    gub_ref[...] = by_expert(mine, other)
    db_ref[...] = by_expert(own[1:2] + own[2:3], theirs[1:2] + theirs[2:3])


def sums_body(in_ref, q_ref, k_ref, v_ref, o_ref, qb_ref, kb_ref, vb_ref, sink_ref, last_ref):
    total = in_ref[0].astype(f32)
    for n in range(1, in_ref.shape[0]):
        total += in_ref[n].astype(f32)
    share = q_ref.shape[0]
    q_ref[...] = total[:share, :128]
    k_ref[...] = total[:share, 128:192]
    v_ref[...] = total[:share, 192:256]
    o_ref[...] = total[:share, 256:]
    sums = jnp.concatenate([total[share:, :128], total[share:, 128:256], total[share:, 256:]], axis=0)
    qb_ref[...] = sums[36:37]
    kb_ref[...] = sums[37:38, :64]
    vb_ref[...] = sums[37:38, 64:]
    sink_ref[...] = sums[38:39, :2]
    for n in range(last_ref.shape[0]):
        last_ref[n] = sums


def last_body(in_ref, router_ref, router_b_ref, o_bias_ref, gain_two_ref, gain_one_ref):
    experts = router_ref.shape[0]
    for n in range(in_ref.shape[0]):
        router_ref[:, n * 128 : (n + 1) * 128] = in_ref[n, :experts, :]
    row = sublanes((8, 128))
    o_bias = gain_two = gain_one = jnp.zeros((8, 128), f32)
    for n in range(in_ref.shape[0]):
        o_bias = jnp.where(row == n, in_ref[n, experts : experts + 1, :], o_bias)
        gain_two = jnp.where(row == n, in_ref[n, experts + 1 : experts + 2, :], gain_two)
        gain_one = gain_one + in_ref[n, experts + 8 :, :]
    o_bias_ref[...] = o_bias
    gain_two_ref[...] = gain_two
    gain_one_ref[...] = gain_one
    router_b_ref[...] = in_ref[0, experts + 2 : experts + 3, :experts]


def unroute_body(
    cap, back_ref, place_ref, gate_ref, h2_ref, res_ref, g_ref, rw_ref, gain_ref, dres_ref, da_ref
):
    tok, experts = gate_ref.shape
    slots, model = place_ref.shape[1], h2_ref.shape[1]
    place = place_ref[...]
    slot = sublanes((slots, experts))
    start = lanes((slots, experts)) * cap
    own = (slot >= start) & (slot < start + cap)
    dgate = jnp.zeros((tok, experts), f32)
    for k in range(3):
        column = back_ref[:, model + k : model + k + 1].astype(f32)
        dgate += dot(place, jnp.where(own, column, 0.0).astype(bf16))
    gate = gate_ref[...]
    dlogits = gate * (dgate - jnp.sum(gate * dgate, axis=-1, keepdims=True))
    high, low = halves(dlogits)
    router = rw_ref[...]
    grad = dot(place, back_ref[:, :model]) + dot(high, router) + dot(low, router)
    h2 = h2_ref[...]
    router_grad = dot(high, h2, ROWS_BY) + dot(low, h2, ROWS_BY)
    residual = res_ref[...]
    root = inv_rms(residual)
    normed = residual * root
    dres = g_ref[...].astype(f32) + norm_back(grad, normed, root, gain_ref[...].astype(f32))
    dres_ref[...] = dres
    o_bias = jnp.sum(dres, axis=0, keepdims=True)
    gain_sum = jnp.sum(grad * normed, axis=0, keepdims=True)
    router_b = jnp.sum(dlogits, axis=0, keepdims=True)
    router_b = jnp.concatenate([router_b, jnp.zeros((1, 128 - experts), f32)], axis=1)
    router_b = jnp.concatenate([router_b] * (model // 128), axis=1)
    row = sublanes((16, model))
    rest = jnp.where(row == 0, o_bias, jnp.where(row == 1, gain_sum, jnp.where(row == 2, router_b, 0.0)))
    da_ref[:tok, :] = dres.astype(bf16)
    da_ref[tok : tok + experts, :] = router_grad.astype(bf16)
    da_ref[tok + experts :, :] = rest.astype(bf16)


def block_back(at_ref, sink, b, q_ref, datt_ref, k_ref, v_ref):
    part = slice(b * WINDOW, (b + 1) * WINDOW)
    near = slice(b * WINDOW, (b + 2) * WINDOW)
    low = lanes((WINDOW, 128)) < 64
    q2 = stack_heads(q_ref[part, :])
    g2 = stack_heads(datt_ref[part, :])
    keys = k_ref[near, :]
    probs, sunk = soft_rows(q2, keys, band(at_ref, b == 0), sink)
    dprobs = dot(g2, v_ref[near, :], BY_ROWS)
    delta = jnp.sum(probs * dprobs, axis=-1, keepdims=True)
    dscores = (probs * (dprobs - delta)).astype(bf16)
    dq2 = dot(dscores, keys)
    dq = jnp.where(low, dq2[:WINDOW], dq2[WINDOW:]) * SCALE
    dk2 = dot(dscores, q2, ROWS_BY) * SCALE
    dv2 = dot(probs.astype(bf16), g2, ROWS_BY)
    wide = lanes(dk2.shape) < 64
    dkv = jnp.where(wide, dk2 + pltpu.roll(dk2, 64, 1), dv2 + pltpu.roll(dv2, 64, 1))
    return dq, dkv, sunk * delta


def turn_back(values, cos, sin):
    return values * cos - swap_halves(values) * sin


def back_first_body(ys, at_ref, sink_ref, *refs):
    pieces, refs = refs[:8], refs[8:]
    w_ref, q_ref, k_ref, v_ref = refs[:4]
    block_ref, datt_ref, head_ref, dq_ref, carry_ref, sink_out_ref, sums_ref = refs[4:]
    tok = block_ref.shape[0] // (2 * ys)
    assemble(at_ref, [piece.at[:tok, :] for piece in pieces], block_ref, tok, ys)
    own = pl.ds(pl.multiple_of((at_ref[0] * 2 + at_ref[1]) * 128, 128), 128)
    total = pieces[0][tok:, own].astype(f32)
    for piece in pieces[1:]:
        total += piece[tok:, own].astype(f32)
    sums_ref[...] = total
    weights = w_ref[:, 256:384]
    for r in range(0, block_ref.shape[0], 256):
        datt_ref[r : r + 256, :] = dot(block_ref[r : r + 256, :], weights).astype(bf16)
    dq, dkv, sunk = block_back(at_ref, sink_column(sink_ref), 0, q_ref, datt_ref, k_ref, v_ref)
    head_ref[...] = dkv[:WINDOW].astype(bf16)
    carry_ref[...] = dkv[WINDOW:]
    dq_ref[...] = dq
    sink_out_ref[...] = jnp.broadcast_to(sunk, sink_out_ref.shape)


def back_rest_body(
    at_ref, sink_ref, datt_ref, q_ref, k_ref, v_ref, within_ref, base_ref, dq_ref, carry_ref, sunk_ref,
    block_ref, att_ref, dqkv_ref, last_ref, sink_out_ref, dwo_ref,
):
    rows = q_ref.shape[0]
    sink = sink_column(sink_ref)
    low = lanes((WINDOW, 128)) < 64
    for d in range(0, dwo_ref.shape[0], 256):
        dwo_ref[d : d + 256, :] = dot(block_ref[:, d : d + 256], att_ref[...], ROWS_BY).astype(bf16)
    sink_sum = sunk_ref[:, :1]
    carry = carry_ref[...]
    for b in range(rows // WINDOW):
        part = slice(b * WINDOW, (b + 1) * WINDOW)
        wave = waves(within_ref, base_ref, b + 1)
        if b == 0:
            dq = dq_ref[...]
        else:
            dq, dkv, sunk = block_back(at_ref, sink, b, q_ref, datt_ref, k_ref, v_ref)
            sink_sum += sunk
            done = carry + dkv[:WINDOW]
            carry = dkv[WINDOW:]
            before = slice((b - 1) * WINDOW, b * WINDOW)
            dqkv_ref[before, 128:] = jnp.where(low, turn_back(done, *last_wave), done).astype(bf16)
        dqkv_ref[part, :128] = turn_back(dq, *wave).astype(bf16)
        last_wave = wave
    last_ref[...] = carry
    dqkv_ref[rows - WINDOW :, 128:] = jnp.zeros((WINDOW, 128), bf16)
    total0 = jnp.sum(sink_sum[:WINDOW], axis=0, keepdims=True)
    total1 = jnp.sum(sink_sum[WINDOW:], axis=0, keepdims=True)
    lane = lanes((8, 128))
    sink_out_ref[...] = -jnp.where(lane == 0, total0, jnp.where(lane == 1, total1, 0.0))


def unproject_body(ys, tok, at_ref, part_ref, last_ref, ret_ref, within_ref, base_ref, w_ref, dqkv_ref, out_ref):
    rows = part_ref.shape[0]
    low = lanes((WINDOW, 128)) < 64
    dqkv_ref[...] = part_ref[...]
    dkv = last_ref[...] + ret_ref[...].astype(f32)
    turned = turn_back(dkv, *waves(within_ref, base_ref, rows // WINDOW))
    dqkv_ref[rows - WINDOW :, 128:] = jnp.where(low, turned, dkv).astype(bf16)
    to_other(at_ref, dqkv_ref, w_ref[:, :256], out_ref, tok, ys)


def attention_weights_body(
    dqkv_ref, block_ref, dwo_ref, w_ref, gain_ref, sink_ref, sums_ref, send_ref
):
    model = block_ref.shape[1]
    bias = jnp.sum(dqkv_ref[...].astype(f32), axis=0, keepdims=True)
    bias = jnp.concatenate([bias, sink_ref[:1, :]], axis=1)
    step = 256
    seqs = send_ref.shape[0]
    share = model // seqs
    per = step // share
    ones = jnp.ones((8, 256), bf16)
    gains = []
    for d in range(0, model, step):
        dw = dot(block_ref[:, d : d + step], dqkv_ref[...], ROWS_BY)
        for k in range(per):
            part = slice(k * share, (k + 1) * share)
            send_ref[d // share + k, :share, :256] = dw[part].astype(bf16)
            send_ref[d // share + k, :share, 256:] = dwo_ref[d + k * share : d + (k + 1) * share, :]
        first, second = halves(dw * w_ref[d : d + step, :256].astype(f32))
        gains.append((dot(ones, first, BY_ROWS) + dot(ones, second, BY_ROWS))[:1])
    gain = jnp.concatenate(gains, axis=1) / gain_ref[...].astype(f32)
    row = sublanes((8, 128))
    middle = sums_ref[32:40, :]
    for n, line in enumerate([bias[:, :128], bias[:, 128:256], bias[:, 256:]]):
        middle = jnp.where(row == n + 4, line, middle)
    gain = jnp.concatenate([gain[:, n * 128 : (n + 1) * 128] for n in range(8)], axis=0)
    third = jnp.concatenate([middle, gain], axis=0)
    tail = jnp.concatenate([sums_ref[:16, :], sums_ref[16:32, :], third], axis=1).astype(bf16)
    for s in range(seqs):
        send_ref[s, share:, :] = tail


def finish_body(first_ref, a_ref, b_ref, c_ref, x_ref, gain_ref, dres_ref, out_ref):
    grad = first_ref[...] + a_ref[...].astype(f32) + b_ref[...].astype(f32) + c_ref[...].astype(f32)
    x = x_ref[...].astype(f32)
    root = inv_rms(x)
    out = dres_ref[...] + norm_back(grad, x * root, root, gain_ref[...].astype(f32))
    out_ref[...] = out.astype(bf16)


def gather_pieces(own):
    mine = [own] + list(lax.optimization_barrier(tuple(along("y", own, s) for s in SHIFTS[1:])))
    return mine + [other_core(piece) for piece in mine]


def sum_pieces(ys, at, rows, weights, lo, hi, out, **where):
    theirs = other_core(out)
    tok, model = out.shape[1:]
    first, *rest = kernel_call(
        lambda *refs: pair_body(ys, lo, hi, *refs),
        [((tok, model), f32)] + [((tok, model), bf16)] * 3,
        [at, rows, weights, theirs],
        **where,
    )
    sent = tuple(along("y", piece, s) for piece, s in zip(rest, SHIFTS[1:]))
    return [first] + list(lax.optimization_barrier(sent))


def shards(
    tokens, cotangent, norm_gain, q_weight, q_bias, key_matrix, key_bias, value_matrix, value_bias,
    o_weight, o_bias, sinks, moe_gain, router_weight, router_bias, gate_up_weight, gate_up_bias,
    down_weight, down_bias, routes,
):
    zs, ys = lax.axis_size("z"), lax.axis_size("y")
    seqs = lax.axis_size("x") * zs
    seq_index = lax.axis_index("x") * zs + lax.axis_index("z")
    core = lax.axis_index("c")
    tok, model = tokens.shape
    rows = tok * ys * 2
    experts = 2 * seqs
    top = routes.shape[1]
    cap = 3 * tok * top // (2 * experts)
    slots = experts * cap
    ff_own = gate_up_weight.shape[-1]
    ff = 2 * ff_own * ys
    at = jnp.stack(
        [lax.axis_index("y"), core, seq_index, 2 * seq_index + core, lax.axis_index("x"), lax.axis_index("z")]
    ).astype(jnp.int32)
    router_rows = router_weight.T

    h_low, packed = kernel_call(
        norm_body,
        [((tok, model), bf16), ((model // seqs, 384), bf16)],
        [tokens, norm_gain.reshape(-1, 128), q_weight, key_matrix, value_matrix, o_weight.T],
        scalars=0,
        vmem=60,
    )
    count = 2 * ys
    last = count - 1
    halo = [lax.ppermute(h_low, ALL, [(s * count + last, (s + 1) * count + last) for s in range(seqs - 1)])]
    halo.append(lax.ppermute(halo[0], FSDP, [(last, last - 1)]))
    block_h = lax.all_gather(h_low, FSDP, axis=0, tiled=True)

    packed = [packed] + [along("x", packed, s) for s in SHIFTS[1:]]
    (packed,) = kernel_call(stack_body, [((4 * model // seqs, 384), bf16)], packed, scalars=0, from_hbm=(0,))
    w_pieces = [packed] + list(lax.optimization_barrier(tuple(along("z", packed, s) for s in SHIFTS[1:])))

    place, g_send, hot = kernel_call(
        lambda *refs: plan_body(cap, experts, *refs),
        [((tok, slots), bf16), ((slots, model + 128), bf16), ((tok, experts), f32)],
        [after(routes, packed), cotangent],
        to_hbm=(1,),
        from_hbm=(1,),
        scalars=0,
        flops=2 * tok * slots * (model + 256),
    )
    halo_both = after(halo[0] + halo[1], g_send, *w_pieces)
    halo = [halo_both] + [
        lax.ppermute(halo_both, FSDP, [(last, place), (last - 1, place - 1)]) for place in range(1, last, 2)
    ]
    g_send = after(g_send, *w_pieces, halo_both)
    g_all = exchange(g_send.reshape(experts, cap, model + 128), COLUMN).reshape(slots, model + 128)

    own, theirs = kernel_call(
        split_experts_body,
        [((3 * ff_own + 16, model), bf16)] * 2,
        [at, gate_up_weight.transpose(0, 2, 3, 1).reshape(2, 2 * ff_own, model), down_weight,
         gate_up_bias.reshape(2, 1, 2 * ff_own)],
        from_hbm=(1, 2),
    )
    (shard,) = kernel_call(
        join_experts_body, [((6 * ff_own + 16, model), bf16)], [own, other_core(theirs)], scalars=0
    )
    b_down = lax.dynamic_index_in_dim(down_bias, core, 0, keepdims=True).astype(f32)

    wave = np.tile(np.arange(HEAD_WIDTH // 2), 4).astype(np.float32)
    inverse = rope_base ** (-(jnp.asarray(wave) * 2.0 / HEAD_WIDTH))
    inner = after(jnp.arange(WINDOW, dtype=f32), w_pieces[0])[:, None] * inverse[None, :]
    starts = after(seq_index, w_pieces[0]) * rows - WINDOW + WINDOW * jnp.arange(16, dtype=jnp.int32)
    outer = starts.astype(f32)[:, None] * inverse[None, :]
    within = jnp.concatenate([jnp.cos(inner), jnp.sin(inner)], axis=0)
    base = jnp.concatenate([jnp.cos(outer), jnp.sin(outer)], axis=0)
    gain_rows = after(jnp.stack([moe_gain, o_bias]), w_pieces[0])
    gain_one = after(norm_gain, w_pieces[0])[None]
    gain_two = gain_rows[:1]
    bias_qkv = jnp.concatenate([after(q_bias, w_pieces[0]), key_bias, value_bias]).astype(f32)[None]
    sink_low = sinks.astype(f32)
    packed, q_low, k_low, v_low, attn_low, out_other = kernel_call(
        lambda *refs: project_body(ys, *refs),
        [((model, 384), bf16), ((rows, 128), bf16), ((rows + WINDOW, 128), bf16), ((rows + WINDOW, 128), bf16),
         ((rows, 128), bf16), ((4, tok, model), bf16)],
        [after(at, gain_rows), sink_low, block_h, *halo, *w_pieces, bias_qkv, within, base],
        to_hbm=(1, 2, 3, 4),
        from_hbm=(2,),
        scalars=2,
        scratch=[pltpu.VMEM((WINDOW, model), bf16)],
        flops=2 * rows * model * 384 + 8 * rows * 2 * WINDOW * 128,
    )
    sums = sum_pieces(ys, at, attn_low, packed, 256, 384, out_other, to_hbm=(0, 1, 2, 3), from_hbm=(1,))

    w_all = lax.all_gather(after(shard, *sums[1:]), "y", axis=0)

    residual, h2_low, gate_probs, h2_send = kernel_call(
        route_body,
        [((tok, model), f32), ((tok, model), bf16), ((tok, experts), f32), ((slots, model), bf16)],
        [*sums, tokens, gain_rows, router_rows, router_bias[None], place, hot],
        to_hbm=(0, 1, 2, 3),
        from_hbm=(0, 4, 6),

        scalars=0,
        flops=2 * tok * slots * model,
    )
    h2_send = after(h2_send, g_all)
    rows_in = exchange(h2_send.reshape(experts, cap, model), COLUMN).reshape(slots, model)

    u, side, wide, wide_bias = by_chunks(
        lambda *refs: early_body(experts, *refs), 512, at, [g_all], [w_all, b_down], [(ff, f32), (128, f32)],
        2 * slots * model * ff,
        [jax.ShapeDtypeStruct((2 * ff, model), bf16), jax.ShapeDtypeStruct((8, 2 * ff), f32)],
    )
    hidden, grad_pre, back, p_rows = by_chunks(
        lambda *refs: expert_body(ys, *refs), 512, at, [rows_in, side, u],
        [wide, wide_bias, router_rows, router_bias[None]],
        [(ff, bf16), (2 * ff, bf16), (model + 128, bf16), (128, f32)], 8 * slots * model * ff,
        vmem=62,
    )
    back = exchange(back.reshape(experts, cap, model + 128), COLUMN).reshape(slots, model + 128)
    (expert_sum,) = kernel_call(
        lambda *refs: weights_body(ys, *refs),
        [((ys, 6 * ff_own + 16, model), bf16)],
        [rows_in, g_all, hidden, grad_pre, p_rows],
        scalars=0,
        flops=6 * slots * model * ff,
        vmem=60,
    )
    (y_send,) = by_chunks(
        lambda *refs: forward_body(ys, *refs), 512, at, [hidden, p_rows], [w_all, b_down], [(model, bf16)],
        2 * slots * model * ff,
    )

    dres, da = kernel_call(
        lambda *refs: unroute_body(cap, *refs),
        [((tok, model), f32), ((tok + experts + 16, model), bf16)],
        [back, after(place, expert_sum, y_send), gate_probs, h2_low, residual, cotangent, router_rows, gain_two],
        to_hbm=(0,),
        from_hbm=(2, 3, 4, 5, 6),
        scalars=0,
        flops=2 * tok * slots * model,
    )
    da_pieces = gather_pieces(da)
    y_back = exchange(y_send.reshape(experts, cap, model), COLUMN).reshape(slots, model)
    block_out = (residual + dot(place, y_back)).astype(bf16)

    expert_sum = lax.psum_scatter(expert_sum, "y", scatter_dimension=0, tiled=False)

    block_grad, datt, head, dq_first, carry, sunk, sums_all = kernel_call(
        lambda *refs: back_first_body(ys, *refs),
        [((rows, model), bf16), ((rows, 128), bf16), ((WINDOW, 128), bf16), ((WINDOW, 128), f32),
         ((WINDOW, 128), f32), ((2 * WINDOW, 128), f32), ((experts + 16, 128), f32)],
        [at, sink_low, *da_pieces, packed, q_low, k_low, v_low],
        scalars=2,
        flops=2 * rows * model * 128,
    )
    returned = lax.ppermute(head, SEQ, [(s + 1, s) for s in range(seqs - 1)])
    dqkv, tail, grad_sinks, grad_wo = kernel_call(
        back_rest_body,
        [((rows, 256), bf16), ((WINDOW, 128), f32), ((8, 128), f32), ((model, 128), bf16)],
        [at, sink_low, datt, q_low, k_low, v_low, within, base, dq_first, carry, sunk, block_grad, attn_low],
        scalars=2,
        flops=20 * rows * 2 * WINDOW * 128,
    )
    dqkv, dh_other = kernel_call(
        lambda *refs: unproject_body(ys, tok, *refs),
        [((rows, 256), bf16), ((4, tok, model), bf16)],
        [at, dqkv, tail, returned, within, base, packed],
        flops=2 * rows * model * 128,
    )
    (grad_w,) = kernel_call(
        attention_weights_body,
        [((seqs, model // seqs + 16, 384), bf16)],
        [dqkv, block_h, grad_wo, packed, gain_one, grad_sinks, sums_all],
        scalars=0,
        flops=2 * rows * model * 384,
    )
    dh_sums = sum_pieces(ys, at, dqkv, packed, 0, 256, dh_other)

    expert_sum = after(expert_sum, dh_sums[0])
    grad_gu, grad_down, grad_gub, grad_db = kernel_call(
        experts_out_body,
        [((2, 2 * ff_own, model), f32), ((2, ff_own, model), f32), ((2, 2 * ff_own), f32), ((2, model), f32)],
        [at, expert_sum, other_core(expert_sum)],
        vmem=60,
    )
    grad_gu = grad_gu.reshape(2, 2, ff_own, model).transpose(0, 3, 1, 2)
    grad_gub = grad_gub.reshape(2, 2, ff_own)
    experts_done = (grad_gu, grad_down, grad_gub, grad_db)

    share = model // seqs
    grad_w = after(exchange(after(grad_w, y_back), SEQ), dh_sums[0], block_out, *experts_done)
    grad_q, grad_k, grad_v, grad_o, grad_qb, grad_kb, grad_vb, grad_sinks, last = kernel_call(
        sums_body,
        [((share, 128), f32), ((share, 64), f32), ((share, 64), f32), ((share, 128), f32), ((1, 128), f32),
         ((1, 64), f32), ((1, 64), f32), ((1, 2), f32), ((2 * ys, experts + 16, 128), f32)],
        [grad_w],
        scalars=0,
    )
    router_grad, router_b_grad, o_bias_grad, gain_two_grad, gain_one_grad = kernel_call(
        last_body, [((experts, model), f32), ((1, experts), f32)] + [((8, 128), f32)] * 3, [exchange(last, FSDP)], scalars=0
    )

    (tokens_grad,) = kernel_call(
        finish_body, [((tok, model), bf16)], [*dh_sums, tokens, gain_one, dres], scalars=0, from_hbm=(6,)
    )

    return (
        block_out, tokens_grad, gain_one_grad.reshape(model), grad_q, grad_qb.reshape(-1), grad_k,
        grad_kb.reshape(-1), grad_v, grad_vb.reshape(-1), grad_o.T, o_bias_grad.reshape(model),
        grad_sinks.reshape(-1), gain_two_grad.reshape(model), router_grad.T, router_b_grad.reshape(-1),
        grad_gu, grad_gub, grad_down, grad_db,
    )


def solution(mesh):
    sizes = dict(mesh.shape)
    side = int(round(sizes["seq"] ** 0.5))
    wide = Mesh(
        mesh.devices.reshape(side, sizes["seq"] // side, sizes["fsdp"] // 2, 2), ("x", "z", "y", "c")
    )
    in_specs = (
        P(ALL, None), P(ALL, None), P(), P(SEQ, FSDP), P(FSDP), P(SEQ, FSDP), P(FSDP), P(SEQ, FSDP), P(FSDP),
        P(FSDP, SEQ), P(), P(FSDP), P(), P(), P(), P(SEQ, None, None, FSDP), P(SEQ, None, FSDP),
        P(SEQ, FSDP, None), P(SEQ, None), P(ALL, None),
    )
    out_specs = (
        P(ALL, None), P(ALL, None), P(), P(SEQ, FSDP), P(FSDP), P(SEQ, FSDP), P(FSDP), P(SEQ, FSDP), P(FSDP),
        P(FSDP, SEQ), P(), P(FSDP), P(), P(), P(), P(SEQ, None, None, FSDP), P(SEQ, None, FSDP),
        P(SEQ, FSDP, None), P(SEQ, None),
    )
    return jax.shard_map(shards, mesh=wide, in_specs=in_specs, out_specs=out_specs, check_vma=False)
```

```python
import jax
import jax.numpy as jnp
import numpy as np
from jax import lax
from jax.experimental import pallas as pl
from jax.experimental.pallas import tpu as pltpu
from jax.sharding import Mesh, PartitionSpec as P

HEAD_WIDTH = 64
WINDOW = 128
norm_eps = 1e-05
rope_base = 150000.0
swiglu_limit = 7.0
glu_alpha = 1.702
masked_score = -1000000000.0

SEQ = ("x", "z")
FSDP = ("y", "c")
COLUMN = ("x", "z", "c")
ALL = ("x", "z", "y", "c")
f32 = jnp.float32
bf16 = jnp.bfloat16
SCALE = HEAD_WIDTH ** (-0.5)
SHIFTS = (0, 1, -1, 2)


def dot(a, b, dims=((1,), (0,))):
    return lax.dot_general(a, b, (dims, ((), ())), preferred_element_type=f32)


ROWS_BY = ((0,), (0,))
BY_ROWS = ((1,), (1,))


def inv_rms(values):
    return lax.rsqrt(jnp.mean(values * values, axis=-1, keepdims=True) + norm_eps)


def norm_back(grad, normed, root, gain):
    scaled = grad * gain
    return root * (scaled - normed * jnp.mean(scaled * normed, axis=-1, keepdims=True))


def halves(value):
    high = value.astype(bf16)
    return high, (value - high.astype(f32)).astype(bf16)


def lanes(shape):
    return lax.broadcasted_iota(jnp.int32, shape, len(shape) - 1)


def sublanes(shape):
    return lax.broadcasted_iota(jnp.int32, shape, len(shape) - 2)


def swap_halves(values):
    lane = lanes(values.shape) % HEAD_WIDTH
    return jnp.where(lane < 32, pltpu.roll(values, 96, 1), pltpu.roll(values, 32, 1))


def turn(values, cos, sin):
    return values * cos + swap_halves(values) * sin


def exchange(value, axes):
    return lax.all_to_all(value, axes, split_axis=0, concat_axis=0, tiled=True)


def broadcast_exchange(value, axes, count):
    return exchange(jnp.broadcast_to(value[None], (count,) + value.shape), axes)


def after(value, *earlier):
    return lax.optimization_barrier((value,) + earlier)[0]


def along(axis, value, steps):
    count = lax.axis_size(axis)
    return lax.ppermute(value, axis, [(k, (k + steps) % count) for k in range(count)])


def other_core(value):
    return lax.ppermute(value, "c", [(0, 1), (1, 0)])


def kernel_call(body, outs, ins, flops=0, scalars=1, scratch=(), vmem=32, to_hbm=(), from_hbm=()):
    specs = [pl.BlockSpec(memory_space=pltpu.SMEM)] * scalars
    specs += [pl.BlockSpec(memory_space=pltpu.VMEM)] * (len(ins) - scalars)
    ins = [pltpu.with_memory_space_constraint(a, pltpu.HBM) if n in from_hbm else a for n, a in enumerate(ins)]
    out_shape = [jax.ShapeDtypeStruct(shape, kind) for shape, kind in outs]
    moved = sum(a.size * a.dtype.itemsize for a in ins)
    moved += sum(s.size * jnp.dtype(s.dtype).itemsize for s in out_shape)
    return pl.pallas_call(
        body,
        out_shape=[pltpu.HBM(s.shape, s.dtype) if n in to_hbm else s for n, s in enumerate(out_shape)],
        in_specs=specs,
        out_specs=[pl.BlockSpec(memory_space=pltpu.VMEM)] * len(outs),
        scratch_shapes=scratch,
        compiler_params=pltpu.CompilerParams(vmem_limit_bytes=vmem << 20),
        cost_estimate=pl.CostEstimate(flops=flops, bytes_accessed=moved, transcendentals=0),
    )(*ins)


def norm_body(x_ref, gain_ref, q_ref, k_ref, v_ref, o_ref, h_ref, packed_ref):
    x = x_ref[...].astype(f32)
    gain = jnp.concatenate([gain_ref[n : n + 1, :].astype(f32) for n in range(gain_ref.shape[0])], axis=1)
    h_ref[...] = (x * inv_rms(x) * gain).astype(bf16)
    packed_ref[...] = jnp.concatenate([q_ref[...], k_ref[...], v_ref[...], o_ref[...]], axis=1)


def stack_body(*refs):
    count = refs[0].shape[0]
    for n, ref in enumerate(refs[:-1]):
        refs[-1][n * count : (n + 1) * count, :] = ref[...]


def waves(within_ref, base_ref, b):
    cos_in, sin_in = within_ref[:WINDOW, :], within_ref[WINDOW:, :]
    cos_at, sin_at = base_ref[b : b + 1, :], base_ref[16 + b : 17 + b, :]
    sine = sin_at * cos_in + cos_at * sin_in
    first = lanes(sine.shape) % HEAD_WIDTH < HEAD_WIDTH // 2
    return cos_at * cos_in - sin_at * sin_in, jnp.where(first, -sine, sine)


def plan_body(cap, experts, routes_ref, g_ref, place_ref, send_ref, hot_ref):
    tok, top = routes_ref.shape
    model = g_ref.shape[1]
    slots = place_ref.shape[1]
    routes = routes_ref[...]
    ids = lanes((tok, 128))
    hot = jnp.zeros((tok, 128), f32)
    for k in range(top):
        hot += (routes[:, k : k + 1] == ids).astype(f32)
    hot_low = hot.astype(bf16)
    before = (lanes((tok, tok)) < sublanes((tok, tok))).astype(f32).astype(bf16)
    rank = dot(before, hot_low)
    marked = jnp.where(hot > 0, rank, -1.0).astype(bf16)
    slot = lanes((128, slots))
    start = sublanes((128, slots)) * cap
    spread = ((slot >= start) & (slot < start + cap)).astype(f32).astype(bf16)
    wide = dot(marked, spread)
    lane = lanes((tok, slots)).astype(f32)
    within = lane - cap * jnp.floor((lane + 0.5) * (1.0 / cap))
    place = (wide == within).astype(f32).astype(bf16)
    place_ref[...] = place
    hot_ref[...] = hot[:, :experts]
    send_ref[:, :model] = dot(place, g_ref[...], ROWS_BY).astype(bf16)
    send_ref[:, model:] = dot(place, hot_low, ROWS_BY).astype(bf16)


def assemble(at_ref, pieces, block_ref, tok, ys):
    y, core = at_ref[0], at_ref[1]
    for n, piece in enumerate(pieces):
        from_y = lax.rem(y - SHIFTS[n % 4] + ys, ys)
        from_core = core if n < 4 else 1 - core
        start = pl.multiple_of((from_y * 2 + from_core) * tok, tok)
        block_ref[pl.ds(start, tok), :] = piece[...]


def project_body(ys, at_ref, sink_ref, *refs):
    block_ref, halos, w_pieces, refs = refs[0], refs[1 : 1 + ys], refs[1 + ys : 5 + ys], refs[5 + ys :]
    bias_ref, within_ref, base_ref = refs[:3]
    w_ref, q_ref, k_ref, v_ref, att_ref, out_ref, halo_ref = refs[3:]
    share = w_pieces[0].shape[0] // 4
    for n, piece in enumerate(w_pieces):
        for k in range(4):
            from_z = lax.rem(at_ref[5] - SHIFTS[n] + 4, 4)
            from_x = lax.rem(at_ref[4] - SHIFTS[k] + 4, 4)
            start = pl.multiple_of((from_x * 4 + from_z) * share, share)
            w_ref[pl.ds(start, share), :] = piece[k * share : (k + 1) * share, :]
    rows = block_ref.shape[0]
    tok = rows // (2 * ys)
    halo_ref[...] = sum((ref[...] for ref in halos[1:]), halos[0][...])
    weights = w_ref[:, :256]
    low = lanes((WINDOW, 128)) < 64

    def keys_values(kv, b, wave):
        at = slice(b * WINDOW, (b + 1) * WINDOW)
        turned = pltpu.roll(kv, 64, 1)
        k_ref[at, :] = turn(jnp.where(low, kv, turned), *wave).astype(bf16)
        v_ref[at, :] = jnp.where(low, turned, kv).astype(bf16)

    keys_values(dot(halo_ref[...], weights[:, 128:]) + bias_ref[:, 128:], 0, waves(within_ref, base_ref, 0))
    for r in range(0, rows, 2 * WINDOW):
        both = dot(block_ref[r : r + 2 * WINDOW, :], weights) + bias_ref[...]
        for k in range(2):
            qkv = both[k * WINDOW : (k + 1) * WINDOW]
            b = r // WINDOW + k
            wave = waves(within_ref, base_ref, b + 1)
            q_ref[b * WINDOW : (b + 1) * WINDOW, :] = turn(qkv[:, :128], *wave).astype(bf16)
            keys_values(qkv[:, 128:], b + 1, wave)
    sink = sink_column(sink_ref)
    for b in range(rows // WINDOW):
        part = slice(b * WINDOW, (b + 1) * WINDOW)
        near = slice(b * WINDOW, (b + 2) * WINDOW)
        q2 = stack_heads(q_ref[part, :])
        probs, _ = soft_rows(q2, k_ref[near, :], band(at_ref, b == 0), sink)
        both = dot(probs.astype(bf16), v_ref[near, :])
        att_ref[part, :] = jnp.where(low, both[:WINDOW], both[WINDOW:]).astype(bf16)
    to_other(at_ref, att_ref, w_ref[:, 256:384], out_ref, tok, ys)


def band(at_ref, first):
    shape = (2 * WINDOW, 2 * WINDOW)
    i, j = sublanes(shape), lanes(shape)
    off = jnp.where(i >= WINDOW, i - WINDOW, i) + WINDOW - j
    allowed = (off >= 0) & (off < WINDOW)
    if first:
        allowed = allowed & ((j >= WINDOW) | (at_ref[2] > 0))
    return allowed


def stack_heads(pair):
    low = lanes(pair.shape) < 64
    zero = jnp.zeros_like(pair)
    return jnp.concatenate([jnp.where(low, pair, zero), jnp.where(low, zero, pair)], axis=0)


def soft_rows(q2, keys, allowed, sink):
    scores = jnp.where(allowed, dot(q2, keys, BY_ROWS) * SCALE, masked_score)
    top = jnp.maximum(jnp.max(scores, axis=-1, keepdims=True), sink)
    weights = jnp.exp(scores - top)
    sunk = jnp.exp(sink - top)
    inverse = 1.0 / (jnp.sum(weights, axis=-1, keepdims=True) + sunk)
    return weights * inverse, sunk * inverse


def sink_column(sink_ref):
    row = sublanes((2 * WINDOW, 1))
    return jnp.where(row < WINDOW, sink_ref[0], sink_ref[1])


def to_other(at_ref, rows_ref, weights, out_ref, tok, ys):
    for n, shift in enumerate(SHIFTS):
        to_y = lax.rem(at_ref[0] + shift + ys, ys)
        theirs = pl.multiple_of((to_y * 2 + 1 - at_ref[1]) * tok, tok)
        out_ref[n] = dot(rows_ref[pl.ds(theirs, tok), :], weights, BY_ROWS).astype(bf16)


def pair_body(ys, lo, hi, at_ref, rows_ref, w_ref, other_ref, *outs):
    tok = other_ref.shape[1]
    for n, shift in enumerate(SHIFTS):
        to_y = lax.rem(at_ref[0] + shift + ys, ys)
        mine = pl.multiple_of((to_y * 2 + at_ref[1]) * tok, tok)
        own = dot(rows_ref[pl.ds(mine, tok), :], w_ref[:, lo:hi], BY_ROWS)
        outs[n][...] = (own + other_ref[n].astype(f32)).astype(outs[n].dtype)


def gates(values, mask):
    masked = jnp.where(mask, values, masked_score)
    ex = jnp.where(mask, jnp.exp(masked - jnp.max(masked, axis=-1, keepdims=True)), 0.0)
    total = jnp.sum(ex, axis=-1, keepdims=True)
    return ex / jnp.where(total > 0, total, 1.0)


def route_body(
    first_ref, a_ref, b_ref, c_ref, x_ref, rows_ref, rw_ref, rb_ref, place_ref, hot_ref,
    res_ref, h2_ref, gate_ref, send_ref,
):
    tok, experts = gate_ref.shape
    total = first_ref[...] + a_ref[...].astype(f32) + b_ref[...].astype(f32) + c_ref[...].astype(f32)
    residual = x_ref[...].astype(f32) + total + rows_ref[1:2, :].astype(f32)
    res_ref[...] = residual
    h2 = (residual * inv_rms(residual) * rows_ref[:1, :].astype(f32)).astype(bf16)
    h2_ref[...] = h2
    send_ref[...] = dot(place_ref[...], h2, ROWS_BY).astype(bf16)
    logits = dot(h2, rw_ref[...], BY_ROWS) + rb_ref[...].astype(f32)
    gate_ref[...] = gates(logits, hot_ref[...] > 0)


def expert_body(
    ys, at_ref, rows_ref, side_ref, u_ref, wide_ref, bias_ref, rw_ref, rb_ref, hidden_ref, dpre_ref, back_ref, p_ref
):
    model = rows_ref.shape[1]
    experts = rw_ref.shape[0]
    half = wide_ref.shape[0] // (2 * ys)
    step = 256
    for r in range(0, rows_ref.shape[0], step):
        at = slice(r, r + step)
        rows = rows_ref[at, :]
        logits = dot(rows, rw_ref[...], BY_ROWS) + rb_ref[...].astype(f32)
        mask = side_ref[at, :experts] > 0
        mine = lanes((step, experts)) == at_ref[3]
        p = jnp.sum(jnp.where(mine, gates(logits, mask), 0.0), axis=-1, keepdims=True)
        p_ref[at, :] = jnp.broadcast_to(p, (step, 128))
        pre = dot(rows, wide_ref[...], BY_ROWS) + bias_ref[:1, :]
        dgate = jnp.zeros((step, half), f32)
        for n in range(ys):
            low = 2 * n * half
            gt = jnp.tanh(pre[:, low : low + half] * (1.0 / swiglu_limit))
            ut = jnp.tanh(pre[:, low + half : low + 2 * half] * (1.0 / swiglu_limit))
            gate, up = swiglu_limit * gt, swiglu_limit * ut + 1.0
            sig = 0.5 * jnp.tanh((0.5 * glu_alpha) * gate) + 0.5
            gs = gate * sig
            hidden = (up * gs).astype(bf16)
            u = u_ref[at, n * half : (n + 1) * half]
            dgate += hidden.astype(f32) * u
            hidden_ref[at, n * half : (n + 1) * half] = hidden
            dh = p * u
            d_gate = dh * up * (sig + glu_alpha * gs * (1.0 - sig)) * (1.0 - gt * gt)
            d_up = dh * gs * (1.0 - ut * ut)
            dpre_ref[at, low : low + half] = d_gate.astype(bf16)
            dpre_ref[at, low + half : low + 2 * half] = d_up.astype(bf16)
        back_ref[at, :model] = dot(dpre_ref[at, :], wide_ref[...]).astype(bf16)
        dgate = jnp.sum(dgate, axis=-1, keepdims=True) + side_ref[at, experts : experts + 1]
        high, rest = halves(dgate)
        middle, low = halves(dgate - high.astype(f32))
        lane = lanes((step, 128))
        parts = jnp.where(lane == 0, high.astype(f32), jnp.where(lane == 1, middle.astype(f32), low.astype(f32)))
        back_ref[at, model:] = jnp.where(lane < 3, parts, 0.0).astype(bf16)


def by_chunks(body, step, at, cut_in, whole_in, outs, flops, whole_out=(), vmem=60):
    slots = cut_in[0].shape[0]

    def cut(width):
        return pl.BlockSpec((step, width), lambda n: (n, 0))

    def whole(a):
        return pl.BlockSpec(a.shape, lambda n: (0,) * a.ndim)

    return pl.pallas_call(
        body,
        grid=(slots // step,),
        out_shape=[jax.ShapeDtypeStruct((slots, w_), kind) for w_, kind in outs] + list(whole_out),
        in_specs=[pl.BlockSpec(memory_space=pltpu.SMEM)]
        + [cut(a.shape[1]) for a in cut_in]
        + [whole(a) for a in whole_in],
        out_specs=[cut(w_) for w_, _ in outs] + [whole(a) for a in whole_out],
        compiler_params=pltpu.CompilerParams(vmem_limit_bytes=vmem << 20),
        cost_estimate=pl.CostEstimate(flops=flops, bytes_accessed=16 << 20, transcendentals=0),
    )(at, *cut_in, *whole_in)


def split_experts_body(at_ref, gu_ref, down_ref, bias_ref, own_ref, theirs_ref):
    wide, half = gu_ref.shape[1], down_ref.shape[1]
    for ref, expert in ((own_ref, at_ref[1]), (theirs_ref, 1 - at_ref[1])):
        ref[:wide, :] = gu_ref[expert]
        ref[wide : wide + half, :] = down_ref[expert]
        ref[wide + half :, :] = jnp.zeros((16, ref.shape[1]), bf16)
        ref[wide + half : wide + half + 1, :wide] = bias_ref[expert]


def join_experts_body(own_ref, theirs_ref, out_ref):
    half = (own_ref.shape[0] - 16) // 3
    for n in range(3):
        part = slice(n * half, (n + 1) * half)
        out_ref[2 * n * half : (2 * n + 1) * half, :] = own_ref[part, :]
        out_ref[(2 * n + 1) * half : (2 * n + 2) * half, :] = theirs_ref[part, :]
    out_ref[6 * half :, :] = jnp.concatenate(
        [own_ref[3 * half : 3 * half + 8, :], theirs_ref[3 * half : 3 * half + 8, :]], axis=0
    )


def early_body(experts, at_ref, g_ref, w_ref, bd_ref, u_ref, side_ref, wide_ref, bias_ref):
    model = w_ref.shape[2]
    half = (w_ref.shape[1] - 16) // 3
    own = half // 2

    @pl.when(pl.program_id(0) == 0)
    def _():
        for n in range(w_ref.shape[0]):
            part = slice(2 * n * half, 2 * (n + 1) * half)
            wide_ref[part, :] = w_ref[n, : 2 * half, :]
            first, second = w_ref[n, 3 * half : 3 * half + 1, :half], w_ref[n, 3 * half + 8 : 3 * half + 9, :half]
            bias = jnp.concatenate([first[:, :own], second[:, :own], first[:, own:], second[:, own:]], axis=1)
            bias_ref[:, part] = jnp.broadcast_to(bias.astype(f32), (8, 2 * half))

    g = g_ref[:, :model]
    for n in range(w_ref.shape[0]):
        u_ref[:, n * half : (n + 1) * half] = dot(g, w_ref[n, 2 * half : 3 * half, :], BY_ROWS)
    bias = jnp.sum(g.astype(f32) * bd_ref[...], axis=-1, keepdims=True)
    hot = g_ref[:, model:].astype(f32)
    side_ref[...] = jnp.where(lanes(hot.shape) < experts, hot, bias)


def weights_body(ys, rows_ref, g_ref, hidden_ref, dpre_ref, p_ref, sum_ref):
    slots, model = rows_ref.shape
    ff = hidden_ref.shape[1]
    half = ff // ys
    own = half // 2
    step = 256
    dys = []
    bias = jnp.zeros((1, model), f32)
    for r in range(0, slots, step):
        part = slice(r, r + step)
        dy = (p_ref[part, :1] * g_ref[part, :model].astype(f32)).astype(bf16)
        bias += jnp.sum(dy.astype(f32), axis=0, keepdims=True)
        dys.append(dy)
    dy = jnp.concatenate(dys, axis=0)
    high, low = halves(bias)
    row = sublanes((16, model))
    for n in range(ys):
        dpre = dpre_ref[:, 2 * n * half : 2 * (n + 1) * half]
        dw = dot(dpre, rows_ref[...], ROWS_BY)
        ddown = dot(hidden_ref[:, n * half : (n + 1) * half], dy, ROWS_BY)
        parts = [dw[:own], dw[half : half + own], ddown[:own], dw[own:half], dw[half + own :], ddown[own:]]
        for k, part in enumerate(parts):
            sum_ref[n, k * own : (k + 1) * own, :] = part.astype(bf16)
        b = jnp.sum(dpre.astype(f32), axis=0, keepdims=True)
        b = jnp.concatenate([b, jnp.zeros((1, model - 2 * half), f32)], axis=1)
        tail = jnp.where(row == 1, high.astype(f32), jnp.where(row == 2, low.astype(f32), 0.0))
        sum_ref[n, 3 * half :, :] = jnp.where(row == 0, b, tail).astype(bf16)


def forward_body(ys, at_ref, hidden_ref, p_ref, w_ref, bd_ref, y_ref):
    half = hidden_ref.shape[1] // ys
    w_down = jnp.concatenate([w_ref[n, 2 * half : 3 * half, :] for n in range(ys)], axis=0)
    y_ref[...] = (p_ref[:, :1] * (dot(hidden_ref[...], w_down) + bd_ref[...])).astype(bf16)


def experts_out_body(at_ref, own_ref, theirs_ref, gu_ref, down_ref, gub_ref, db_ref):
    core = at_ref[1]
    half = down_ref.shape[1]
    gu_ref[core] = own_ref[: 2 * half, :].astype(f32)
    gu_ref[1 - core] = theirs_ref[3 * half : 5 * half, :].astype(f32)
    down_ref[core] = own_ref[2 * half : 3 * half, :].astype(f32)
    down_ref[1 - core] = theirs_ref[5 * half : 6 * half, :].astype(f32)
    own, theirs = own_ref[6 * half :, :].astype(f32), theirs_ref[6 * half :, :].astype(f32)

    def by_expert(mine, other):
        return jnp.where(sublanes((2, mine.shape[1])) == core, mine, other)

    mine = jnp.concatenate([own[:1, :half], own[:1, 2 * half : 3 * half]], axis=1)
    other = jnp.concatenate([theirs[:1, half : 2 * half], theirs[:1, 3 * half : 4 * half]], axis=1)
    gub_ref[...] = by_expert(mine, other)
    db_ref[...] = by_expert(own[1:2] + own[2:3], theirs[1:2] + theirs[2:3])


def sums_body(in_ref, q_ref, k_ref, v_ref, o_ref, qb_ref, kb_ref, vb_ref, sink_ref, last_ref):
    total = in_ref[0].astype(f32)
    for n in range(1, in_ref.shape[0]):
        total += in_ref[n].astype(f32)
    share = q_ref.shape[0]
    q_ref[...] = total[:share, :128]
    k_ref[...] = total[:share, 128:192]
    v_ref[...] = total[:share, 192:256]
    o_ref[...] = total[:share, 256:]
    sums = jnp.concatenate([total[share:, :128], total[share:, 128:256], total[share:, 256:]], axis=0)
    qb_ref[...] = sums[36:37]
    kb_ref[...] = sums[37:38, :64]
    vb_ref[...] = sums[37:38, 64:]
    sink_ref[...] = sums[38:39, :2]
    for n in range(last_ref.shape[0]):
        last_ref[n] = sums


def last_body(in_ref, router_ref, router_b_ref, o_bias_ref, gain_two_ref, gain_one_ref):
    experts = router_ref.shape[0]
    for n in range(in_ref.shape[0]):
        router_ref[:, n * 128 : (n + 1) * 128] = in_ref[n, :experts, :]
    row = sublanes((8, 128))
    o_bias = gain_two = gain_one = jnp.zeros((8, 128), f32)
    for n in range(in_ref.shape[0]):
        o_bias = jnp.where(row == n, in_ref[n, experts : experts + 1, :], o_bias)
        gain_two = jnp.where(row == n, in_ref[n, experts + 1 : experts + 2, :], gain_two)
        gain_one = gain_one + in_ref[n, experts + 8 :, :]
    o_bias_ref[...] = o_bias
    gain_two_ref[...] = gain_two
    gain_one_ref[...] = gain_one
    router_b_ref[...] = in_ref[0, experts + 2 : experts + 3, :experts]


def unroute_body(
    cap, back_ref, place_ref, gate_ref, h2_ref, res_ref, g_ref, rw_ref, gain_ref, dres_ref, da_ref
):
    tok, experts = gate_ref.shape
    slots, model = place_ref.shape[1], h2_ref.shape[1]
    place = place_ref[...]
    slot = sublanes((slots, experts))
    start = lanes((slots, experts)) * cap
    own = (slot >= start) & (slot < start + cap)
    dgate = jnp.zeros((tok, experts), f32)
    for k in range(3):
        column = back_ref[:, model + k : model + k + 1].astype(f32)
        dgate += dot(place, jnp.where(own, column, 0.0).astype(bf16))
    gate = gate_ref[...]
    dlogits = gate * (dgate - jnp.sum(gate * dgate, axis=-1, keepdims=True))
    high, low = halves(dlogits)
    router = rw_ref[...]
    grad = dot(place, back_ref[:, :model]) + dot(high, router) + dot(low, router)
    h2 = h2_ref[...]
    router_grad = dot(high, h2, ROWS_BY) + dot(low, h2, ROWS_BY)
    residual = res_ref[...]
    root = inv_rms(residual)
    normed = residual * root
    dres = g_ref[...].astype(f32) + norm_back(grad, normed, root, gain_ref[...].astype(f32))
    dres_ref[...] = dres
    o_bias = jnp.sum(dres, axis=0, keepdims=True)
    gain_sum = jnp.sum(grad * normed, axis=0, keepdims=True)
    router_b = jnp.sum(dlogits, axis=0, keepdims=True)
    router_b = jnp.concatenate([router_b, jnp.zeros((1, 128 - experts), f32)], axis=1)
    router_b = jnp.concatenate([router_b] * (model // 128), axis=1)
    row = sublanes((16, model))
    rest = jnp.where(row == 0, o_bias, jnp.where(row == 1, gain_sum, jnp.where(row == 2, router_b, 0.0)))
    da_ref[:tok, :] = dres.astype(bf16)
    da_ref[tok : tok + experts, :] = router_grad.astype(bf16)
    da_ref[tok + experts :, :] = rest.astype(bf16)


def block_back(at_ref, sink, b, q_ref, datt_ref, k_ref, v_ref):
    part = slice(b * WINDOW, (b + 1) * WINDOW)
    near = slice(b * WINDOW, (b + 2) * WINDOW)
    low = lanes((WINDOW, 128)) < 64
    q2 = stack_heads(q_ref[part, :])
    g2 = stack_heads(datt_ref[part, :])
    keys = k_ref[near, :]
    probs, sunk = soft_rows(q2, keys, band(at_ref, b == 0), sink)
    dprobs = dot(g2, v_ref[near, :], BY_ROWS)
    delta = jnp.sum(probs * dprobs, axis=-1, keepdims=True)
    dscores = (probs * (dprobs - delta)).astype(bf16)
    dq2 = dot(dscores, keys)
    dq = jnp.where(low, dq2[:WINDOW], dq2[WINDOW:]) * SCALE
    dk2 = dot(dscores, q2, ROWS_BY) * SCALE
    dv2 = dot(probs.astype(bf16), g2, ROWS_BY)
    wide = lanes(dk2.shape) < 64
    dkv = jnp.where(wide, dk2 + pltpu.roll(dk2, 64, 1), dv2 + pltpu.roll(dv2, 64, 1))
    return dq, dkv, sunk * delta


def turn_back(values, cos, sin):
    return values * cos - swap_halves(values) * sin


def back_first_body(ys, at_ref, sink_ref, *refs):
    pieces, refs = refs[:8], refs[8:]
    w_ref, q_ref, k_ref, v_ref = refs[:4]
    block_ref, datt_ref, head_ref, dq_ref, carry_ref, sink_out_ref, sums_ref = refs[4:]
    tok = block_ref.shape[0] // (2 * ys)
    assemble(at_ref, [piece.at[:tok, :] for piece in pieces], block_ref, tok, ys)
    own = pl.ds(pl.multiple_of((at_ref[0] * 2 + at_ref[1]) * 128, 128), 128)
    total = pieces[0][tok:, own].astype(f32)
    for piece in pieces[1:]:
        total += piece[tok:, own].astype(f32)
    sums_ref[...] = total
    weights = w_ref[:, 256:384]
    for r in range(0, block_ref.shape[0], 256):
        datt_ref[r : r + 256, :] = dot(block_ref[r : r + 256, :], weights).astype(bf16)
    dq, dkv, sunk = block_back(at_ref, sink_column(sink_ref), 0, q_ref, datt_ref, k_ref, v_ref)
    head_ref[...] = dkv[:WINDOW].astype(bf16)
    carry_ref[...] = dkv[WINDOW:]
    dq_ref[...] = dq
    sink_out_ref[...] = jnp.broadcast_to(sunk, sink_out_ref.shape)


def back_rest_body(
    at_ref, sink_ref, datt_ref, q_ref, k_ref, v_ref, within_ref, base_ref, dq_ref, carry_ref, sunk_ref,
    block_ref, att_ref, dqkv_ref, last_ref, sink_out_ref, dwo_ref,
):
    rows = q_ref.shape[0]
    sink = sink_column(sink_ref)
    low = lanes((WINDOW, 128)) < 64
    for d in range(0, dwo_ref.shape[0], 256):
        dwo_ref[d : d + 256, :] = dot(block_ref[:, d : d + 256], att_ref[...], ROWS_BY).astype(bf16)
    sink_sum = sunk_ref[:, :1]
    carry = carry_ref[...]
    for b in range(rows // WINDOW):
        part = slice(b * WINDOW, (b + 1) * WINDOW)
        wave = waves(within_ref, base_ref, b + 1)
        if b == 0:
            dq = dq_ref[...]
        else:
            dq, dkv, sunk = block_back(at_ref, sink, b, q_ref, datt_ref, k_ref, v_ref)
            sink_sum += sunk
            done = carry + dkv[:WINDOW]
            carry = dkv[WINDOW:]
            before = slice((b - 1) * WINDOW, b * WINDOW)
            dqkv_ref[before, 128:] = jnp.where(low, turn_back(done, *last_wave), done).astype(bf16)
        dqkv_ref[part, :128] = turn_back(dq, *wave).astype(bf16)
        last_wave = wave
    last_ref[...] = carry
    dqkv_ref[rows - WINDOW :, 128:] = jnp.zeros((WINDOW, 128), bf16)
    total0 = jnp.sum(sink_sum[:WINDOW], axis=0, keepdims=True)
    total1 = jnp.sum(sink_sum[WINDOW:], axis=0, keepdims=True)
    lane = lanes((8, 128))
    sink_out_ref[...] = -jnp.where(lane == 0, total0, jnp.where(lane == 1, total1, 0.0))


def unproject_body(ys, tok, at_ref, part_ref, last_ref, ret_ref, within_ref, base_ref, w_ref, dqkv_ref, out_ref):
    rows = part_ref.shape[0]
    low = lanes((WINDOW, 128)) < 64
    dqkv_ref[...] = part_ref[...]
    dkv = last_ref[...] + ret_ref[...].astype(f32)
    turned = turn_back(dkv, *waves(within_ref, base_ref, rows // WINDOW))
    dqkv_ref[rows - WINDOW :, 128:] = jnp.where(low, turned, dkv).astype(bf16)
    to_other(at_ref, dqkv_ref, w_ref[:, :256], out_ref, tok, ys)


def attention_weights_body(
    dqkv_ref, block_ref, dwo_ref, w_ref, gain_ref, sink_ref, sums_ref, send_ref
):
    model = block_ref.shape[1]
    bias = jnp.sum(dqkv_ref[...].astype(f32), axis=0, keepdims=True)
    bias = jnp.concatenate([bias, sink_ref[:1, :]], axis=1)
    step = 256
    seqs = send_ref.shape[0]
    share = model // seqs
    per = step // share
    ones = jnp.ones((8, 256), bf16)
    gains = []
    for d in range(0, model, step):
        dw = dot(block_ref[:, d : d + step], dqkv_ref[...], ROWS_BY)
        for k in range(per):
            part = slice(k * share, (k + 1) * share)
            send_ref[d // share + k, :share, :256] = dw[part].astype(bf16)
            send_ref[d // share + k, :share, 256:] = dwo_ref[d + k * share : d + (k + 1) * share, :]
        first, second = halves(dw * w_ref[d : d + step, :256].astype(f32))
        gains.append((dot(ones, first, BY_ROWS) + dot(ones, second, BY_ROWS))[:1])
    gain = jnp.concatenate(gains, axis=1) / gain_ref[...].astype(f32)
    row = sublanes((8, 128))
    middle = sums_ref[32:40, :]
    for n, line in enumerate([bias[:, :128], bias[:, 128:256], bias[:, 256:]]):
        middle = jnp.where(row == n + 4, line, middle)
    gain = jnp.concatenate([gain[:, n * 128 : (n + 1) * 128] for n in range(8)], axis=0)
    third = jnp.concatenate([middle, gain], axis=0)
    tail = jnp.concatenate([sums_ref[:16, :], sums_ref[16:32, :], third], axis=1).astype(bf16)
    for s in range(seqs):
        send_ref[s, share:, :] = tail


def finish_body(first_ref, a_ref, b_ref, c_ref, x_ref, gain_ref, dres_ref, out_ref):
    grad = first_ref[...] + a_ref[...].astype(f32) + b_ref[...].astype(f32) + c_ref[...].astype(f32)
    x = x_ref[...].astype(f32)
    root = inv_rms(x)
    out = dres_ref[...] + norm_back(grad, x * root, root, gain_ref[...].astype(f32))
    out_ref[...] = out.astype(bf16)


def gather_pieces(own):
    mine = [own] + list(lax.optimization_barrier(tuple(along("y", own, s) for s in SHIFTS[1:])))
    return mine + [other_core(piece) for piece in mine]


def sum_pieces(ys, at, rows, weights, lo, hi, out, **where):
    theirs = other_core(out)
    tok, model = out.shape[1:]
    first, *rest = kernel_call(
        lambda *refs: pair_body(ys, lo, hi, *refs),
        [((tok, model), f32)] + [((tok, model), bf16)] * 3,
        [at, rows, weights, theirs],
        **where,
    )
    sent = tuple(along("y", piece, s) for piece, s in zip(rest, SHIFTS[1:]))
    return [first] + list(lax.optimization_barrier(sent))


def shards(
    tokens, cotangent, norm_gain, q_weight, q_bias, key_matrix, key_bias, value_matrix, value_bias,
    o_weight, o_bias, sinks, moe_gain, router_weight, router_bias, gate_up_weight, gate_up_bias,
    down_weight, down_bias, routes,
):
    zs, ys = lax.axis_size("z"), lax.axis_size("y")
    seqs = lax.axis_size("x") * zs
    seq_index = lax.axis_index("x") * zs + lax.axis_index("z")
    core = lax.axis_index("c")
    tok, model = tokens.shape
    rows = tok * ys * 2
    experts = 2 * seqs
    top = routes.shape[1]
    cap = 3 * tok * top // (2 * experts)
    slots = experts * cap
    ff_own = gate_up_weight.shape[-1]
    ff = 2 * ff_own * ys
    at = jnp.stack(
        [lax.axis_index("y"), core, seq_index, 2 * seq_index + core, lax.axis_index("x"), lax.axis_index("z")]
    ).astype(jnp.int32)
    router_rows = router_weight.T

    h_low, packed = kernel_call(
        norm_body,
        [((tok, model), bf16), ((model // seqs, 384), bf16)],
        [tokens, norm_gain.reshape(-1, 128), q_weight, key_matrix, value_matrix, o_weight.T],
        scalars=0,
        vmem=60,
    )
    count = 2 * ys
    last = count - 1
    halo = [lax.ppermute(h_low, ALL, [(s * count + last, (s + 1) * count + last) for s in range(seqs - 1)])]
    halo.append(lax.ppermute(halo[0], FSDP, [(last, last - 1)]))
    block_h = lax.all_gather(h_low, FSDP, axis=0, tiled=True)

    packed = [packed] + [along("x", packed, s) for s in SHIFTS[1:]]
    (packed,) = kernel_call(stack_body, [((4 * model // seqs, 384), bf16)], packed, scalars=0, from_hbm=(0,))
    w_pieces = [packed] + list(lax.optimization_barrier(tuple(along("z", packed, s) for s in SHIFTS[1:])))

    place, g_send, hot = kernel_call(
        lambda *refs: plan_body(cap, experts, *refs),
        [((tok, slots), bf16), ((slots, model + 128), bf16), ((tok, experts), f32)],
        [after(routes, packed), cotangent],
        to_hbm=(1,),
        from_hbm=(1,),
        scalars=0,
        flops=2 * tok * slots * (model + 256),
    )
    halo_both = after(halo[0] + halo[1], g_send, *w_pieces)
    halo = [halo_both] + [
        lax.ppermute(halo_both, FSDP, [(last, place), (last - 1, place - 1)]) for place in range(1, last, 2)
    ]
    g_send = after(g_send, *w_pieces, halo_both)
    g_all = exchange(g_send.reshape(experts, cap, model + 128), COLUMN).reshape(slots, model + 128)

    own, theirs = kernel_call(
        split_experts_body,
        [((3 * ff_own + 16, model), bf16)] * 2,
        [at, gate_up_weight.transpose(0, 2, 3, 1).reshape(2, 2 * ff_own, model), down_weight,
         gate_up_bias.reshape(2, 1, 2 * ff_own)],
        from_hbm=(1, 2),
    )
    (shard,) = kernel_call(
        join_experts_body, [((6 * ff_own + 16, model), bf16)], [own, other_core(theirs)], scalars=0
    )
    b_down = lax.dynamic_index_in_dim(down_bias, core, 0, keepdims=True).astype(f32)

    wave = np.tile(np.arange(HEAD_WIDTH // 2), 4).astype(np.float32)
    inverse = rope_base ** (-(jnp.asarray(wave) * 2.0 / HEAD_WIDTH))
    inner = after(jnp.arange(WINDOW, dtype=f32), w_pieces[0])[:, None] * inverse[None, :]
    starts = after(seq_index, w_pieces[0]) * rows - WINDOW + WINDOW * jnp.arange(16, dtype=jnp.int32)
    outer = starts.astype(f32)[:, None] * inverse[None, :]
    within = jnp.concatenate([after(jnp.cos(inner), block_h), jnp.sin(inner)], axis=0)
    base = jnp.concatenate([after(jnp.cos(outer), block_h), jnp.sin(outer)], axis=0)
    gain_rows = after(jnp.stack([moe_gain, o_bias]), w_pieces[0])
    gain_one = after(norm_gain, w_pieces[0])[None]
    gain_two = gain_rows[:1]
    bias_qkv = jnp.concatenate([after(q_bias, block_h), key_bias, value_bias]).astype(f32)[None]
    sink_low = sinks.astype(f32)
    packed, q_low, k_low, v_low, attn_low, out_other = kernel_call(
        lambda *refs: project_body(ys, *refs),
        [((model, 384), bf16), ((rows, 128), bf16), ((rows + WINDOW, 128), bf16), ((rows + WINDOW, 128), bf16),
         ((rows, 128), bf16), ((4, tok, model), bf16)],
        [after(at, gain_rows), sink_low, block_h, *halo, *w_pieces, bias_qkv, within, base],
        to_hbm=(1, 2, 3, 4),
        from_hbm=(2,),
        scalars=2,
        scratch=[pltpu.VMEM((WINDOW, model), bf16)],
        flops=2 * rows * model * 384 + 8 * rows * 2 * WINDOW * 128,
    )
    sums = sum_pieces(ys, at, attn_low, packed, 256, 384, out_other, to_hbm=(0, 1, 2, 3), from_hbm=(1,))

    w_all = lax.all_gather(after(shard, *sums[1:]), "y", axis=0)

    residual, h2_low, gate_probs, h2_send = kernel_call(
        route_body,
        [((tok, model), f32), ((tok, model), bf16), ((tok, experts), f32), ((slots, model), bf16)],
        [*sums, tokens, gain_rows, router_rows, router_bias[None], place, hot],
        to_hbm=(0, 1, 2, 3),
        from_hbm=(0, 4, 6),

        scalars=0,
        flops=2 * tok * slots * model,
    )
    h2_send = after(h2_send, g_all)
    rows_in = exchange(h2_send.reshape(experts, cap, model), COLUMN).reshape(slots, model)

    u, side, wide, wide_bias = by_chunks(
        lambda *refs: early_body(experts, *refs), 512, at, [g_all], [w_all, b_down], [(ff, f32), (128, f32)],
        2 * slots * model * ff,
        [jax.ShapeDtypeStruct((2 * ff, model), bf16), jax.ShapeDtypeStruct((8, 2 * ff), f32)],
    )
    hidden, grad_pre, back, p_rows = by_chunks(
        lambda *refs: expert_body(ys, *refs), 512, at, [rows_in, side, u],
        [wide, wide_bias, router_rows, router_bias[None]],
        [(ff, bf16), (2 * ff, bf16), (model + 128, bf16), (128, f32)], 8 * slots * model * ff,
        vmem=62,
    )
    back = exchange(back.reshape(experts, cap, model + 128), COLUMN).reshape(slots, model + 128)
    (expert_sum,) = kernel_call(
        lambda *refs: weights_body(ys, *refs),
        [((ys, 6 * ff_own + 16, model), bf16)],
        [rows_in, g_all, hidden, grad_pre, p_rows],
        scalars=0,
        flops=6 * slots * model * ff,
        vmem=60,
    )
    (y_send,) = by_chunks(
        lambda *refs: forward_body(ys, *refs), 512, at, [hidden, p_rows], [w_all, b_down], [(model, bf16)],
        2 * slots * model * ff,
    )

    dres, da = kernel_call(
        lambda *refs: unroute_body(cap, *refs),
        [((tok, model), f32), ((tok + experts + 16, model), bf16)],
        [back, after(place, expert_sum, y_send), gate_probs, h2_low, residual, cotangent, router_rows, gain_two],
        to_hbm=(0,),
        from_hbm=(2, 3, 4, 5, 6),
        scalars=0,
        flops=2 * tok * slots * model,
    )
    da_pieces = gather_pieces(da)
    y_back = exchange(y_send.reshape(experts, cap, model), COLUMN).reshape(slots, model)
    block_out = (residual + dot(place, y_back)).astype(bf16)

    expert_sum = lax.psum_scatter(expert_sum, "y", scatter_dimension=0, tiled=False)

    block_grad, datt, head, dq_first, carry, sunk, sums_all = kernel_call(
        lambda *refs: back_first_body(ys, *refs),
        [((rows, model), bf16), ((rows, 128), bf16), ((WINDOW, 128), bf16), ((WINDOW, 128), f32),
         ((WINDOW, 128), f32), ((2 * WINDOW, 128), f32), ((experts + 16, 128), f32)],
        [at, sink_low, *da_pieces, packed, q_low, k_low, v_low],
        scalars=2,
        flops=2 * rows * model * 128,
    )
    returned = lax.ppermute(head, SEQ, [(s + 1, s) for s in range(seqs - 1)])
    dqkv, tail, grad_sinks, grad_wo = kernel_call(
        back_rest_body,
        [((rows, 256), bf16), ((WINDOW, 128), f32), ((8, 128), f32), ((model, 128), bf16)],
        [at, sink_low, datt, q_low, k_low, v_low, within, base, dq_first, carry, sunk, block_grad, attn_low],
        scalars=2,
        flops=20 * rows * 2 * WINDOW * 128,
    )
    dqkv, dh_other = kernel_call(
        lambda *refs: unproject_body(ys, tok, *refs),
        [((rows, 256), bf16), ((4, tok, model), bf16)],
        [at, dqkv, tail, returned, within, base, packed],
        flops=2 * rows * model * 128,
    )
    (grad_w,) = kernel_call(
        attention_weights_body,
        [((seqs, model // seqs + 16, 384), bf16)],
        [dqkv, block_h, grad_wo, packed, gain_one, grad_sinks, sums_all],
        scalars=0,
        flops=2 * rows * model * 384,
    )
    dh_sums = sum_pieces(ys, at, dqkv, packed, 0, 256, dh_other)

    expert_sum = after(expert_sum, dh_sums[0])
    grad_gu, grad_down, grad_gub, grad_db = kernel_call(
        experts_out_body,
        [((2, 2 * ff_own, model), f32), ((2, ff_own, model), f32), ((2, 2 * ff_own), f32), ((2, model), f32)],
        [at, expert_sum, other_core(expert_sum)],
        vmem=60,
    )
    grad_gu = grad_gu.reshape(2, 2, ff_own, model).transpose(0, 3, 1, 2)
    grad_gub = grad_gub.reshape(2, 2, ff_own)
    experts_done = (grad_gu, grad_down, grad_gub, grad_db)

    share = model // seqs
    grad_w = after(exchange(after(grad_w, y_back), SEQ), dh_sums[0], block_out, *experts_done)
    grad_q, grad_k, grad_v, grad_o, grad_qb, grad_kb, grad_vb, grad_sinks, last = kernel_call(
        sums_body,
        [((share, 128), f32), ((share, 64), f32), ((share, 64), f32), ((share, 128), f32), ((1, 128), f32),
         ((1, 64), f32), ((1, 64), f32), ((1, 2), f32), ((2 * ys, experts + 16, 128), f32)],
        [grad_w],
        scalars=0,
    )
    router_grad, router_b_grad, o_bias_grad, gain_two_grad, gain_one_grad = kernel_call(
        last_body, [((experts, model), f32), ((1, experts), f32)] + [((8, 128), f32)] * 3, [exchange(last, FSDP)], scalars=0
    )

    (tokens_grad,) = kernel_call(
        finish_body, [((tok, model), bf16)], [*dh_sums, tokens, gain_one, dres], scalars=0, from_hbm=(6,)
    )

    return (
        block_out, tokens_grad, gain_one_grad.reshape(model), grad_q, grad_qb.reshape(-1), grad_k,
        grad_kb.reshape(-1), grad_v, grad_vb.reshape(-1), grad_o.T, o_bias_grad.reshape(model),
        grad_sinks.reshape(-1), gain_two_grad.reshape(model), router_grad.T, router_b_grad.reshape(-1),
        grad_gu, grad_gub, grad_down, grad_db,
    )


def solution(mesh):
    sizes = dict(mesh.shape)
    side = int(round(sizes["seq"] ** 0.5))
    wide = Mesh(
        mesh.devices.reshape(side, sizes["seq"] // side, sizes["fsdp"] // 2, 2), ("x", "z", "y", "c")
    )
    in_specs = (
        P(ALL, None), P(ALL, None), P(), P(SEQ, FSDP), P(FSDP), P(SEQ, FSDP), P(FSDP), P(SEQ, FSDP), P(FSDP),
        P(FSDP, SEQ), P(), P(FSDP), P(), P(), P(), P(SEQ, None, None, FSDP), P(SEQ, None, FSDP),
        P(SEQ, FSDP, None), P(SEQ, None), P(ALL, None),
    )
    out_specs = (
        P(ALL, None), P(ALL, None), P(), P(SEQ, FSDP), P(FSDP), P(SEQ, FSDP), P(FSDP), P(SEQ, FSDP), P(FSDP),
        P(FSDP, SEQ), P(), P(FSDP), P(), P(), P(), P(SEQ, None, None, FSDP), P(SEQ, None, FSDP),
        P(SEQ, FSDP, None), P(SEQ, None),
    )
    return jax.shard_map(shards, mesh=wide, in_specs=in_specs, out_specs=out_specs, check_vma=False)
```
